32 devices in a mesh: grp: 2 (over x), row: 16 (over z, y, core).
Axes of the slice: x: 2, y: 2, z: 4, core: 2. Of those that a mesh axis runs over, the one named last changes fastest.
Arguments:
- alignment_features: bfloat16 [192, 512, 256], P(('grp', 'row')), parts along dimension 0, may hold values from -6 to 6
- pairwise_features: bfloat16 [32, 128, 128, 128], P(('grp', 'row')), parts along dimension 0, may hold values from -6 to 6
- standardize_scaling: float32 [256], replicated, may hold values from 0.1 to 1.9
- standardize_additive: float32 [256], replicated, may hold values from -3 to 3
- first_factor_matrix: bfloat16 [256, 32], replicated, may hold values from -0.375 to 0.375
- first_factor_intercept: float32 [32], replicated, may hold values from -3 to 3
- second_factor_matrix: bfloat16 [256, 32], replicated, may hold values from -0.375 to 0.375
- second_factor_intercept: float32 [32], replicated, may hold values from -3 to 3
- final_matrix: bfloat16 [1024, 128], replicated, may hold values from -1 to 1
- final_intercept: float32 [128], replicated, may hold values from -3 to 3
Outputs:
- new_pair: bfloat16 [32, 128, 128, 128], P(('grp', 'row')), parts along dimension 0
The draws below stay inside these ranges and needn't reach their ends.
There are 2 independent parts, one for each index of `grp`. The reference program is written for one: setup_inputs(seed, part) draws one part's arguments, and reference() takes and returns one part's arrays. A program takes and returns all parts, laid end to end along the dimension named above; an argument that names none is the same for every part. Nothing has to cross between parts.
All inputs are finite; a program needn't handle non-finite values.
Results may differ from the reference program's by a relative error of at most 0.0053.
Values may be sent and summed in bfloat16 or wider, within the bound.
No kernel may reach another device: no remote copies, remote signals or barrier semaphores. Data moves between devices by JAX's collectives and lax.ppermute only.
A program may use at most 128 MiB of HBM per device.

```python
import jax
import jax.numpy as jnp
from jax import lax

FEATURE_DEPTH = 256
HIDDEN_WIDTH = 32
CZ = 128
TILE = 128
SIDE = 4
AMINO_TOTAL = 512
ALIGNED_TOTAL = 96
N_ROW = 16


def levels(key, dims, split, low, largest):
    def one(position, parts):
        draws = jax.random.uniform(jax.random.fold_in(jax.random.fold_in(key, 6), position), (parts,), jnp.float32, low / len(split), largest / len(split))
        return jnp.repeat(jnp.exp(draws), dims[position] // parts).reshape((-1,) + (1,) * (len(dims) - position - 1))

    factor_of = one(*split[0])
    for cut in split[1:]:
        factor_of = factor_of * one(*cut)
    return factor_of


def gaussian(stream_key, extent, deviation, most, cuts=(), dtype=jnp.bfloat16):
    values = jax.random.normal(stream_key, extent, jnp.float32) * deviation
    if len(cuts) > 0:
        values = levels(stream_key, extent, cuts, -0.22, 0.18) * values
    return jnp.clip(values, min=-most, max=most).astype(dtype)


def setup_inputs(seed: int = 0, part: int = 0) -> dict:
    keys = jax.random.split(jax.random.key(seed), 11)
    part_keys = jax.random.split(jax.random.fold_in(keys[10], part), 11)
    return {
        "alignment_features": gaussian(part_keys[0], (ALIGNED_TOTAL, AMINO_TOTAL, FEATURE_DEPTH), 1.0, 6.0, ((0, 16),)),
        "pairwise_features": gaussian(part_keys[1], (N_ROW, TILE, TILE, CZ), 1.0, 6.0, ((0, 16),)),
        "standardize_scaling": jnp.clip(1.0 + 0.18 * jax.random.normal(keys[2], (FEATURE_DEPTH,), jnp.float32), 0.1, 1.9),
        "standardize_additive": gaussian(keys[3], (FEATURE_DEPTH,), 0.5, 3.0, (), jnp.float32),
        "first_factor_matrix": gaussian(keys[4], (FEATURE_DEPTH, HIDDEN_WIDTH), FEATURE_DEPTH ** -0.5, 0.375),
        "first_factor_intercept": gaussian(keys[5], (HIDDEN_WIDTH,), 0.5, 3.0, (), jnp.float32),
        "second_factor_matrix": gaussian(keys[6], (FEATURE_DEPTH, HIDDEN_WIDTH), FEATURE_DEPTH ** -0.5, 0.375),
        "second_factor_intercept": gaussian(keys[7], (HIDDEN_WIDTH,), 0.5, 3.0, (), jnp.float32),
        "final_matrix": gaussian(keys[8], (HIDDEN_WIDTH * HIDDEN_WIDTH, CZ), HIDDEN_WIDTH ** -0.5, 1.0),
        "final_intercept": gaussian(keys[9], (CZ,), 0.5, 3.0, (), jnp.float32),
    }


def standardize_rows(computed_entries, standardize_scaling, standardize_additive):
    wide = computed_entries.astype(jnp.float32)
    center = wide - lax.optimization_barrier(jnp.mean(wide, axis=-1, keepdims=True))
    variance = lax.optimization_barrier(jnp.mean(center * center, axis=-1, keepdims=True))
    return (center * lax.rsqrt(variance + 1e-05) * standardize_scaling + standardize_additive).astype(jnp.bfloat16)

def reference(alignment_features, pairwise_features, standardize_scaling, standardize_additive, first_factor_matrix, first_factor_intercept, second_factor_matrix, second_factor_intercept, final_matrix, final_intercept):
    standardized_alignment = standardize_rows(alignment_features, standardize_scaling, standardize_additive).reshape(ALIGNED_TOTAL * AMINO_TOTAL, FEATURE_DEPTH)
    first_factor_mapped = (jnp.dot(standardized_alignment, first_factor_matrix, preferred_element_type=jnp.float32) + first_factor_intercept).astype(jnp.bfloat16).reshape(ALIGNED_TOTAL, AMINO_TOTAL, HIDDEN_WIDTH)
    second_factor_mapped = (jnp.dot(standardized_alignment, second_factor_matrix, preferred_element_type=jnp.float32) + second_factor_intercept).astype(jnp.bfloat16).reshape(ALIGNED_TOTAL, AMINO_TOTAL, HIDDEN_WIDTH)
    blocks_left = first_factor_mapped.reshape(ALIGNED_TOTAL, SIDE, TILE, HIDDEN_WIDTH).transpose(1, 0, 2, 3)
    right_wide = second_factor_mapped.astype(jnp.float32)

    def one_block(block_left):
        outer_mean = jnp.einsum('sic,sje->ijce', block_left.astype(jnp.float32), right_wide) / ALIGNED_TOTAL
        outer_mean = outer_mean.astype(jnp.bfloat16).reshape(TILE * AMINO_TOTAL, HIDDEN_WIDTH * HIDDEN_WIDTH)
        update = jnp.dot(outer_mean, final_matrix, preferred_element_type=jnp.float32) + final_intercept
        return update.reshape(TILE, SIDE, TILE, CZ).transpose(1, 0, 2, 3)
    update = lax.map(one_block, blocks_left).reshape(N_ROW, TILE, TILE, CZ)
    return (pairwise_features.astype(jnp.float32) + update).astype(jnp.bfloat16)
```

```python
import functools
import math

import jax
import jax.numpy as jnp
from jax import lax
from jax.experimental import pallas as pl
from jax.experimental.pallas import tpu as pltpu
from jax.sharding import PartitionSpec as P

LANES = 128
VMEM_BYTES = 48 * 1024 * 1024


def project_kernel(side, place_ref, x_ref, gain_ref, offset_ref, wl_ref, bl_ref, wr_ref, br_ref, *rest):
    left_out, right_out, normed_ref = rest[:side], rest[side : 2 * side], rest[2 * side]
    width = wr_ref.shape[0]
    tile = x_ref.shape[1] // side
    pack = LANES // width
    rows = tile // pack
    x = x_ref[0].astype(jnp.float32)
    center = x - jnp.mean(x, axis=-1, keepdims=True)
    variance = jnp.mean(center * center, axis=-1, keepdims=True)
    normed_ref[...] = (
        center * lax.rsqrt(variance + 1e-05) * gain_ref[...] + offset_ref[...]
    ).astype(jnp.bfloat16)
    lane_group = lax.broadcasted_iota(jnp.int32, wl_ref.shape, 1) // width
    wl = wl_ref[...]
    left_parts = [jnp.where(lane_group == h, wl, jnp.zeros_like(wl)) for h in range(pack)]
    for d in range(side):
        a = lax.rem(place_ref[0] + d, side)
        block = normed_ref[pl.ds(pl.multiple_of(a * tile, tile), tile), :]
        total = bl_ref[...]
        for h in range(pack):
            total = total + jnp.dot(
                block[h * rows : (h + 1) * rows], left_parts[h], preferred_element_type=jnp.float32
            )
        left_out[d][0] = total.astype(jnp.bfloat16)
        b = lax.rem(place_ref[1] + d, side)
        block = normed_ref[pl.ds(pl.multiple_of(b * tile, tile), tile), :]
        right = lax.dot_general(
            wr_ref[...], block, (((1,), (1,)), ((), ())), preferred_element_type=jnp.float32
        )
        right_out[d][0] = (right + br_ref[...]).astype(jnp.bfloat16)


def project(side, place, x, gain, offset, wl, bl, wr, br):
    seqs, residues, chans = x.shape
    width = wl.shape[1]
    pack = LANES // width
    tile = residues // side
    rows = tile // pack
    whole = lambda *shape: pl.BlockSpec(shape, lambda s, place: (0,) * len(shape))
    out_spec = [pl.BlockSpec((1, rows, LANES), lambda s, place: (s, 0, 0))] * side
    out_spec += [pl.BlockSpec((1, width, tile), lambda s, place: (s, 0, 0))] * side
    out = pl.pallas_call(
        functools.partial(project_kernel, side),
        grid_spec=pltpu.PrefetchScalarGridSpec(
            num_scalar_prefetch=1,
            grid=(seqs,),
            in_specs=[
                pl.BlockSpec((1, residues, chans), lambda s, place: (s, 0, 0)),
                whole(1, chans),
                whole(1, chans),
                whole(chans, LANES),
                whole(1, LANES),
                whole(width, chans),
                whole(width, 1),
            ],
            out_specs=out_spec,
            scratch_shapes=[pltpu.VMEM((residues, chans), jnp.bfloat16)],
        ),
        out_shape=[jax.ShapeDtypeStruct((seqs, rows, LANES), jnp.bfloat16)] * side
        + [jax.ShapeDtypeStruct((seqs, width, tile), jnp.bfloat16)] * side,
        compiler_params=pltpu.CompilerParams(vmem_limit_bytes=VMEM_BYTES),
        name="project",
    )(
        place,
        x,
        gain[None],
        offset[None],
        jnp.tile(wl, (1, pack)),
        jnp.tile(bl, pack)[None],
        wr.T,
        br[:, None],
    )
    return out[:side], out[side:]


def update_kernel(side, seqs, seq_total, *refs):
    left_refs, right_refs = refs[:side], refs[side : 2 * side]
    wt_ref, bias_ref, pair_ref, out_ref, left_wide, right_wide, right_flat, outer = refs[2 * side :]
    _, rows, lanes = left_refs[0].shape
    _, width, tile = right_refs[0].shape
    depth = right_flat.shape[0]
    pack, group = pair_ref.shape[0], pair_ref.shape[1]
    step = pl.program_id(0)

    @pl.when(step == 0)
    def _():
        part = side * seqs
        for dy in range(side):
            left_wide[dy * part * rows : (dy + 1) * part * rows] = (
                left_refs[dy][...].astype(jnp.float32).reshape(part * rows, lanes)
            )
            for dz in range(side):
                at = (dy * side + dz) * seqs
                right_wide[at * width : (at + seqs) * width] = (
                    right_refs[dz][dy * seqs : (dy + 1) * seqs]
                    .astype(jnp.float32)
                    .reshape(seqs * width, tile)
                )
        if depth > seq_total:
            left_wide[seq_total * rows :] = jnp.zeros(
                ((depth - seq_total) * rows, lanes), jnp.float32
            )
            right_wide[seq_total * width :] = jnp.zeros(
                ((depth - seq_total) * width, tile), jnp.float32
            )
        for e in range(width):
            right_flat[:, e * tile : (e + 1) * tile] = right_wide[
                pl.ds(e, depth, stride=width), :
            ].astype(jnp.bfloat16)

    for q in range(group):
        x = left_wide[pl.ds(step * group + q, depth, stride=rows), :]
        left = x.T.astype(jnp.bfloat16)
        for n in range(width // 2):
            both = jnp.dot(
                left, right_flat[:, 2 * n * tile : (2 * n + 2) * tile], preferred_element_type=jnp.float32
            ).astype(jnp.bfloat16)
            for k in range(2):
                e = 2 * n + k
                for h in range(pack):
                    outer[
                        q * (pack // 2) + h // 2,
                        e * width : (e + 1) * width,
                        (h % 2) * tile : (h % 2 + 1) * tile,
                    ] = both[h * width : (h + 1) * width, k * tile : (k + 1) * tile]
    for q in range(group):
        for g in range(pack // 2):
            update = jnp.dot(
                wt_ref[...], outer[q * (pack // 2) + g], preferred_element_type=jnp.float32
            )
            for k in range(2):
                h = 2 * g + k
                part = update[:, k * tile : (k + 1) * tile].T * (1.0 / seq_total) + bias_ref[...]
                out_ref[h, q] = (pair_ref[h, q].astype(jnp.float32) + part).astype(jnp.bfloat16)


def tile_update(side, seqs, left, right, pair, wt, bias):
    part, rows, lanes = left[0].shape
    _, width, tile = right[0].shape
    seq_total = part * side
    depth = -(-seq_total // LANES) * LANES
    chans = wt.shape[0]
    pack = tile // rows
    group = 4
    whole = lambda shape: pl.BlockSpec(shape, lambda g: (0,) * len(shape))
    pair_spec = pl.BlockSpec((pack, group, tile, chans), lambda g: (0, g, 0, 0))
    out = pl.pallas_call(
        functools.partial(update_kernel, side, seqs, seq_total),
        grid=(rows // group,),
        in_specs=[whole(x.shape) for x in left + right] + [whole(wt.shape), whole((1, chans)), pair_spec],
        out_specs=pair_spec,
        out_shape=jax.ShapeDtypeStruct((pack, rows, tile, chans), jnp.bfloat16),
        scratch_shapes=[
            pltpu.VMEM((depth * rows, lanes), jnp.float32),
            pltpu.VMEM((depth * width, tile), jnp.float32),
            pltpu.VMEM((depth, width * tile), jnp.bfloat16),
            pltpu.VMEM((group * pack // 2, width * width, 2 * tile), jnp.bfloat16),
        ],
        compiler_params=pltpu.CompilerParams(vmem_limit_bytes=VMEM_BYTES),
        name="tile_update",
    )(*left, *right, wt, bias[None], pair.reshape(pack, rows, tile, chans))
    return out.reshape(1, tile, tile, chans)


def local(
    alignment_features,
    pairwise_features,
    standardize_scaling,
    standardize_additive,
    first_factor_matrix,
    first_factor_intercept,
    second_factor_matrix,
    second_factor_intercept,
    final_matrix,
    final_intercept,
):
    devices = lax.axis_size("row")
    side = math.isqrt(devices)
    me = lax.axis_index("row")
    place = jnp.stack([me // side, me % side]).astype(jnp.int32)
    seqs = alignment_features.shape[0]
    width = first_factor_matrix.shape[1]
    left, right = project(
        side,
        place,
        alignment_features,
        standardize_scaling,
        standardize_additive,
        first_factor_matrix,
        first_factor_intercept,
        second_factor_matrix,
        second_factor_intercept,
    )

    def along_a(x, d):
        perm = [(i, (i // side + d) % side * side + i % side) for i in range(devices)]
        return lax.ppermute(x, "row", perm)

    def along_b(x, d):
        perm = [(i, i // side * side + (i % side + d) % side) for i in range(devices)]
        return lax.ppermute(x, "row", perm)

    left = jnp.concatenate([left[0]] + [along_a(left[d], d) for d in range(1, side)])
    right = jnp.concatenate([right[0]] + [along_b(right[d], d) for d in range(1, side)])
    left = [left] + [along_b(left, d) for d in range(1, side)]
    right = [right] + [along_a(right, d) for d in range(1, side)]
    wt = final_matrix.reshape(width, width, -1).transpose(2, 1, 0).reshape(-1, width * width)
    return tile_update(side, seqs, left, right, pairwise_features, wt, final_intercept)


def solution(mesh):
    placed = (
        P(("grp", "row"), None, None),
        P(("grp", "row"), None, None, None),
        P(),
        P(),
        P(),
        P(),
        P(),
        P(),
        P(),
        P(),
    )
    return jax.shard_map(
        local,
        mesh=mesh,
        in_specs=placed,
        out_specs=P(("grp", "row"), None, None, None),
        check_vma=False,
    )
```

```python
import functools
import math

import jax
import jax.numpy as jnp
from jax import lax
from jax.experimental import pallas as pl
from jax.experimental.pallas import tpu as pltpu
from jax.sharding import PartitionSpec as P

LANES = 128
VMEM_BYTES = 60 * 1024 * 1024


def project_kernel(side, x_ref, gain_ref, offset_ref, wl_ref, bl_ref, wr_ref, br_ref, left_ref, right_ref):
    width, chans = wl_ref.shape
    residues = x_ref.shape[1]
    tile = residues // side
    pack = LANES // width
    rows = tile // pack
    x = x_ref[0].astype(jnp.float32)
    center = x - jnp.mean(x, axis=-1, keepdims=True)
    variance = jnp.mean(center * center, axis=-1, keepdims=True)
    normed = (center * lax.rsqrt(variance + 1e-05) * gain_ref[...] + offset_ref[...]).astype(
        jnp.bfloat16
    )
    nt = (((1,), (1,)), ((), ()))
    wl = wl_ref[...]
    total = jnp.concatenate([bl_ref[...]] * pack, axis=1)
    for h in range(pack):
        placed = jnp.concatenate(
            [wl if k == h else jnp.zeros_like(wl) for k in range(pack)], axis=0
        )
        picked = jnp.concatenate(
            [normed[a * tile + h * rows : a * tile + (h + 1) * rows] for a in range(side)], axis=0
        )
        total = total + lax.dot_general(picked, placed, nt, preferred_element_type=jnp.float32)
    left = total.astype(jnp.bfloat16)
    bias = jnp.broadcast_to(br_ref[...], (tile, width)).T
    right = lax.dot_general(wr_ref[...], normed, nt, preferred_element_type=jnp.float32)
    for a in range(side):
        left_ref[a, 0] = left[a * rows : (a + 1) * rows]
        right_ref[a, 0] = (right[:, a * tile : (a + 1) * tile] + bias).astype(jnp.bfloat16)


def project(side, x, gain, offset, wl, bl, wr, br):
    seqs, residues, chans = x.shape
    width = wl.shape[1]
    tile = residues // side
    rows = tile * width // LANES
    whole = lambda *shape: pl.BlockSpec(shape, lambda s: (0,) * len(shape))
    return pl.pallas_call(
        functools.partial(project_kernel, side),
        grid=(seqs,),
        in_specs=[
            pl.BlockSpec((1, residues, chans), lambda s: (s, 0, 0)),
            whole(1, chans),
            whole(1, chans),
            whole(width, chans),
            whole(1, width),
            whole(width, chans),
            whole(1, width),
        ],
        out_specs=[
            pl.BlockSpec((side, 1, rows, LANES), lambda s: (0, s, 0, 0)),
            pl.BlockSpec((side, 1, width, tile), lambda s: (0, s, 0, 0)),
        ],
        out_shape=[
            jax.ShapeDtypeStruct((side, seqs, rows, LANES), jnp.bfloat16),
            jax.ShapeDtypeStruct((side, seqs, width, tile), jnp.bfloat16),
        ],
        compiler_params=pltpu.CompilerParams(vmem_limit_bytes=VMEM_BYTES),
        name="project",
    )(x, gain[None], offset[None], wl.T, bl[None], wr.T, br[None])


def update_kernel(side, seqs, seq_total, *refs):
    left_ref, right_ref, wt_ref, bias_ref, pair_ref = refs[:5]
    out_ref, left_wide, right_wide, right_flat, outer = refs[5:]
    _, rows, lanes = left_ref.shape
    _, width, tile = right_ref.shape
    depth = right_flat.shape[0]
    pack, group = pair_ref.shape[0], pair_ref.shape[1]
    step = pl.program_id(0)

    @pl.when(step == 0)
    def _():
        left_wide[: seq_total * rows] = (
            left_ref[...].astype(jnp.float32).reshape(seq_total * rows, lanes)
        )
        for a in range(side):
            for b in range(side):
                at, to = (a * side + b) * seqs, (b * side + a) * seqs
                right_wide[to * width : (to + seqs) * width] = (
                    right_ref[at : at + seqs].astype(jnp.float32).reshape(seqs * width, tile)
                )
        if depth > seq_total:
            left_wide[seq_total * rows :] = jnp.zeros(
                ((depth - seq_total) * rows, lanes), jnp.float32
            )
            right_wide[seq_total * width :] = jnp.zeros(
                ((depth - seq_total) * width, tile), jnp.float32
            )
        for e in range(width):
            right_flat[:, e * tile : (e + 1) * tile] = right_wide[
                pl.ds(e, depth, stride=width), :
            ].astype(jnp.bfloat16)

    for q in range(group):
        x = left_wide[pl.ds(step * group + q, depth, stride=rows), :]
        left = x.T.astype(jnp.bfloat16)
        for n in range(width // 2):
            both = jnp.dot(
                left, right_flat[:, 2 * n * tile : (2 * n + 2) * tile], preferred_element_type=jnp.float32
            ).astype(jnp.bfloat16)
            for k in range(2):
                e = 2 * n + k
                for h in range(pack):
                    outer[
                        q * (pack // 2) + h // 2,
                        e * width : (e + 1) * width,
                        (h % 2) * tile : (h % 2 + 1) * tile,
                    ] = both[h * width : (h + 1) * width, k * tile : (k + 1) * tile]
    for q in range(group):
        for g in range(pack // 2):
            update = jnp.dot(
                wt_ref[...], outer[q * (pack // 2) + g], preferred_element_type=jnp.float32
            )
            for k in range(2):
                h = 2 * g + k
                part = update[:, k * tile : (k + 1) * tile].T * (1.0 / seq_total) + bias_ref[...]
                out_ref[h, q] = (pair_ref[h, q].astype(jnp.float32) + part).astype(jnp.bfloat16)


def tile_update(side, seqs, left, right, pair, wt, bias):
    seq_total, rows, lanes = left.shape
    _, width, tile = right.shape
    depth = -(-seq_total // LANES) * LANES
    chans = wt.shape[0]
    pack = tile // rows
    group = 4
    whole = lambda shape: pl.BlockSpec(shape, lambda g: (0,) * len(shape))
    pair_spec = pl.BlockSpec((pack, group, tile, chans), lambda g: (0, g, 0, 0))
    out = pl.pallas_call(
        functools.partial(update_kernel, side, seqs, seq_total),
        grid=(rows // group,),
        in_specs=[whole(left.shape), whole(right.shape), whole(wt.shape), whole((1, chans)), pair_spec],
        out_specs=pair_spec,
        out_shape=jax.ShapeDtypeStruct((pack, rows, tile, chans), jnp.bfloat16),
        scratch_shapes=[
            pltpu.VMEM((depth * rows, lanes), jnp.float32),
            pltpu.VMEM((depth * width, tile), jnp.float32),
            pltpu.VMEM((depth, width * tile), jnp.bfloat16),
            pltpu.VMEM((group * pack // 2, width * width, 2 * tile), jnp.bfloat16),
        ],
        compiler_params=pltpu.CompilerParams(vmem_limit_bytes=VMEM_BYTES),
        name="tile_update",
    )(left, right, wt, bias[None], pair.reshape(pack, rows, tile, chans))
    return out.reshape(1, tile, tile, chans)


def local(
    alignment_features,
    pairwise_features,
    standardize_scaling,
    standardize_additive,
    first_factor_matrix,
    first_factor_intercept,
    second_factor_matrix,
    second_factor_intercept,
    final_matrix,
    final_intercept,
):
    devices = lax.axis_size("row")
    side = math.isqrt(devices)
    seqs = alignment_features.shape[0]
    width = first_factor_matrix.shape[1]
    left, right = project(
        side,
        alignment_features,
        standardize_scaling,
        standardize_additive,
        first_factor_matrix,
        first_factor_intercept,
        second_factor_matrix,
        second_factor_intercept,
    )
    same_a = [[a * side + b for b in range(side)] for a in range(side)]
    same_b = [[a * side + b for a in range(side)] for b in range(side)]

    def spread(x, groups):
        x = lax.all_to_all(x, "row", 0, 0, axis_index_groups=groups, tiled=True)
        return x.reshape((side * seqs,) + x.shape[2:])

    def collect(x, groups):
        return lax.all_gather(x, "row", axis_index_groups=groups, tiled=True)

    right = collect(spread(right, same_a), same_b)
    left = collect(spread(left, same_b), same_a)
    wt = final_matrix.reshape(width, width, -1).transpose(2, 1, 0).reshape(-1, width * width)
    return tile_update(side, seqs, left, right, pairwise_features, wt, final_intercept)


def solution(mesh):
    placed = (
        P(("grp", "row"), None, None),
        P(("grp", "row"), None, None, None),
        P(),
        P(),
        P(),
        P(),
        P(),
        P(),
        P(),
        P(),
    )
    return jax.shard_map(
        local,
        mesh=mesh,
        in_specs=placed,
        out_specs=P(("grp", "row"), None, None, None),
        check_vma=False,
    )
```

```python
import functools
import math

import jax
import jax.numpy as jnp
from jax import lax
from jax.experimental import pallas as pl
from jax.experimental.pallas import tpu as pltpu
from jax.sharding import PartitionSpec as P

LANES = 128
VMEM_BYTES = 60 * 1024 * 1024


def project_kernel(side, x_ref, gain_ref, offset_ref, wl_ref, bl_ref, wr_ref, br_ref, left_ref, right_ref):
    width, chans = wl_ref.shape
    residues = x_ref.shape[1]
    tile = residues // side
    pack = LANES // width
    rows = tile // pack
    x = x_ref[0].astype(jnp.float32)
    center = x - jnp.mean(x, axis=-1, keepdims=True)
    variance = jnp.mean(center * center, axis=-1, keepdims=True)
    normed = (center * lax.rsqrt(variance + 1e-05) * gain_ref[...] + offset_ref[...]).astype(
        jnp.bfloat16
    )
    nt = (((1,), (1,)), ((), ()))
    wl = wl_ref[...]
    total = jnp.concatenate([bl_ref[...]] * pack, axis=1)
    for h in range(pack):
        placed = jnp.concatenate(
            [wl if k == h else jnp.zeros_like(wl) for k in range(pack)], axis=0
        )
        picked = jnp.concatenate(
            [normed[a * tile + h * rows : a * tile + (h + 1) * rows] for a in range(side)], axis=0
        )
        total = total + lax.dot_general(picked, placed, nt, preferred_element_type=jnp.float32)
    left = total.astype(jnp.bfloat16)
    bias = jnp.broadcast_to(br_ref[...], (tile, width)).T
    right = lax.dot_general(wr_ref[...], normed, nt, preferred_element_type=jnp.float32)
    for a in range(side):
        left_ref[a, 0] = left[a * rows : (a + 1) * rows]
        right_ref[a, 0] = (right[:, a * tile : (a + 1) * tile] + bias).astype(jnp.bfloat16)


def project(side, x, gain, offset, wl, bl, wr, br):
    seqs, residues, chans = x.shape
    width = wl.shape[1]
    tile = residues // side
    rows = tile * width // LANES
    whole = lambda *shape: pl.BlockSpec(shape, lambda s: (0,) * len(shape))
    return pl.pallas_call(
        functools.partial(project_kernel, side),
        grid=(seqs,),
        in_specs=[
            pl.BlockSpec((1, residues, chans), lambda s: (s, 0, 0)),
            whole(1, chans),
            whole(1, chans),
            whole(width, chans),
            whole(1, width),
            whole(width, chans),
            whole(1, width),
        ],
        out_specs=[
            pl.BlockSpec((side, 1, rows, LANES), lambda s: (0, s, 0, 0)),
            pl.BlockSpec((side, 1, width, tile), lambda s: (0, s, 0, 0)),
        ],
        out_shape=[
            jax.ShapeDtypeStruct((side, seqs, rows, LANES), jnp.bfloat16),
            jax.ShapeDtypeStruct((side, seqs, width, tile), jnp.bfloat16),
        ],
        compiler_params=pltpu.CompilerParams(vmem_limit_bytes=VMEM_BYTES),
        name="project",
    )(x, gain[None], offset[None], wl.T, bl[None], wr.T, br[None])


def update_kernel(side, seqs, seq_total, *refs):
    place_ref, left_refs = refs[0], refs[1 : 1 + side]
    right_ref, wt_ref, bias_ref, pair_ref, out_ref = refs[1 + side : 6 + side]
    left_wide, right_wide, right_flat, left_rows, outer = refs[6 + side :]
    _, rows, lanes = left_refs[0].shape
    _, _, width, tile = right_ref.shape
    depth = right_flat.shape[0]
    pack, group = pair_ref.shape[0], pair_ref.shape[1]
    step = pl.program_id(0)

    @pl.when(step == 0)
    def _():
        part = side * seqs
        for d in range(side):
            left_wide[d * part * rows : (d + 1) * part * rows] = (
                left_refs[d][...].astype(jnp.float32).reshape(part * rows, lanes)
            )
            b = lax.rem(place_ref[0] + side - d, side)
            for a in range(side):
                to = (d * side + a) * seqs
                right_wide[to * width : (to + seqs) * width] = (
                    right_ref[0, pl.ds((a * side + b) * seqs, seqs)]
                    .astype(jnp.float32)
                    .reshape(seqs * width, tile)
                )
        if depth > seq_total:
            left_wide[seq_total * rows :] = jnp.zeros(
                ((depth - seq_total) * rows, lanes), jnp.float32
            )
            right_wide[seq_total * width :] = jnp.zeros(
                ((depth - seq_total) * width, tile), jnp.float32
            )
        for e in range(width):
            right_flat[:, e * tile : (e + 1) * tile] = right_wide[
                pl.ds(e, depth, stride=width), :
            ].astype(jnp.bfloat16)

    for q in range(group):
        x = left_wide[pl.ds(step * group + q, depth, stride=rows), :]
        left_rows[q * lanes : (q + 1) * lanes] = x.T.astype(jnp.bfloat16)
    for n in range(width // 2):
        both = jnp.dot(
            left_rows[...],
            right_flat[:, 2 * n * tile : (2 * n + 2) * tile],
            preferred_element_type=jnp.float32,
        ).astype(jnp.bfloat16)
        for k in range(2):
            e = 2 * n + k
            for h in range(group * pack):
                outer[
                    h // 2, e * width : (e + 1) * width, (h % 2) * tile : (h % 2 + 1) * tile
                ] = both[h * width : (h + 1) * width, k * tile : (k + 1) * tile]
    for q in range(group):
        for g in range(pack // 2):
            update = jnp.dot(
                wt_ref[...], outer[q * (pack // 2) + g], preferred_element_type=jnp.float32
            )
            for k in range(2):
                h = 2 * g + k
                part = update[:, k * tile : (k + 1) * tile].T * (1.0 / seq_total) + bias_ref[...]
                out_ref[h, q] = (pair_ref[h, q].astype(jnp.float32) + part).astype(jnp.bfloat16)


def tile_update(side, seqs, place, left, right, pair, wt, bias):
    part, rows, lanes = left[0].shape
    _, seq_total, width, tile = right.shape
    depth = -(-seq_total // LANES) * LANES
    chans = wt.shape[0]
    pack = tile // rows
    group = 4
    whole = lambda shape: pl.BlockSpec(shape, lambda g, place: (0,) * len(shape))
    pair_spec = pl.BlockSpec((pack, group, tile, chans), lambda g, place: (0, g, 0, 0))
    out = pl.pallas_call(
        functools.partial(update_kernel, side, seqs, seq_total),
        grid_spec=pltpu.PrefetchScalarGridSpec(
            num_scalar_prefetch=1,
            grid=(rows // group,),
            in_specs=[whole(x.shape) for x in left]
            + [
                pl.BlockSpec((1, seq_total, width, tile), lambda g, place: (place[0], 0, 0, 0)),
                whole(wt.shape),
                whole((1, chans)),
                pair_spec,
            ],
            out_specs=pair_spec,
            scratch_shapes=[
                pltpu.VMEM((depth * rows, lanes), jnp.float32),
                pltpu.VMEM((depth * width, tile), jnp.float32),
                pltpu.VMEM((depth, width * tile), jnp.bfloat16),
                pltpu.VMEM((group * lanes, depth), jnp.bfloat16),
                pltpu.VMEM((group * pack // 2, width * width, 2 * tile), jnp.bfloat16),
            ],
        ),
        out_shape=jax.ShapeDtypeStruct((pack, rows, tile, chans), jnp.bfloat16),
        compiler_params=pltpu.CompilerParams(vmem_limit_bytes=VMEM_BYTES),
        name="tile_update",
    )(place, *left, right, wt, bias[None], pair.reshape(pack, rows, tile, chans))
    return out.reshape(1, tile, tile, chans)


def local(
    alignment_features,
    pairwise_features,
    standardize_scaling,
    standardize_additive,
    first_factor_matrix,
    first_factor_intercept,
    second_factor_matrix,
    second_factor_intercept,
    final_matrix,
    final_intercept,
):
    devices = lax.axis_size("row")
    side = math.isqrt(devices)
    seqs = alignment_features.shape[0]
    width = first_factor_matrix.shape[1]
    left, right = project(
        side,
        alignment_features,
        standardize_scaling,
        standardize_additive,
        first_factor_matrix,
        first_factor_intercept,
        second_factor_matrix,
        second_factor_intercept,
    )
    same_b = [[a * side + b for a in range(side)] for b in range(side)]

    def spread(x, groups):
        x = lax.all_to_all(x, "row", 0, 0, axis_index_groups=groups, tiled=True)
        return x.reshape((side * seqs,) + x.shape[2:])

    right = lax.all_gather(right, "row", axis=1, tiled=True)
    left = spread(left, same_b)
    pieces = [left] + [
        lax.ppermute(
            left, "row", [(i, i // side * side + (i % side + d) % side) for i in range(devices)]
        )
        for d in range(1, side)
    ]
    place = (lax.axis_index("row") % side).reshape(1).astype(jnp.int32)
    wt = final_matrix.reshape(width, width, -1).transpose(2, 1, 0).reshape(-1, width * width)
    return tile_update(side, seqs, place, pieces, right, pairwise_features, wt, final_intercept)


def solution(mesh):
    placed = (
        P(("grp", "row"), None, None),
        P(("grp", "row"), None, None, None),
        P(),
        P(),
        P(),
        P(),
        P(),
        P(),
        P(),
        P(),
    )
    return jax.shard_map(
        local,
        mesh=mesh,
        in_specs=placed,
        out_specs=P(("grp", "row"), None, None, None),
        check_vma=False,
    )
```

```python
import functools
import math

import jax
import jax.numpy as jnp
from jax import lax
from jax.experimental import pallas as pl
from jax.experimental.pallas import tpu as pltpu
from jax.sharding import PartitionSpec as P

LANES = 128
PARTS = 2
MIB = 1024 * 1024


def project_kernel(side, place_ref, x_ref, gain_ref, offset_ref, wl_ref, bl_ref, wr_ref, br_ref, *rest):
    left_out, right_out, normed_ref = rest[:side], rest[side : 2 * side], rest[2 * side]
    width, chans = wl_ref.shape
    tile = x_ref.shape[1] // side
    pack = LANES // width
    rows = tile // pack
    x = x_ref[0].astype(jnp.float32)
    center = x - jnp.mean(x, axis=-1, keepdims=True)
    variance = jnp.mean(center * center, axis=-1, keepdims=True)
    normed_ref[...] = (
        center * lax.rsqrt(variance + 1e-05) * gain_ref[...] + offset_ref[...]
    ).astype(jnp.bfloat16)
    nt = (((1,), (1,)), ((), ()))
    blocks = []
    for d in range(side):
        a = place_ref[0] ^ d
        blocks.append(normed_ref[pl.ds(pl.multiple_of(a * tile, tile), tile), :])
    wl = wl_ref[...]
    total = jnp.concatenate([bl_ref[...]] * pack, axis=1)
    for h in range(pack):
        placed = jnp.concatenate(
            [wl if k == h else jnp.zeros_like(wl) for k in range(pack)], axis=0
        )
        picked = jnp.concatenate([block[h * rows : (h + 1) * rows] for block in blocks], axis=0)
        total = total + lax.dot_general(picked, placed, nt, preferred_element_type=jnp.float32)
    left = total.astype(jnp.bfloat16)
    bias = jnp.broadcast_to(br_ref[...], (tile, width)).T
    for d in range(side):
        left_out[d][0] = left[d * rows : (d + 1) * rows]
        b = place_ref[1] ^ d
        block = normed_ref[pl.ds(pl.multiple_of(b * tile, tile), tile), :]
        right = lax.dot_general(wr_ref[...], block, nt, preferred_element_type=jnp.float32) + bias
        right_out[d][:, 0] = right.astype(jnp.bfloat16).reshape(PARTS, width // PARTS, tile)


def project(side, place, x, gain, offset, wl, bl, wr, br):
    seqs, residues, chans = x.shape
    width = wl.shape[1]
    tile = residues // side
    rows = tile * width // LANES
    some = width // PARTS
    whole = lambda *shape: pl.BlockSpec(shape, lambda s, place: (0,) * len(shape))
    out = pl.pallas_call(
        functools.partial(project_kernel, side),
        grid_spec=pltpu.PrefetchScalarGridSpec(
            num_scalar_prefetch=1,
            grid=(seqs,),
            in_specs=[
                pl.BlockSpec((1, residues, chans), lambda s, place: (s, 0, 0)),
                whole(1, chans),
                whole(1, chans),
                whole(width, chans),
                whole(1, width),
                whole(width, chans),
                whole(1, width),
            ],
            out_specs=[pl.BlockSpec((1, rows, LANES), lambda s, place: (s, 0, 0))] * side
            + [pl.BlockSpec((PARTS, 1, some, tile), lambda s, place: (0, s, 0, 0))] * side,
            scratch_shapes=[pltpu.VMEM((residues, chans), jnp.bfloat16)],
        ),
        out_shape=[jax.ShapeDtypeStruct((seqs, rows, LANES), jnp.bfloat16)] * side
        + [jax.ShapeDtypeStruct((PARTS, seqs, some, tile), jnp.bfloat16)] * side,
        compiler_params=pltpu.CompilerParams(vmem_limit_bytes=60 * MIB),
        name="project",
    )(place, x, gain[None], offset[None], wl.T, bl[None], wr.T, br[None])
    return out[:side], out[side:]


def update_kernel(side, seqs, order, lefts, first, last, *refs):
    left_refs, refs = refs[:lefts], refs[lefts:]
    right_refs, refs = refs[:side], refs[side:]
    wt_ref, refs = refs[0], refs[1:]
    if not first:
        before_ref, refs = refs[0], refs[1:]
    if last:
        bias_ref, pair_ref, refs = refs[0], refs[1], refs[2:]
    out_ref, left_wide, right_wide, right_flat, outer = refs
    _, rows, lanes = left_refs[0].shape
    _, some, tile = right_refs[0].shape
    depth = right_flat.shape[0]
    pack = tile // rows
    width = lanes // pack
    halves = pack // 2
    group = outer.shape[0] // halves
    seq_total = side * side * seqs
    step = pl.program_id(0)

    @pl.when(step == 0)
    def _():
        at = 0
        for ref in left_refs:
            count = ref.shape[0] * rows
            left_wide[at : at + count] = ref[...].astype(jnp.float32).reshape(count, lanes)
            at += count
        for dz in range(side):
            for k, dy in enumerate(order):
                to = (k * side + dz) * seqs
                right_wide[to * some : (to + seqs) * some] = (
                    right_refs[dz][dy * seqs : (dy + 1) * seqs]
                    .astype(jnp.float32)
                    .reshape(seqs * some, tile)
                )
        if depth > seq_total:
            left_wide[seq_total * rows :] = jnp.zeros(
                ((depth - seq_total) * rows, lanes), jnp.float32
            )
            right_wide[seq_total * some :] = jnp.zeros(
                ((depth - seq_total) * some, tile), jnp.float32
            )
        for e in range(some):
            right_flat[:, e * tile : (e + 1) * tile] = right_wide[
                pl.ds(e, depth, stride=some), :
            ].astype(jnp.bfloat16)

    for q in range(group):
        x = left_wide[pl.ds(step * group + q, depth, stride=rows), :]
        left = x.T.astype(jnp.bfloat16)
        for n in range(some // 2):
            both = jnp.dot(
                left, right_flat[:, 2 * n * tile : (2 * n + 2) * tile], preferred_element_type=jnp.float32
            ).astype(jnp.bfloat16)
            for k in range(2):
                e = 2 * n + k
                for h in range(pack):
                    outer[
                        q * halves + h // 2,
                        e * width : (e + 1) * width,
                        (h % 2) * tile : (h % 2 + 1) * tile,
                    ] = both[h * width : (h + 1) * width, k * tile : (k + 1) * tile]
    for q in range(group):
        for g in range(halves):
            update = jnp.dot(wt_ref[...], outer[q * halves + g], preferred_element_type=jnp.float32)
            if not first:
                update = update + before_ref[q, g]
            if not last:
                out_ref[q, g] = update
                continue
            for k in range(2):
                h = 2 * g + k
                share = update[:, k * tile : (k + 1) * tile].T * (1.0 / seq_total) + bias_ref[...]
                out_ref[h, q] = (pair_ref[h, q].astype(jnp.float32) + share).astype(jnp.bfloat16)


def update_part(side, seqs, order, part, left, right, wt, before, bias, pair):
    _, rows, lanes = left[0].shape
    _, some, tile = right[0].shape
    chans = wt.shape[0]
    pack = tile // rows
    width = lanes // pack
    halves = pack // 2
    depth = -(-side * side * seqs // LANES) * LANES
    group = 4
    first, last = part == 0, part == PARTS - 1
    whole = lambda shape: pl.BlockSpec(shape, lambda g: (0,) * len(shape))
    sum_spec = pl.BlockSpec((group, halves, chans, 2 * tile), lambda g: (g, 0, 0, 0))
    pair_spec = pl.BlockSpec((pack, group, tile, chans), lambda g: (0, g, 0, 0))
    operands = list(left) + list(right) + [wt]
    specs = [whole(x.shape) for x in operands[:-1]]
    specs.append(pl.BlockSpec((chans, some * width), lambda g: (0, part)))
    if not first:
        operands.append(before)
        specs.append(sum_spec)
    if last:
        operands += [bias[None], pair.reshape(pack, rows, tile, chans)]
        specs += [whole((1, chans)), pair_spec]
        out_shape, out_spec = jax.ShapeDtypeStruct((pack, rows, tile, chans), jnp.bfloat16), pair_spec
    else:
        out_shape = jax.ShapeDtypeStruct((rows, halves, chans, 2 * tile), jnp.float32)
        out_spec = sum_spec
    return pl.pallas_call(
        functools.partial(update_kernel, side, seqs, order, len(left), first, last),
        grid=(rows // group,),
        in_specs=specs,
        out_specs=out_spec,
        out_shape=out_shape,
        scratch_shapes=[
            pltpu.VMEM((depth * rows, lanes), jnp.float32),
            pltpu.VMEM((depth * some, tile), jnp.float32),
            pltpu.VMEM((depth, some * tile), jnp.bfloat16),
            pltpu.VMEM((group * halves, some * width, 2 * tile), jnp.bfloat16),
        ],
        compiler_params=pltpu.CompilerParams(vmem_limit_bytes=48 * MIB),
        cost_estimate=pl.CostEstimate(
            flops=2 * tile * tile * some * width * (side * side * seqs + chans),
            bytes_accessed=16 * MIB,
            transcendentals=0,
        ),
        name="update_%d" % part,
    )(*operands)


def local(
    alignment_features,
    pairwise_features,
    standardize_scaling,
    standardize_additive,
    first_factor_matrix,
    first_factor_intercept,
    second_factor_matrix,
    second_factor_intercept,
    final_matrix,
    final_intercept,
):
    devices = lax.axis_size("row")
    side = math.isqrt(devices)
    me = lax.axis_index("row")
    place = jnp.stack([me // side, me % side]).astype(jnp.int32)
    seqs, residues, _ = alignment_features.shape
    tile = residues // side
    width = first_factor_matrix.shape[1]
    left, right = project(
        side,
        place,
        alignment_features,
        standardize_scaling,
        standardize_additive,
        first_factor_matrix,
        first_factor_intercept,
        second_factor_matrix,
        second_factor_intercept,
    )

    def swap(x, da, db):
        return lax.ppermute(x, "row", [(i, i ^ (da * side + db)) for i in range(devices)])

    right = [right[0]] + [swap(right[d], 0, d) for d in range(1, side)]
    left = jnp.concatenate([left[0]] + [swap(left[d], d, 0) for d in range(1, side)])
    parts = []
    for part in range(PARTS):
        mine = jnp.concatenate([x[part] for x in right])
        parts.append([mine] + [swap(mine, d, 0) for d in range(1, side)])
    order = [0]
    lefts = [left]
    step = side // 2
    while step > 0:
        left = jnp.concatenate(lefts) if len(lefts) > 1 else lefts[0]
        lefts = [left, swap(left, 0, step)]
        order += [o ^ step for o in order]
        step //= 2
    wt = final_matrix.reshape(width, width, -1).transpose(2, 1, 0).reshape(-1, width * width)
    total = None
    for part in range(PARTS):
        total = update_part(
            side, seqs, order, part, lefts, parts[part], wt, total, final_intercept, pairwise_features
        )
    return total.reshape(1, tile, tile, -1)


def solution(mesh):
    placed = (
        P(("grp", "row"), None, None),
        P(("grp", "row"), None, None, None),
        P(),
        P(),
        P(),
        P(),
        P(),
        P(),
        P(),
        P(),
    )
    return jax.shard_map(
        local,
        mesh=mesh,
        in_specs=placed,
        out_specs=P(("grp", "row"), None, None, None),
        check_vma=False,
    )
```

```python
import functools
import math

import jax
import jax.numpy as jnp
from jax import lax
from jax.experimental import pallas as pl
from jax.experimental.pallas import tpu as pltpu
from jax.sharding import PartitionSpec as P

LANES = 128
PARTS = 1
MIB = 1024 * 1024


def project_kernel(side, *refs):
    sources, refs = refs[:7], refs[7:]
    left_out, right_out, refs = refs[:side], refs[side : 2 * side], refs[2 * side :]
    buffers, normed_ref, sems, x_sems = refs[:7], refs[7], refs[8], refs[9]
    x_ref, gain_ref, offset_ref, wl_ref, bl_ref, wr_ref, br_ref = buffers
    seqs, residues, chans = x_ref.shape
    width = wl_ref.shape[0]
    tile = residues // side
    pack = LANES // width
    rows = tile // pack
    x_copies = [
        pltpu.make_async_copy(sources[0].at[s], x_ref.at[s], x_sems.at[s]) for s in range(seqs)
    ]
    copies = [
        pltpu.make_async_copy(sources[k], buffers[k], sems.at[k]) for k in range(1, len(buffers))
    ]
    for copy in x_copies[:1] + copies + x_copies[1:]:
        copy.start()
    for copy in copies:
        copy.wait()
    me = lax.axis_index("row")
    place_a, place_b = me // side, lax.rem(me, side)
    nt = (((1,), (1,)), ((), ()))
    wl = wl_ref[...]
    placed = [
        jnp.concatenate([wl if k == h else jnp.zeros_like(wl) for k in range(pack)], axis=0)
        for h in range(pack)
    ]
    left_bias = jnp.concatenate([bl_ref[...]] * pack, axis=1)
    right_bias = jnp.broadcast_to(br_ref[...], (tile, width)).T
    for s in range(seqs):
        x_copies[s].wait()
        normed = normed_ref.at[s % 2]
        x = x_ref[s].astype(jnp.float32)
        center = x - jnp.mean(x, axis=-1, keepdims=True)
        variance = jnp.mean(center * center, axis=-1, keepdims=True)
        normed[...] = (
            center * lax.rsqrt(variance + 1e-05) * gain_ref[...] + offset_ref[...]
        ).astype(jnp.bfloat16)
        blocks = []
        for d in range(side):
            b = place_b ^ d
            block = normed[pl.ds(pl.multiple_of(b * tile, tile), tile), :]
            right = lax.dot_general(wr_ref[...], block, nt, preferred_element_type=jnp.float32)
            right_out[d][:, s] = (
                (right + right_bias).astype(jnp.bfloat16).reshape(PARTS, width // PARTS, tile)
            )
            a = place_a ^ d
            blocks.append(normed[pl.ds(pl.multiple_of(a * tile, tile), tile), :])
        total = left_bias
        for h in range(pack):
            picked = jnp.concatenate([block[h * rows : (h + 1) * rows] for block in blocks], axis=0)
            total = total + lax.dot_general(
                picked, placed[h], nt, preferred_element_type=jnp.float32
            )
        left = total.astype(jnp.bfloat16)
        for d in range(side):
            left_out[d][s] = left[d * rows : (d + 1) * rows]


def project(side, x, gain, offset, wl, bl, wr, br):
    seqs, residues, chans = x.shape
    width = wl.shape[1]
    tile = residues // side
    rows = tile * width // LANES
    operands = (x, gain[None], offset[None], wl.T, bl[None], wr.T, br[None])
    out = pl.pallas_call(
        functools.partial(project_kernel, side),
        in_specs=[pl.BlockSpec(memory_space=pltpu.HBM)] * len(operands),
        out_specs=[pl.BlockSpec(memory_space=pltpu.VMEM)] * (2 * side),
        out_shape=[jax.ShapeDtypeStruct((seqs, rows, LANES), jnp.bfloat16)] * side
        + [jax.ShapeDtypeStruct((PARTS, seqs, width // PARTS, tile), jnp.bfloat16)] * side,
        scratch_shapes=[pltpu.VMEM(o.shape, o.dtype) for o in operands]
        + [
            pltpu.VMEM((2, residues, chans), jnp.bfloat16),
            pltpu.SemaphoreType.DMA((len(operands),)),
            pltpu.SemaphoreType.DMA((seqs,)),
        ],
        compiler_params=pltpu.CompilerParams(vmem_limit_bytes=32 * MIB),
        name="project",
    )(*operands)
    return out[:side], out[side:]


def update_kernel(side, seqs, order, lefts, first, last, *refs):
    left_refs, refs = refs[:lefts], refs[lefts:]
    right_refs, refs = refs[:side], refs[side:]
    wt_ref, refs = refs[0], refs[1:]
    if not first:
        before_ref, refs = refs[0], refs[1:]
    if last:
        bias_ref, pair_ref, refs = refs[0], refs[1], refs[2:]
    out_ref, left_wide, right_wide, right_flat, outer = refs
    _, rows, lanes = left_refs[0].shape
    _, some, tile = right_refs[0].shape
    depth = right_flat.shape[0]
    pack = tile // rows
    width = lanes // pack
    halves = pack // 2
    group = outer.shape[0] // halves
    seq_total = side * side * seqs
    step = pl.program_id(0)

    @pl.when(step == 0)
    def _():
        at = 0
        for ref in left_refs:
            count = ref.shape[0] * rows
            left_wide[at : at + count] = ref[...].astype(jnp.float32).reshape(count, lanes)
            at += count
        for dz in range(side):
            for k, dy in enumerate(order):
                to = (k * side + dz) * seqs
                right_wide[to * some : (to + seqs) * some] = (
                    right_refs[dz][dy * seqs : (dy + 1) * seqs]
                    .astype(jnp.float32)
                    .reshape(seqs * some, tile)
                )
        if depth > seq_total:
            left_wide[seq_total * rows :] = jnp.zeros(
                ((depth - seq_total) * rows, lanes), jnp.float32
            )
            right_wide[seq_total * some :] = jnp.zeros(
                ((depth - seq_total) * some, tile), jnp.float32
            )
        for e in range(some):
            right_flat[:, e * tile : (e + 1) * tile] = right_wide[
                pl.ds(e, depth, stride=some), :
            ].astype(jnp.bfloat16)

    for q in range(group):
        x = left_wide[pl.ds(step * group + q, depth, stride=rows), :]
        left = x.T.astype(jnp.bfloat16)
        for n in range(some // 2):
            both = jnp.dot(
                left, right_flat[:, 2 * n * tile : (2 * n + 2) * tile], preferred_element_type=jnp.float32
            ).astype(jnp.bfloat16)
            for k in range(2):
                e = 2 * n + k
                for h in range(pack):
                    outer[
                        q * halves + h // 2,
                        e * width : (e + 1) * width,
                        (h % 2) * tile : (h % 2 + 1) * tile,
                    ] = both[h * width : (h + 1) * width, k * tile : (k + 1) * tile]
    for q in range(group):
        for g in range(halves):
            update = jnp.dot(wt_ref[...], outer[q * halves + g], preferred_element_type=jnp.float32)
            if not first:
                update = update + before_ref[q, g]
            if not last:
                out_ref[q, g] = update
                continue
            for k in range(2):
                h = 2 * g + k
                share = update[:, k * tile : (k + 1) * tile].T * (1.0 / seq_total) + bias_ref[...]
                out_ref[h, q] = (pair_ref[h, q].astype(jnp.float32) + share).astype(jnp.bfloat16)


def update_part(side, seqs, order, part, left, right, wt, before, bias, pair):
    _, rows, lanes = left[0].shape
    _, some, tile = right[0].shape
    chans = wt.shape[0]
    pack = tile // rows
    width = lanes // pack
    halves = pack // 2
    depth = -(-side * side * seqs // LANES) * LANES
    group = 4
    first, last = part == 0, part == PARTS - 1
    whole = lambda shape: pl.BlockSpec(shape, lambda g: (0,) * len(shape))
    sum_spec = pl.BlockSpec((group, halves, chans, 2 * tile), lambda g: (g, 0, 0, 0))
    pair_spec = pl.BlockSpec((pack, group, tile, chans), lambda g: (0, g, 0, 0))
    operands = list(left) + list(right) + [wt]
    specs = [whole(x.shape) for x in operands[:-1]]
    specs.append(pl.BlockSpec((chans, some * width), lambda g: (0, part)))
    if not first:
        operands.append(before)
        specs.append(sum_spec)
    if last:
        operands += [bias[None], pair.reshape(pack, rows, tile, chans)]
        specs += [whole((1, chans)), pair_spec]
        out_shape, out_spec = jax.ShapeDtypeStruct((pack, rows, tile, chans), jnp.bfloat16), pair_spec
    else:
        out_shape = jax.ShapeDtypeStruct((rows, halves, chans, 2 * tile), jnp.float32)
        out_spec = sum_spec
    return pl.pallas_call(
        functools.partial(update_kernel, side, seqs, order, len(left), first, last),
        grid=(rows // group,),
        in_specs=specs,
        out_specs=out_spec,
        out_shape=out_shape,
        scratch_shapes=[
            pltpu.VMEM((depth * rows, lanes), jnp.float32),
            pltpu.VMEM((depth * some, tile), jnp.float32),
            pltpu.VMEM((depth, some * tile), jnp.bfloat16),
            pltpu.VMEM((group * halves, some * width, 2 * tile), jnp.bfloat16),
        ],
        compiler_params=pltpu.CompilerParams(vmem_limit_bytes=48 * MIB),
        cost_estimate=pl.CostEstimate(
            flops=2 * tile * tile * some * width * (side * side * seqs + chans),
            bytes_accessed=16 * MIB,
            transcendentals=0,
        ),
        name="update_%d" % part,
    )(*operands)


def local(
    alignment_features,
    pairwise_features,
    standardize_scaling,
    standardize_additive,
    first_factor_matrix,
    first_factor_intercept,
    second_factor_matrix,
    second_factor_intercept,
    final_matrix,
    final_intercept,
):
    devices = lax.axis_size("row")
    side = math.isqrt(devices)
    seqs, residues, _ = alignment_features.shape
    tile = residues // side
    width = first_factor_matrix.shape[1]
    left, right = project(
        side,
        alignment_features,
        standardize_scaling,
        standardize_additive,
        first_factor_matrix,
        first_factor_intercept,
        second_factor_matrix,
        second_factor_intercept,
    )

    def swap(x, da, db):
        return lax.ppermute(x, "row", [(i, i ^ (da * side + db)) for i in range(devices)])

    right = [right[0]] + [swap(right[d], 0, d) for d in range(1, side)]
    *left, right[1] = lax.optimization_barrier((*left, right[1]))
    left = jnp.concatenate([left[0]] + [swap(left[d], d, 0) for d in range(1, side)])
    parts = []
    for part in range(PARTS):
        mine = jnp.concatenate([x[part] for x in right])
        if part > 0:
            mine, left = lax.optimization_barrier((mine, left))
        parts.append([mine] + [swap(mine, d, 0) for d in range(1, side)])
    order = [0]
    lefts = [left]
    step = side // 2
    while step > 0:
        left = jnp.concatenate(lefts) if len(lefts) > 1 else lefts[0]
        if len(lefts) > 1:
            left, parts[0][1] = lax.optimization_barrier((left, parts[0][1]))
        lefts = [left, swap(left, 0, step)]
        order += [o ^ step for o in order]
        step //= 2
    wt = final_matrix.reshape(width, width, -1).transpose(2, 1, 0).reshape(-1, width * width)
    total = None
    for part in range(PARTS):
        total = update_part(
            side, seqs, order, part, lefts, parts[part], wt, total, final_intercept, pairwise_features
        )
    return total.reshape(1, tile, tile, -1)


def solution(mesh):
    placed = (
        P(("grp", "row"), None, None),
        P(("grp", "row"), None, None, None),
        P(),
        P(),
        P(),
        P(),
        P(),
        P(),
        P(),
        P(),
    )
    return jax.shard_map(
        local,
        mesh=mesh,
        in_specs=placed,
        out_specs=P(("grp", "row"), None, None, None),
        check_vma=False,
    )
```

```python
import functools
import math

import jax
import jax.numpy as jnp
from jax import lax
from jax.experimental import pallas as pl
from jax.experimental.pallas import tpu as pltpu
from jax.sharding import PartitionSpec as P

LANES = 128
PARTS = 2
MIB = 1024 * 1024


def in_hbm(x):
    return pltpu.with_memory_space_constraint(x, pltpu.HBM)


def project_kernel(side, *refs):
    sources, refs = refs[:7], refs[7:]
    left_out, right_out, refs = refs[:side], refs[side : 2 * side], refs[2 * side :]
    buffers, normed_ref, sems, x_sems = refs[:7], refs[7], refs[8], refs[9]
    x_ref, gain_ref, offset_ref, wl_ref, bl_ref, wr_ref, br_ref = buffers
    seqs, residues, chans = x_ref.shape
    width = wl_ref.shape[0]
    tile = residues // side
    pack = LANES // width
    rows = tile // pack
    x_copies = [
        pltpu.make_async_copy(sources[0].at[s], x_ref.at[s], x_sems.at[s]) for s in range(seqs)
    ]
    copies = [
        pltpu.make_async_copy(sources[k], buffers[k], sems.at[k]) for k in range(1, len(buffers))
    ]
    for copy in x_copies[:1] + copies + x_copies[1:]:
        copy.start()
    for copy in copies:
        copy.wait()
    me = lax.axis_index("row")
    place_a, place_b = me // side, lax.rem(me, side)
    nt = (((1,), (1,)), ((), ()))
    wl = wl_ref[...]
    placed = [
        jnp.concatenate([wl if k == h else jnp.zeros_like(wl) for k in range(pack)], axis=0)
        for h in range(pack)
    ]
    left_bias = jnp.concatenate([bl_ref[...]] * pack, axis=1)
    right_bias = jnp.broadcast_to(br_ref[...], (tile, width)).T
    for s in range(seqs):
        x_copies[s].wait()
        normed = normed_ref.at[s % 2]
        x = x_ref[s].astype(jnp.float32)
        center = x - jnp.mean(x, axis=-1, keepdims=True)
        variance = jnp.mean(center * center, axis=-1, keepdims=True)
        normed[...] = (
            center * lax.rsqrt(variance + 1e-05) * gain_ref[...] + offset_ref[...]
        ).astype(jnp.bfloat16)
        blocks = []
        for d in range(side):
            b = place_b ^ d
            block = normed[pl.ds(pl.multiple_of(b * tile, tile), tile), :]
            right = lax.dot_general(wr_ref[...], block, nt, preferred_element_type=jnp.float32)
            right_out[d][:, s] = (
                (right + right_bias).astype(jnp.bfloat16).reshape(PARTS, width // PARTS, tile)
            )
            a = place_a ^ d
            blocks.append(normed[pl.ds(pl.multiple_of(a * tile, tile), tile), :])
        total = left_bias
        for h in range(pack):
            picked = jnp.concatenate([block[h * rows : (h + 1) * rows] for block in blocks], axis=0)
            total = total + lax.dot_general(
                picked, placed[h], nt, preferred_element_type=jnp.float32
            )
        left = total.astype(jnp.bfloat16)
        for d in range(side):
            left_out[d][s] = left[d * rows : (d + 1) * rows]


def project(side, x, gain, offset, wl, bl, wr, br):
    seqs, residues, chans = x.shape
    width = wl.shape[1]
    tile = residues // side
    rows = tile * width // LANES
    operands = [in_hbm(o) for o in (x, gain[None], offset[None], wl.T, bl[None], wr.T, br[None])]
    out = pl.pallas_call(
        functools.partial(project_kernel, side),
        in_specs=[pl.BlockSpec(memory_space=pltpu.HBM)] * len(operands),
        out_specs=[pl.BlockSpec(memory_space=pltpu.VMEM)] * (2 * side),
        out_shape=[jax.ShapeDtypeStruct((seqs, rows, LANES), jnp.bfloat16)] * side
        + [jax.ShapeDtypeStruct((PARTS, seqs, width // PARTS, tile), jnp.bfloat16)] * side,
        scratch_shapes=[pltpu.VMEM(o.shape, o.dtype) for o in operands]
        + [
            pltpu.VMEM((2, residues, chans), jnp.bfloat16),
            pltpu.SemaphoreType.DMA((len(operands),)),
            pltpu.SemaphoreType.DMA((seqs,)),
        ],
        compiler_params=pltpu.CompilerParams(vmem_limit_bytes=32 * MIB),
        name="project",
    )(*operands)
    return out[:side], out[side:]


def update_kernel(side, seqs, order, lefts, first, last, *refs):
    left_refs, refs = refs[:lefts], refs[lefts:]
    right_refs, refs = refs[:side], refs[side:]
    wt_ref, refs = refs[0], refs[1:]
    if not first:
        before_ref, refs = refs[0], refs[1:]
    if last:
        bias_ref, pair_ref, refs = refs[0], refs[1], refs[2:]
    out_ref, left_wide, right_wide, right_flat, outer = refs
    _, rows, lanes = left_refs[0].shape
    _, some, tile = right_refs[0].shape
    depth = right_flat.shape[0]
    pack = tile // rows
    width = lanes // pack
    halves = pack // 2
    group = outer.shape[0] // halves
    seq_total = side * side * seqs
    step = pl.program_id(0)

    @pl.when(step == 0)
    def _():
        at = 0
        for ref in left_refs:
            count = ref.shape[0] * rows
            left_wide[at : at + count] = ref[...].astype(jnp.float32).reshape(count, lanes)
            at += count
        for dz in range(side):
            for k, dy in enumerate(order):
                to = (k * side + dz) * seqs
                right_wide[to * some : (to + seqs) * some] = (
                    right_refs[dz][dy * seqs : (dy + 1) * seqs]
                    .astype(jnp.float32)
                    .reshape(seqs * some, tile)
                )
        if depth > seq_total:
            left_wide[seq_total * rows :] = jnp.zeros(
                ((depth - seq_total) * rows, lanes), jnp.float32
            )
            right_wide[seq_total * some :] = jnp.zeros(
                ((depth - seq_total) * some, tile), jnp.float32
            )
        for e in range(some):
            right_flat[:, e * tile : (e + 1) * tile] = right_wide[
                pl.ds(e, depth, stride=some), :
            ].astype(jnp.bfloat16)

    for q in range(group):
        x = left_wide[pl.ds(step * group + q, depth, stride=rows), :]
        left = x.T.astype(jnp.bfloat16)
        for n in range(some // 2):
            both = jnp.dot(
                left, right_flat[:, 2 * n * tile : (2 * n + 2) * tile], preferred_element_type=jnp.float32
            ).astype(jnp.bfloat16)
            for k in range(2):
                e = 2 * n + k
                for h in range(pack):
                    outer[
                        q * halves + h // 2,
                        e * width : (e + 1) * width,
                        (h % 2) * tile : (h % 2 + 1) * tile,
                    ] = both[h * width : (h + 1) * width, k * tile : (k + 1) * tile]
    for q in range(group):
        for g in range(halves):
            update = jnp.dot(wt_ref[...], outer[q * halves + g], preferred_element_type=jnp.float32)
            if not first:
                update = update + before_ref[q, g]
            if not last:
                out_ref[q, g] = update
                continue
            for k in range(2):
                h = 2 * g + k
                share = update[:, k * tile : (k + 1) * tile].T * (1.0 / seq_total) + bias_ref[...]
                out_ref[h, q] = (pair_ref[h, q].astype(jnp.float32) + share).astype(jnp.bfloat16)


def update_part(side, seqs, order, part, left, right, wt, before, bias, pair):
    _, rows, lanes = left[0].shape
    _, some, tile = right[0].shape
    chans = wt.shape[0]
    pack = tile // rows
    width = lanes // pack
    halves = pack // 2
    depth = -(-side * side * seqs // LANES) * LANES
    group = 8
    first, last = part == 0, part == PARTS - 1
    whole = lambda shape: pl.BlockSpec(shape, lambda g: (0,) * len(shape))
    sum_spec = pl.BlockSpec((group, halves, chans, 2 * tile), lambda g: (g, 0, 0, 0))
    pair_spec = pl.BlockSpec((pack, group, tile, chans), lambda g: (0, g, 0, 0))
    operands = list(left) + list(right) + [wt]
    specs = [whole(x.shape) for x in operands[:-1]]
    specs.append(pl.BlockSpec((chans, some * width), lambda g: (0, part)))
    if not first:
        operands.append(before)
        specs.append(sum_spec)
    if last:
        operands += [in_hbm(bias[None]), in_hbm(pair.reshape(pack, rows, tile, chans))]
        specs += [whole((1, chans)), pair_spec]
        out_shape, out_spec = jax.ShapeDtypeStruct((pack, rows, tile, chans), jnp.bfloat16), pair_spec
    else:
        out_shape = jax.ShapeDtypeStruct((rows, halves, chans, 2 * tile), jnp.float32)
        out_spec = sum_spec
    return pl.pallas_call(
        functools.partial(update_kernel, side, seqs, order, len(left), first, last),
        grid=(rows // group,),
        in_specs=specs,
        out_specs=out_spec,
        out_shape=out_shape,
        scratch_shapes=[
            pltpu.VMEM((depth * rows, lanes), jnp.float32),
            pltpu.VMEM((depth * some, tile), jnp.float32),
            pltpu.VMEM((depth, some * tile), jnp.bfloat16),
            pltpu.VMEM((group * halves, some * width, 2 * tile), jnp.bfloat16),
        ],
        compiler_params=pltpu.CompilerParams(vmem_limit_bytes=48 * MIB),
        cost_estimate=pl.CostEstimate(
            flops=2 * tile * tile * some * width * (side * side * seqs + chans),
            bytes_accessed=16 * MIB,
            transcendentals=0,
        ),
        name="update_%d" % part,
    )(*operands)


def local(
    alignment_features,
    pairwise_features,
    standardize_scaling,
    standardize_additive,
    first_factor_matrix,
    first_factor_intercept,
    second_factor_matrix,
    second_factor_intercept,
    final_matrix,
    final_intercept,
):
    devices = lax.axis_size("row")
    side = math.isqrt(devices)
    seqs, residues, _ = alignment_features.shape
    tile = residues // side
    width = first_factor_matrix.shape[1]
    left, right = project(
        side,
        alignment_features,
        standardize_scaling,
        standardize_additive,
        first_factor_matrix,
        first_factor_intercept,
        second_factor_matrix,
        second_factor_intercept,
    )

    def swap(x, da, db):
        return lax.ppermute(x, "row", [(i, i ^ (da * side + db)) for i in range(devices)])

    right = [right[0]] + [swap(right[d], 0, d) for d in range(1, side)]
    *left, right[1] = lax.optimization_barrier((*left, right[1]))
    left = jnp.concatenate([left[0]] + [swap(left[d], d, 0) for d in range(1, side)])
    parts = []
    for part in range(PARTS):
        mine = jnp.concatenate([x[part] for x in right])
        parts.append([mine] + [swap(mine, d, 0) for d in range(1, side)])
    order = [0]
    lefts = [left]
    step = side // 2
    while step > 0:
        left = jnp.concatenate(lefts) if len(lefts) > 1 else lefts[0]
        if len(lefts) > 1:
            left, *parts[0] = lax.optimization_barrier((left, *parts[0]))
        lefts = [left, swap(left, 0, step)]
        order += [o ^ step for o in order]
        step //= 2
    wt = final_matrix.reshape(width, width, -1).transpose(2, 1, 0).reshape(-1, width * width)
    total = None
    for part in range(PARTS):
        total = update_part(
            side, seqs, order, part, lefts, parts[part], wt, total, final_intercept, pairwise_features
        )
    return total.reshape(1, tile, tile, -1)


def solution(mesh):
    placed = (
        P(("grp", "row"), None, None),
        P(("grp", "row"), None, None, None),
        P(),
        P(),
        P(),
        P(),
        P(),
        P(),
        P(),
        P(),
    )
    return jax.shard_map(
        local,
        mesh=mesh,
        in_specs=placed,
        out_specs=P(("grp", "row"), None, None, None),
        check_vma=False,
    )
```

```python
import functools
import math

import jax
import jax.numpy as jnp
from jax import lax
from jax.experimental import pallas as pl
from jax.experimental.pallas import tpu as pltpu
from jax.sharding import PartitionSpec as P

LANES = 128
PARTS = 2
MIB = 1024 * 1024


def in_hbm(x):
    return pltpu.with_memory_space_constraint(x, pltpu.HBM)


def project_kernel(side, *refs):
    sources, refs = refs[:7], refs[7:]
    left_out, right_out, refs = refs[:side], refs[side : side + PARTS], refs[side + PARTS :]
    buffers, normed_ref, sems, x_sems = refs[:7], refs[7], refs[8], refs[9]
    x_ref, gain_ref, offset_ref, wl_ref, bl_ref, wr_ref, br_ref = buffers
    seqs, residues, chans = x_ref.shape
    width = wl_ref.shape[0]
    tile = residues // side
    pack = LANES // width
    rows = tile // pack
    some = width // PARTS
    x_copies = [
        pltpu.make_async_copy(sources[0].at[s], x_ref.at[s], x_sems.at[s]) for s in range(seqs)
    ]
    copies = [
        pltpu.make_async_copy(sources[k], buffers[k], sems.at[k]) for k in range(1, len(buffers))
    ]
    for copy in x_copies[:1] + copies + x_copies[1:]:
        copy.start()
    for copy in copies:
        copy.wait()
    place_a = lax.axis_index("row") // side
    nt = (((1,), (1,)), ((), ()))
    wl = wl_ref[...]
    placed = [
        jnp.concatenate([wl if k == h else jnp.zeros_like(wl) for k in range(pack)], axis=0)
        for h in range(pack)
    ]
    left_bias = jnp.concatenate([bl_ref[...]] * pack, axis=1)
    right_bias = jnp.broadcast_to(br_ref[...], (tile, width)).T
    for s in range(seqs):
        x_copies[s].wait()
        normed = normed_ref.at[s % 2]
        x = x_ref[s].astype(jnp.float32)
        center = x - jnp.mean(x, axis=-1, keepdims=True)
        variance = jnp.mean(center * center, axis=-1, keepdims=True)
        normed[...] = (
            center * lax.rsqrt(variance + 1e-05) * gain_ref[...] + offset_ref[...]
        ).astype(jnp.bfloat16)
        right = lax.dot_general(wr_ref[...], normed[...], nt, preferred_element_type=jnp.float32)
        for b in range(side):
            block = (right[:, b * tile : (b + 1) * tile] + right_bias).astype(jnp.bfloat16)
            for part in range(PARTS):
                for a in range(side):
                    right_out[part][a * side + b, s] = block[part * some : (part + 1) * some]
        blocks = []
        for d in range(side):
            a = place_a ^ d
            blocks.append(normed[pl.ds(pl.multiple_of(a * tile, tile), tile), :])
        total = left_bias
        for h in range(pack):
            picked = jnp.concatenate([block[h * rows : (h + 1) * rows] for block in blocks], axis=0)
            total = total + lax.dot_general(
                picked, placed[h], nt, preferred_element_type=jnp.float32
            )
        left = total.astype(jnp.bfloat16)
        for d in range(side):
            left_out[d][s] = left[d * rows : (d + 1) * rows]


def project(side, x, gain, offset, wl, bl, wr, br):
    seqs, residues, chans = x.shape
    width = wl.shape[1]
    tile = residues // side
    rows = tile * width // LANES
    operands = [in_hbm(o) for o in (x, gain[None], offset[None], wl.T, bl[None], wr.T, br[None])]
    out = pl.pallas_call(
        functools.partial(project_kernel, side),
        in_specs=[pl.BlockSpec(memory_space=pltpu.HBM)] * len(operands),
        out_specs=[pl.BlockSpec(memory_space=pltpu.VMEM)] * (side + PARTS),
        out_shape=[jax.ShapeDtypeStruct((seqs, rows, LANES), jnp.bfloat16)] * side
        + [jax.ShapeDtypeStruct((side * side, seqs, width // PARTS, tile), jnp.bfloat16)] * PARTS,
        scratch_shapes=[pltpu.VMEM(o.shape, o.dtype) for o in operands]
        + [
            pltpu.VMEM((2, residues, chans), jnp.bfloat16),
            pltpu.SemaphoreType.DMA((len(operands),)),
            pltpu.SemaphoreType.DMA((seqs,)),
        ],
        compiler_params=pltpu.CompilerParams(vmem_limit_bytes=32 * MIB),
        name="project",
    )(*operands)
    return out[:side], out[side:]


def update_kernel(side, seqs, order, lefts, first, last, *refs):
    left_refs, refs = refs[:lefts], refs[lefts:]
    right_ref, wt_ref, refs = refs[0], refs[1], refs[2:]
    if not first:
        before_ref, refs = refs[0], refs[1:]
    if last:
        bias_ref, pair_ref, refs = refs[0], refs[1], refs[2:]
    out_ref, left_wide, right_wide, right_flat, outer = refs
    _, rows, lanes = left_refs[0].shape
    _, _, some, tile = right_ref.shape
    depth = right_flat.shape[0]
    pack = tile // rows
    width = lanes // pack
    halves = pack // 2
    group = outer.shape[0] // halves
    seq_total = side * side * seqs
    step = pl.program_id(0)

    @pl.when(step == 0)
    def _():
        me = lax.axis_index("row")
        place_a, place_b = me // side, lax.rem(me, side)
        for k, db in enumerate(order):
            ref = left_refs[k * lefts // side]
            start = (k * side * seqs) % ref.shape[0]
            for dz in range(side):
                piece = ref[start + dz * seqs : start + (dz + 1) * seqs]
                to = ((place_a ^ dz) * side + (place_b ^ db)) * (seqs * rows)
                left_wide[pl.ds(pl.multiple_of(to, seqs * rows), seqs * rows)] = piece.astype(
                    jnp.float32
                ).reshape(seqs * rows, lanes)
        right_wide[: seq_total * some] = (
            right_ref[...].astype(jnp.float32).reshape(seq_total * some, tile)
        )
        if depth > seq_total:
            left_wide[seq_total * rows :] = jnp.zeros(
                ((depth - seq_total) * rows, lanes), jnp.float32
            )
            right_wide[seq_total * some :] = jnp.zeros(
                ((depth - seq_total) * some, tile), jnp.float32
            )
        for e in range(some):
            right_flat[:, e * tile : (e + 1) * tile] = right_wide[
                pl.ds(e, depth, stride=some), :
            ].astype(jnp.bfloat16)

    for q in range(group):
        x = left_wide[pl.ds(step * group + q, depth, stride=rows), :]
        left = x.T.astype(jnp.bfloat16)
        for n in range(some // 2):
            both = jnp.dot(
                left, right_flat[:, 2 * n * tile : (2 * n + 2) * tile], preferred_element_type=jnp.float32
            ).astype(jnp.bfloat16)
            for k in range(2):
                e = 2 * n + k
                for h in range(pack):
                    outer[
                        q * halves + h // 2,
                        e * width : (e + 1) * width,
                        (h % 2) * tile : (h % 2 + 1) * tile,
                    ] = both[h * width : (h + 1) * width, k * tile : (k + 1) * tile]
    for q in range(group):
        for g in range(halves):
            update = jnp.dot(wt_ref[...], outer[q * halves + g], preferred_element_type=jnp.float32)
            if not first:
                update = update + before_ref[q, g]
            if not last:
                out_ref[q, g] = update
                continue
            for k in range(2):
                h = 2 * g + k
                share = update[:, k * tile : (k + 1) * tile].T * (1.0 / seq_total) + bias_ref[...]
                out_ref[h, q] = (pair_ref[h, q].astype(jnp.float32) + share).astype(jnp.bfloat16)


def update_part(side, seqs, order, part, left, right, wt, before, bias, pair):
    _, rows, lanes = left[0].shape
    _, _, some, tile = right.shape
    chans = wt.shape[0]
    pack = tile // rows
    width = lanes // pack
    halves = pack // 2
    depth = -(-side * side * seqs // LANES) * LANES
    group = 8
    first, last = part == 0, part == PARTS - 1
    whole = lambda shape: pl.BlockSpec(shape, lambda g: (0,) * len(shape))
    sum_spec = pl.BlockSpec((group, halves, chans, 2 * tile), lambda g: (g, 0, 0, 0))
    pair_spec = pl.BlockSpec((pack, group, tile, chans), lambda g: (0, g, 0, 0))
    operands = list(left) + [right, wt]
    specs = [whole(x.shape) for x in operands[:-1]]
    specs.append(pl.BlockSpec((chans, some * width), lambda g: (0, part)))
    if not first:
        operands.append(before)
        specs.append(sum_spec)
    if last:
        operands += [in_hbm(bias[None]), in_hbm(pair.reshape(pack, rows, tile, chans))]
        specs += [whole((1, chans)), pair_spec]
        out_shape, out_spec = jax.ShapeDtypeStruct((pack, rows, tile, chans), jnp.bfloat16), pair_spec
    else:
        out_shape = jax.ShapeDtypeStruct((rows, halves, chans, 2 * tile), jnp.float32)
        out_spec = sum_spec
    return pl.pallas_call(
        functools.partial(update_kernel, side, seqs, order, len(left), first, last),
        grid=(rows // group,),
        in_specs=specs,
        out_specs=out_spec,
        out_shape=out_shape,
        scratch_shapes=[
            pltpu.VMEM((depth * rows, lanes), jnp.float32),
            pltpu.VMEM((depth * some, tile), jnp.float32),
            pltpu.VMEM((depth, some * tile), jnp.bfloat16),
            pltpu.VMEM((group * halves, some * width, 2 * tile), jnp.bfloat16),
        ],
        compiler_params=pltpu.CompilerParams(vmem_limit_bytes=48 * MIB),
        cost_estimate=pl.CostEstimate(
            flops=2 * tile * tile * some * width * (side * side * seqs + chans),
            bytes_accessed=16 * MIB,
            transcendentals=0,
        ),
        name="update_%d" % part,
    )(*operands)


def local(
    alignment_features,
    pairwise_features,
    standardize_scaling,
    standardize_additive,
    first_factor_matrix,
    first_factor_intercept,
    second_factor_matrix,
    second_factor_intercept,
    final_matrix,
    final_intercept,
):
    devices = lax.axis_size("row")
    side = math.isqrt(devices)
    seqs, residues, _ = alignment_features.shape
    tile = residues // side
    width = first_factor_matrix.shape[1]
    left, right = project(
        side,
        alignment_features,
        standardize_scaling,
        standardize_additive,
        first_factor_matrix,
        first_factor_intercept,
        second_factor_matrix,
        second_factor_intercept,
    )

    def swap(x, da, db):
        return lax.ppermute(x, "row", [(i, i ^ (da * side + db)) for i in range(devices)])

    left = jnp.concatenate([left[0]] + [swap(left[d], d, 0) for d in range(1, side)])
    parts = []
    for part in range(PARTS):
        mine = right[part]
        if part > 0:
            mine, left = lax.optimization_barrier((mine, left))
        parts.append(lax.all_to_all(mine, "row", 0, 0, tiled=True))
    order = [0]
    lefts = [left]
    step = side // 2
    while step > 0:
        left = jnp.concatenate(lefts) if len(lefts) > 1 else lefts[0]
        lefts = [left, swap(left, 0, step)]
        order += [o ^ step for o in order]
        step //= 2
    wt = final_matrix.reshape(width, width, -1).transpose(2, 1, 0).reshape(-1, width * width)
    total = None
    for part in range(PARTS):
        total = update_part(
            side, seqs, order, part, lefts, parts[part], wt, total, final_intercept, pairwise_features
        )
    return total.reshape(1, tile, tile, -1)


def solution(mesh):
    placed = (
        P(("grp", "row"), None, None),
        P(("grp", "row"), None, None, None),
        P(),
        P(),
        P(),
        P(),
        P(),
        P(),
        P(),
        P(),
    )
    return jax.shard_map(
        local,
        mesh=mesh,
        in_specs=placed,
        out_specs=P(("grp", "row"), None, None, None),
        check_vma=False,
    )
```

```python
import functools
import math

import jax
import jax.numpy as jnp
from jax import lax
from jax.experimental import pallas as pl
from jax.experimental.pallas import tpu as pltpu
from jax.sharding import PartitionSpec as P

LANES = 128
PARTS = 2
MIB = 1024 * 1024


def in_hbm(x):
    return pltpu.with_memory_space_constraint(x, pltpu.HBM)


def project_kernel(side, *refs):
    sources, refs = refs[:7], refs[7:]
    left_out, right_out, refs = refs[:side], refs[side : side + PARTS], refs[side + PARTS :]
    buffers, normed_ref, sems, x_sems = refs[:7], refs[7], refs[8], refs[9]
    x_ref, gain_ref, offset_ref, wl_ref, bl_ref, wr_ref, br_ref = buffers
    seqs, residues, chans = x_ref.shape
    width = wl_ref.shape[0]
    tile = residues // side
    pack = LANES // width
    rows = tile // pack
    some = width // PARTS
    x_copies = [
        pltpu.make_async_copy(sources[0].at[s], x_ref.at[s], x_sems.at[s]) for s in range(seqs)
    ]
    copies = [
        pltpu.make_async_copy(sources[k], buffers[k], sems.at[k]) for k in range(1, len(buffers))
    ]
    for copy in x_copies[:1] + copies + x_copies[1:]:
        copy.start()
    for copy in copies:
        copy.wait()
    place_a = lax.axis_index("row") // side
    nt = (((1,), (1,)), ((), ()))
    wl = wl_ref[...]
    placed = [
        jnp.concatenate([wl if k == h else jnp.zeros_like(wl) for k in range(pack)], axis=0)
        for h in range(pack)
    ]
    left_bias = jnp.concatenate([bl_ref[...]] * pack, axis=1)
    right_bias = jnp.broadcast_to(br_ref[...], (tile, width)).T
    for s in range(seqs):
        x_copies[s].wait()
        normed = normed_ref.at[s % 2]
        x = x_ref[s].astype(jnp.float32)
        center = x - jnp.mean(x, axis=-1, keepdims=True)
        variance = jnp.mean(center * center, axis=-1, keepdims=True)
        normed[...] = (
            center * lax.rsqrt(variance + 1e-05) * gain_ref[...] + offset_ref[...]
        ).astype(jnp.bfloat16)
        right = lax.dot_general(wr_ref[...], normed[...], nt, preferred_element_type=jnp.float32)
        for b in range(side):
            block = (right[:, b * tile : (b + 1) * tile] + right_bias).astype(jnp.bfloat16)
            for part in range(PARTS):
                for a in range(side):
                    right_out[part][a * side + b, s] = block[part * some : (part + 1) * some]
        blocks = []
        for d in range(side):
            a = place_a ^ d
            blocks.append(normed[pl.ds(pl.multiple_of(a * tile, tile), tile), :])
        total = left_bias
        for h in range(pack):
            picked = jnp.concatenate([block[h * rows : (h + 1) * rows] for block in blocks], axis=0)
            total = total + lax.dot_general(
                picked, placed[h], nt, preferred_element_type=jnp.float32
            )
        left = total.astype(jnp.bfloat16)
        for d in range(side):
            left_out[d][s] = left[d * rows : (d + 1) * rows]


def project(side, x, gain, offset, wl, bl, wr, br):
    seqs, residues, chans = x.shape
    width = wl.shape[1]
    tile = residues // side
    rows = tile * width // LANES
    operands = [in_hbm(o) for o in (x, gain[None], offset[None], wl.T, bl[None], wr.T, br[None])]
    out = pl.pallas_call(
        functools.partial(project_kernel, side),
        in_specs=[pl.BlockSpec(memory_space=pltpu.HBM)] * len(operands),
        out_specs=[pl.BlockSpec(memory_space=pltpu.VMEM)] * (side + PARTS),
        out_shape=[jax.ShapeDtypeStruct((seqs, rows, LANES), jnp.bfloat16)] * side
        + [jax.ShapeDtypeStruct((side * side, seqs, width // PARTS, tile), jnp.bfloat16)] * PARTS,
        scratch_shapes=[pltpu.VMEM(o.shape, o.dtype) for o in operands]
        + [
            pltpu.VMEM((2, residues, chans), jnp.bfloat16),
            pltpu.SemaphoreType.DMA((len(operands),)),
            pltpu.SemaphoreType.DMA((seqs,)),
        ],
        compiler_params=pltpu.CompilerParams(vmem_limit_bytes=32 * MIB),
        name="project",
    )(*operands)
    return list(out[:side]), list(out[side:])


def update_kernel(side, seqs, order, lefts, first, last, *refs):
    left_refs, refs = refs[:lefts], refs[lefts:]
    right_ref, wt_ref, refs = refs[0], refs[1], refs[2:]
    if not first:
        before_ref, refs = refs[0], refs[1:]
    if last:
        bias_ref, pair_ref, refs = refs[0], refs[1], refs[2:]
    out_ref, left_wide, right_wide, right_flat, outer = refs
    _, rows, lanes = left_refs[0].shape
    _, _, some, tile = right_ref.shape
    depth = right_flat.shape[0]
    pack = tile // rows
    width = lanes // pack
    halves = pack // 2
    group = outer.shape[0] // halves
    seq_total = side * side * seqs
    step = pl.program_id(0)

    @pl.when(step == 0)
    def _():
        me = lax.axis_index("row")
        place_a, place_b = me // side, lax.rem(me, side)
        for k, db in enumerate(order):
            ref = left_refs[k * lefts // side]
            start = (k * side * seqs) % ref.shape[0]
            for dz in range(side):
                piece = ref[start + dz * seqs : start + (dz + 1) * seqs]
                to = ((place_a ^ dz) * side + (place_b ^ db)) * (seqs * rows)
                left_wide[pl.ds(pl.multiple_of(to, seqs * rows), seqs * rows)] = piece.astype(
                    jnp.float32
                ).reshape(seqs * rows, lanes)
        right_wide[: seq_total * some] = (
            right_ref[...].astype(jnp.float32).reshape(seq_total * some, tile)
        )
        if depth > seq_total:
            left_wide[seq_total * rows :] = jnp.zeros(
                ((depth - seq_total) * rows, lanes), jnp.float32
            )
            right_wide[seq_total * some :] = jnp.zeros(
                ((depth - seq_total) * some, tile), jnp.float32
            )
        for e in range(some):
            right_flat[:, e * tile : (e + 1) * tile] = right_wide[
                pl.ds(e, depth, stride=some), :
            ].astype(jnp.bfloat16)

    for q in range(group):
        x = left_wide[pl.ds(step * group + q, depth, stride=rows), :]
        left = x.T.astype(jnp.bfloat16)
        for n in range(some // 2):
            both = jnp.dot(
                left, right_flat[:, 2 * n * tile : (2 * n + 2) * tile], preferred_element_type=jnp.float32
            ).astype(jnp.bfloat16)
            for k in range(2):
                e = 2 * n + k
                for h in range(pack):
                    outer[
                        q * halves + h // 2,
                        e * width : (e + 1) * width,
                        (h % 2) * tile : (h % 2 + 1) * tile,
                    ] = both[h * width : (h + 1) * width, k * tile : (k + 1) * tile]
    for q in range(group):
        for g in range(halves):
            update = jnp.dot(wt_ref[...], outer[q * halves + g], preferred_element_type=jnp.float32)
            if not first:
                update = update + before_ref[q, g]
            if not last:
                out_ref[q, g] = update
                continue
            for k in range(2):
                h = 2 * g + k
                share = update[:, k * tile : (k + 1) * tile].T * (1.0 / seq_total) + bias_ref[...]
                out_ref[h, q] = (pair_ref[h, q].astype(jnp.float32) + share).astype(jnp.bfloat16)


def update_part(side, seqs, order, part, left, right, wt, before, bias, pair):
    _, rows, lanes = left[0].shape
    _, _, some, tile = right.shape
    chans = wt.shape[0]
    pack = tile // rows
    width = lanes // pack
    halves = pack // 2
    depth = -(-side * side * seqs // LANES) * LANES
    group = 8
    first, last = part == 0, part == PARTS - 1
    whole = lambda shape: pl.BlockSpec(shape, lambda g: (0,) * len(shape))
    sum_spec = pl.BlockSpec((group, halves, chans, 2 * tile), lambda g: (g, 0, 0, 0))
    pair_spec = pl.BlockSpec((pack, group, tile, chans), lambda g: (0, g, 0, 0))
    operands = list(left) + [right, wt]
    specs = [whole(x.shape) for x in operands[:-1]]
    specs.append(pl.BlockSpec((chans, some * width), lambda g: (0, part)))
    if not first:
        operands.append(before)
        specs.append(sum_spec)
    if last:
        operands += [in_hbm(bias[None]), in_hbm(pair.reshape(pack, rows, tile, chans))]
        specs += [whole((1, chans)), pair_spec]
        out_shape, out_spec = jax.ShapeDtypeStruct((pack, rows, tile, chans), jnp.bfloat16), pair_spec
    else:
        out_shape = jax.ShapeDtypeStruct((rows, halves, chans, 2 * tile), jnp.float32)
        out_spec = sum_spec
    return pl.pallas_call(
        functools.partial(update_kernel, side, seqs, order, len(left), first, last),
        grid=(rows // group,),
        in_specs=specs,
        out_specs=out_spec,
        out_shape=out_shape,
        scratch_shapes=[
            pltpu.VMEM((depth * rows, lanes), jnp.float32),
            pltpu.VMEM((depth * some, tile), jnp.float32),
            pltpu.VMEM((depth, some * tile), jnp.bfloat16),
            pltpu.VMEM((group * halves, some * width, 2 * tile), jnp.bfloat16),
        ],
        compiler_params=pltpu.CompilerParams(vmem_limit_bytes=48 * MIB),
        cost_estimate=pl.CostEstimate(flops=MIB, bytes_accessed=MIB, transcendentals=0),
        name="update_%d" % part,
    )(*operands)


def local(
    alignment_features,
    pairwise_features,
    standardize_scaling,
    standardize_additive,
    first_factor_matrix,
    first_factor_intercept,
    second_factor_matrix,
    second_factor_intercept,
    final_matrix,
    final_intercept,
):
    devices = lax.axis_size("row")
    side = math.isqrt(devices)
    seqs, residues, _ = alignment_features.shape
    tile = residues // side
    width = first_factor_matrix.shape[1]
    left, right = project(
        side,
        alignment_features,
        standardize_scaling,
        standardize_additive,
        first_factor_matrix,
        first_factor_intercept,
        second_factor_matrix,
        second_factor_intercept,
    )

    def swap(x, da, db):
        return lax.ppermute(x, "row", [(i, i ^ (da * side + db)) for i in range(devices)])

    left = [left[0]] + [swap(left[d], d, 0) for d in range(1, side)]
    left[1], right[0] = lax.optimization_barrier((left[1], right[0]))
    left = jnp.concatenate(left)
    parts = []
    for part in range(PARTS):
        mine = right[part]
        if part > 0:
            mine, left = lax.optimization_barrier((mine, left))
        parts.append(lax.all_to_all(mine, "row", 0, 0, tiled=True))
    order = [0]
    lefts = [left]
    step = side // 2
    while step > 0:
        left = jnp.concatenate(lefts) if len(lefts) > 1 else lefts[0]
        lefts = [left, swap(left, 0, step)]
        order += [o ^ step for o in order]
        step //= 2
    wt = final_matrix.reshape(width, width, -1).transpose(2, 1, 0).reshape(-1, width * width)
    total = None
    for part in range(PARTS):
        total = update_part(
            side, seqs, order, part, lefts, parts[part], wt, total, final_intercept, pairwise_features
        )
    return total.reshape(1, tile, tile, -1)


def solution(mesh):
    placed = (
        P(("grp", "row"), None, None),
        P(("grp", "row"), None, None, None),
        P(),
        P(),
        P(),
        P(),
        P(),
        P(),
        P(),
        P(),
    )
    return jax.shard_map(
        local,
        mesh=mesh,
        in_specs=placed,
        out_specs=P(("grp", "row"), None, None, None),
        check_vma=False,
    )
```

```python
import functools
import math

import jax
import jax.numpy as jnp
from jax import lax
from jax.experimental import pallas as pl
from jax.experimental.pallas import tpu as pltpu
from jax.sharding import PartitionSpec as P

LANES = 128
PARTS = 2
MIB = 1024 * 1024


def in_hbm(x):
    return pltpu.with_memory_space_constraint(x, pltpu.HBM)


def project_kernel(side, *refs):
    sources, refs = refs[:7], refs[7:]
    left_out, right_out, refs = refs[:side], refs[side : 2 * side], refs[2 * side :]
    buffers, normed_ref, sems, x_sems = refs[:7], refs[7], refs[8], refs[9]
    x_ref, gain_ref, offset_ref, wl_ref, bl_ref, wr_ref, br_ref = buffers
    seqs, residues, chans = x_ref.shape
    width = wl_ref.shape[0]
    tile = residues // side
    pack = LANES // width
    rows = tile // pack
    x_copies = [
        pltpu.make_async_copy(sources[0].at[s], x_ref.at[s], x_sems.at[s]) for s in range(seqs)
    ]
    copies = [
        pltpu.make_async_copy(sources[k], buffers[k], sems.at[k]) for k in range(1, len(buffers))
    ]
    for copy in x_copies[:1] + copies + x_copies[1:]:
        copy.start()
    for copy in copies:
        copy.wait()
    me = lax.axis_index("row")
    place_a, place_b = me // side, lax.rem(me, side)
    nt = (((1,), (1,)), ((), ()))
    wl = wl_ref[...]
    placed = [
        jnp.concatenate([wl if k == h else jnp.zeros_like(wl) for k in range(pack)], axis=0)
        for h in range(pack)
    ]
    left_bias = jnp.concatenate([bl_ref[...]] * pack, axis=1)
    right_bias = jnp.broadcast_to(br_ref[...], (tile, width)).T
    for s in range(seqs):
        x_copies[s].wait()
        normed = normed_ref.at[s % 2]
        x = x_ref[s].astype(jnp.float32)
        center = x - jnp.mean(x, axis=-1, keepdims=True)
        variance = jnp.mean(center * center, axis=-1, keepdims=True)
        normed[...] = (
            center * lax.rsqrt(variance + 1e-05) * gain_ref[...] + offset_ref[...]
        ).astype(jnp.bfloat16)
        blocks = []
        for d in range(side):
            b = place_b ^ d
            block = normed[pl.ds(pl.multiple_of(b * tile, tile), tile), :]
            right = lax.dot_general(wr_ref[...], block, nt, preferred_element_type=jnp.float32)
            right_out[d][:, s] = (
                (right + right_bias).astype(jnp.bfloat16).reshape(PARTS, width // PARTS, tile)
            )
            a = place_a ^ d
            blocks.append(normed[pl.ds(pl.multiple_of(a * tile, tile), tile), :])
        total = left_bias
        for h in range(pack):
            picked = jnp.concatenate([block[h * rows : (h + 1) * rows] for block in blocks], axis=0)
            total = total + lax.dot_general(
                picked, placed[h], nt, preferred_element_type=jnp.float32
            )
        left = total.astype(jnp.bfloat16)
        for d in range(side):
            left_out[d][s] = left[d * rows : (d + 1) * rows]


def project(side, x, gain, offset, wl, bl, wr, br):
    seqs, residues, chans = x.shape
    width = wl.shape[1]
    tile = residues // side
    rows = tile * width // LANES
    operands = [in_hbm(o) for o in (x, gain[None], offset[None], wl.T, bl[None], wr.T, br[None])]
    out = pl.pallas_call(
        functools.partial(project_kernel, side),
        in_specs=[pl.BlockSpec(memory_space=pltpu.HBM)] * len(operands),
        out_specs=[pl.BlockSpec(memory_space=pltpu.VMEM)] * (2 * side),
        out_shape=[jax.ShapeDtypeStruct((seqs, rows, LANES), jnp.bfloat16)] * side
        + [jax.ShapeDtypeStruct((PARTS, seqs, width // PARTS, tile), jnp.bfloat16)] * side,
        scratch_shapes=[pltpu.VMEM(o.shape, o.dtype) for o in operands]
        + [
            pltpu.VMEM((2, residues, chans), jnp.bfloat16),
            pltpu.SemaphoreType.DMA((len(operands),)),
            pltpu.SemaphoreType.DMA((seqs,)),
        ],
        compiler_params=pltpu.CompilerParams(vmem_limit_bytes=32 * MIB),
        name="project",
    )(*operands)
    return out[:side], out[side:]


def update_kernel(side, seqs, order, lefts, first, last, *refs):
    left_refs, refs = refs[:lefts], refs[lefts:]
    right_refs, refs = refs[:side], refs[side:]
    wt_ref, refs = refs[0], refs[1:]
    if not first:
        before_ref, refs = refs[0], refs[1:]
    if last:
        bias_ref, pair_ref, refs = refs[0], refs[1], refs[2:]
    out_ref, left_wide, right_wide, right_flat, outer = refs
    _, rows, lanes = left_refs[0].shape
    _, some, tile = right_refs[0].shape
    depth = right_flat.shape[0]
    pack = tile // rows
    width = lanes // pack
    halves = pack // 2
    group = outer.shape[0] // halves
    seq_total = side * side * seqs
    step = pl.program_id(0)

    @pl.when(step == 0)
    def _():
        at = 0
        for ref in left_refs:
            count = ref.shape[0] * rows
            left_wide[at : at + count] = ref[...].astype(jnp.float32).reshape(count, lanes)
            at += count
        for dz in range(side):
            for k, dy in enumerate(order):
                to = (k * side + dz) * seqs
                right_wide[to * some : (to + seqs) * some] = (
                    right_refs[dz][dy * seqs : (dy + 1) * seqs]
                    .astype(jnp.float32)
                    .reshape(seqs * some, tile)
                )
        if depth > seq_total:
            left_wide[seq_total * rows :] = jnp.zeros(
                ((depth - seq_total) * rows, lanes), jnp.float32
            )
            right_wide[seq_total * some :] = jnp.zeros(
                ((depth - seq_total) * some, tile), jnp.float32
            )
        for e in range(some):
            right_flat[:, e * tile : (e + 1) * tile] = right_wide[
                pl.ds(e, depth, stride=some), :
            ].astype(jnp.bfloat16)

    for q in range(group):
        x = left_wide[pl.ds(step * group + q, depth, stride=rows), :]
        left = x.T.astype(jnp.bfloat16)
        for n in range(some // 2):
            both = jnp.dot(
                left, right_flat[:, 2 * n * tile : (2 * n + 2) * tile], preferred_element_type=jnp.float32
            ).astype(jnp.bfloat16)
            for k in range(2):
                e = 2 * n + k
                for h in range(pack):
                    outer[
                        q * halves + h // 2,
                        e * width : (e + 1) * width,
                        (h % 2) * tile : (h % 2 + 1) * tile,
                    ] = both[h * width : (h + 1) * width, k * tile : (k + 1) * tile]
    for q in range(group):
        for g in range(halves):
            update = jnp.dot(wt_ref[...], outer[q * halves + g], preferred_element_type=jnp.float32)
            if not first:
                update = update + before_ref[q, g]
            if not last:
                out_ref[q, g] = update
                continue
            for k in range(2):
                h = 2 * g + k
                share = update[:, k * tile : (k + 1) * tile].T * (1.0 / seq_total) + bias_ref[...]
                out_ref[h, q] = (pair_ref[h, q].astype(jnp.float32) + share).astype(jnp.bfloat16)


def update_part(side, seqs, order, part, left, right, wt, before, bias, pair):
    _, rows, lanes = left[0].shape
    _, some, tile = right[0].shape
    chans = wt.shape[0]
    pack = tile // rows
    width = lanes // pack
    halves = pack // 2
    depth = -(-side * side * seqs // LANES) * LANES
    group = 8
    first, last = part == 0, part == PARTS - 1
    whole = lambda shape: pl.BlockSpec(shape, lambda g: (0,) * len(shape))
    sum_spec = pl.BlockSpec((group, halves, chans, 2 * tile), lambda g: (g, 0, 0, 0))
    pair_spec = pl.BlockSpec((pack, group, tile, chans), lambda g: (0, g, 0, 0))
    operands = list(left) + list(right) + [wt]
    specs = [whole(x.shape) for x in operands[:-1]]
    specs.append(pl.BlockSpec((chans, some * width), lambda g: (0, part)))
    if not first:
        operands.append(before)
        specs.append(sum_spec)
    if last:
        operands += [in_hbm(bias[None]), in_hbm(pair.reshape(pack, rows, tile, chans))]
        specs += [whole((1, chans)), pair_spec]
        out_shape, out_spec = jax.ShapeDtypeStruct((pack, rows, tile, chans), jnp.bfloat16), pair_spec
    else:
        out_shape = jax.ShapeDtypeStruct((rows, halves, chans, 2 * tile), jnp.float32)
        out_spec = sum_spec
    return pl.pallas_call(
        functools.partial(update_kernel, side, seqs, order, len(left), first, last),
        grid=(rows // group,),
        in_specs=specs,
        out_specs=out_spec,
        out_shape=out_shape,
        scratch_shapes=[
            pltpu.VMEM((depth * rows, lanes), jnp.float32),
            pltpu.VMEM((depth * some, tile), jnp.float32),
            pltpu.VMEM((depth, some * tile), jnp.bfloat16),
            pltpu.VMEM((group * halves, some * width, 2 * tile), jnp.bfloat16),
        ],
        compiler_params=pltpu.CompilerParams(vmem_limit_bytes=48 * MIB),
        cost_estimate=pl.CostEstimate(
            flops=2 * tile * tile * some * width * (side * side * seqs + chans),
            bytes_accessed=16 * MIB,
            transcendentals=0,
        ),
        name="update_%d" % part,
    )(*operands)


def local(
    alignment_features,
    pairwise_features,
    standardize_scaling,
    standardize_additive,
    first_factor_matrix,
    first_factor_intercept,
    second_factor_matrix,
    second_factor_intercept,
    final_matrix,
    final_intercept,
):
    devices = lax.axis_size("row")
    side = math.isqrt(devices)
    seqs, residues, _ = alignment_features.shape
    tile = residues // side
    width = first_factor_matrix.shape[1]
    left, right = project(
        side,
        alignment_features,
        standardize_scaling,
        standardize_additive,
        first_factor_matrix,
        first_factor_intercept,
        second_factor_matrix,
        second_factor_intercept,
    )

    def swap(x, da, db):
        return lax.ppermute(x, "row", [(i, i ^ (da * side + db)) for i in range(devices)])

    left = [left[0]] + [swap(left[d], d, 0) for d in range(1, side)]
    right = [right[0]] + [swap(right[d], 0, d) for d in range(1, side)]
    left = jnp.concatenate(left)
    mines = [jnp.concatenate([x[part] for x in right]) for part in range(PARTS)]
    left, *mines = lax.optimization_barrier((left, *mines))
    lefts = [left] + [swap(left, 0, d) for d in range(1, side)]
    parts = [[mine] + [swap(mine, d, 0) for d in range(1, side)] for mine in mines]
    order = list(range(side))
    wt = final_matrix.reshape(width, width, -1).transpose(2, 1, 0).reshape(-1, width * width)
    total = None
    for part in range(PARTS):
        total = update_part(
            side, seqs, order, part, lefts, parts[part], wt, total, final_intercept, pairwise_features
        )
    return total.reshape(1, tile, tile, -1)


def solution(mesh):
    placed = (
        P(("grp", "row"), None, None),
        P(("grp", "row"), None, None, None),
        P(),
        P(),
        P(),
        P(),
        P(),
        P(),
        P(),
        P(),
    )
    return jax.shard_map(
        local,
        mesh=mesh,
        in_specs=placed,
        out_specs=P(("grp", "row"), None, None, None),
        check_vma=False,
    )
```

```python
import functools
import math

import jax
import jax.numpy as jnp
from jax import lax
from jax.experimental import pallas as pl
from jax.experimental.pallas import tpu as pltpu
from jax.sharding import PartitionSpec as P

LANES = 128
PARTS = 2
MIB = 1024 * 1024


def in_hbm(x):
    return pltpu.with_memory_space_constraint(x, pltpu.HBM)


def project_kernel(side, *refs):
    sources, refs = refs[:7], refs[7:]
    left_out, right_out, refs = refs[:side], refs[side : 2 * side], refs[2 * side :]
    buffers, normed_ref, sems, x_sems = refs[:7], refs[7], refs[8], refs[9]
    x_ref, gain_ref, offset_ref, wl_ref, bl_ref, wr_ref, br_ref = buffers
    seqs, residues, chans = x_ref.shape
    width = wl_ref.shape[0]
    tile = residues // side
    pack = LANES // width
    rows = tile // pack
    x_copies = [
        pltpu.make_async_copy(sources[0].at[s], x_ref.at[s], x_sems.at[s]) for s in range(seqs)
    ]
    copies = [
        pltpu.make_async_copy(sources[k], buffers[k], sems.at[k]) for k in range(1, len(buffers))
    ]
    for copy in x_copies[:1] + copies + x_copies[1:]:
        copy.start()
    for copy in copies:
        copy.wait()
    me = lax.axis_index("row")
    place_a, place_b = me // side, lax.rem(me, side)
    nt = (((1,), (1,)), ((), ()))
    wl = wl_ref[...]
    placed = [
        jnp.concatenate([wl if k == h else jnp.zeros_like(wl) for k in range(pack)], axis=0)
        for h in range(pack)
    ]
    left_bias = jnp.concatenate([bl_ref[...]] * pack, axis=1)
    right_bias = jnp.broadcast_to(br_ref[...], (tile, width)).T
    for s in range(seqs):
        x_copies[s].wait()
        normed = normed_ref.at[s % 2]
        x = x_ref[s].astype(jnp.float32)
        center = x - jnp.mean(x, axis=-1, keepdims=True)
        variance = jnp.mean(center * center, axis=-1, keepdims=True)
        normed[...] = (
            center * lax.rsqrt(variance + 1e-05) * gain_ref[...] + offset_ref[...]
        ).astype(jnp.bfloat16)
        blocks = []
        for d in range(side):
            b = place_b ^ d
            block = normed[pl.ds(pl.multiple_of(b * tile, tile), tile), :]
            right = lax.dot_general(wr_ref[...], block, nt, preferred_element_type=jnp.float32)
            right_out[d][:, s] = (
                (right + right_bias).astype(jnp.bfloat16).reshape(PARTS, width // PARTS, tile)
            )
            a = place_a ^ d
            blocks.append(normed[pl.ds(pl.multiple_of(a * tile, tile), tile), :])
        total = left_bias
        for h in range(pack):
            picked = jnp.concatenate([block[h * rows : (h + 1) * rows] for block in blocks], axis=0)
            total = total + lax.dot_general(
                picked, placed[h], nt, preferred_element_type=jnp.float32
            )
        left = total.astype(jnp.bfloat16)
        for d in range(side):
            left_out[d][s] = left[d * rows : (d + 1) * rows]


def project(side, x, gain, offset, wl, bl, wr, br):
    seqs, residues, chans = x.shape
    width = wl.shape[1]
    tile = residues // side
    rows = tile * width // LANES
    operands = [in_hbm(o) for o in (x, gain[None], offset[None], wl.T, bl[None], wr.T, br[None])]
    out = pl.pallas_call(
        functools.partial(project_kernel, side),
        in_specs=[pl.BlockSpec(memory_space=pltpu.HBM)] * len(operands),
        out_specs=[pl.BlockSpec(memory_space=pltpu.VMEM)] * (2 * side),
        out_shape=[jax.ShapeDtypeStruct((seqs, rows, LANES), jnp.bfloat16)] * side
        + [jax.ShapeDtypeStruct((PARTS, seqs, width // PARTS, tile), jnp.bfloat16)] * side,
        scratch_shapes=[pltpu.VMEM(o.shape, o.dtype) for o in operands]
        + [
            pltpu.VMEM((2, residues, chans), jnp.bfloat16),
            pltpu.SemaphoreType.DMA((len(operands),)),
            pltpu.SemaphoreType.DMA((seqs,)),
        ],
        compiler_params=pltpu.CompilerParams(vmem_limit_bytes=32 * MIB),
        name="project",
    )(*operands)
    return out[:side], out[side:]


def arrange_kernel(seq_total, *refs):
    left_refs, out_ref, wide = refs[:-2], refs[-2], refs[-1]
    _, rows, lanes = left_refs[0].shape
    depth = out_ref.shape[2]
    at = 0
    for ref in left_refs:
        count = ref.shape[0] * rows
        wide[at : at + count] = ref[...].astype(jnp.float32).reshape(count, lanes)
        at += count
    if depth > seq_total:
        wide[seq_total * rows :] = jnp.zeros(((depth - seq_total) * rows, lanes), jnp.float32)
    for r in range(rows):
        out_ref[r] = wide[pl.ds(r, depth, stride=rows), :].T.astype(jnp.bfloat16)


def arrange_left(lefts, tile):
    _, rows, lanes = lefts[0].shape
    seq_total = sum(x.shape[0] for x in lefts)
    depth = -(-seq_total // LANES) * LANES
    return pl.pallas_call(
        functools.partial(arrange_kernel, seq_total),
        in_specs=[pl.BlockSpec(memory_space=pltpu.VMEM)] * len(lefts),
        out_specs=pl.BlockSpec(memory_space=pltpu.VMEM),
        out_shape=jax.ShapeDtypeStruct((rows, lanes, depth), jnp.bfloat16),
        scratch_shapes=[pltpu.VMEM((depth * rows, lanes), jnp.float32)],
        compiler_params=pltpu.CompilerParams(vmem_limit_bytes=32 * MIB),
        cost_estimate=pl.CostEstimate(flops=MIB, bytes_accessed=8 * MIB, transcendentals=0),
        name="arrange_left",
    )(*lefts)


def update_kernel(side, seqs, order, rights, first, last, left_ref, *refs):
    right_refs, refs = refs[:rights], refs[rights:]
    wt_ref, refs = refs[0], refs[1:]
    if not first:
        before_ref, refs = refs[0], refs[1:]
    if last:
        bias_ref, pair_ref, refs = refs[0], refs[1], refs[2:]
    out_ref, right_wide, right_flat, outer = refs
    group, lanes, depth = left_ref.shape
    some, tile = right_refs[0].shape[-2:]
    halves = outer.shape[0] // group
    pack = 2 * halves
    width = lanes // pack
    seq_total = side * side * seqs

    @pl.when(pl.program_id(0) == 0)
    def _():
        place_a = lax.axis_index("row") // side
        for dz in range(side):
            source = right_refs[dz] if rights > 1 else right_refs[0].at[place_a ^ dz]
            for k, dy in enumerate(order):
                to = (k * side + dz) * seqs
                right_wide[to * some : (to + seqs) * some] = (
                    source[dy * seqs : (dy + 1) * seqs]
                    .astype(jnp.float32)
                    .reshape(seqs * some, tile)
                )
        if depth > seq_total:
            right_wide[seq_total * some :] = jnp.zeros(
                ((depth - seq_total) * some, tile), jnp.float32
            )
        for e in range(some):
            right_flat[:, e * tile : (e + 1) * tile] = right_wide[
                pl.ds(e, depth, stride=some), :
            ].astype(jnp.bfloat16)

    for q in range(group):
        for n in range(some // 2):
            both = jnp.dot(
                left_ref[q],
                right_flat[:, 2 * n * tile : (2 * n + 2) * tile],
                preferred_element_type=jnp.float32,
            ).astype(jnp.bfloat16)
            for k in range(2):
                e = 2 * n + k
                for h in range(pack):
                    outer[
                        q * halves + h // 2,
                        e * width : (e + 1) * width,
                        (h % 2) * tile : (h % 2 + 1) * tile,
                    ] = both[h * width : (h + 1) * width, k * tile : (k + 1) * tile]
    for q in range(group):
        for g in range(halves):
            update = jnp.dot(wt_ref[...], outer[q * halves + g], preferred_element_type=jnp.float32)
            if not first:
                update = update + before_ref[q, g]
            if not last:
                out_ref[q, g] = update
                continue
            for k in range(2):
                h = 2 * g + k
                share = update[:, k * tile : (k + 1) * tile].T * (1.0 / seq_total) + bias_ref[...]
                out_ref[h, q] = (pair_ref[h, q].astype(jnp.float32) + share).astype(jnp.bfloat16)


def update_part(side, seqs, order, part, left, right, wt, before, bias, pair):
    rows, lanes, depth = left.shape
    some, tile = right[0].shape[-2:]
    chans = wt.shape[0]
    pack = tile // rows
    width = lanes // pack
    halves = pack // 2
    group = 8
    first, last = part == 0, part == PARTS - 1
    whole = lambda shape: pl.BlockSpec(shape, lambda g: (0,) * len(shape))
    sum_spec = pl.BlockSpec((group, halves, chans, 2 * tile), lambda g: (g, 0, 0, 0))
    pair_spec = pl.BlockSpec((pack, group, tile, chans), lambda g: (0, g, 0, 0))
    operands = [left] + list(right) + [wt]
    specs = [pl.BlockSpec((group, lanes, depth), lambda g: (g, 0, 0))]
    specs += [whole(x.shape) for x in right]
    specs.append(pl.BlockSpec((chans, some * width), lambda g: (0, part)))
    if not first:
        operands.append(before)
        specs.append(sum_spec)
    if last:
        operands += [in_hbm(bias[None]), in_hbm(pair.reshape(pack, rows, tile, chans))]
        specs += [whole((1, chans)), pair_spec]
        out_shape, out_spec = jax.ShapeDtypeStruct((pack, rows, tile, chans), jnp.bfloat16), pair_spec
    else:
        out_shape = jax.ShapeDtypeStruct((rows, halves, chans, 2 * tile), jnp.float32)
        out_spec = sum_spec
    return pl.pallas_call(
        functools.partial(update_kernel, side, seqs, order, len(right), first, last),
        grid=(rows // group,),
        in_specs=specs,
        out_specs=out_spec,
        out_shape=out_shape,
        scratch_shapes=[
            pltpu.VMEM((depth * some, tile), jnp.float32),
            pltpu.VMEM((depth, some * tile), jnp.bfloat16),
            pltpu.VMEM((group * halves, some * width, 2 * tile), jnp.bfloat16),
        ],
        compiler_params=pltpu.CompilerParams(vmem_limit_bytes=48 * MIB),
        cost_estimate=pl.CostEstimate(
            flops=2 * tile * tile * some * width * (side * side * seqs + chans),
            bytes_accessed=16 * MIB,
            transcendentals=0,
        ),
        name="update_%d" % part,
    )(*operands)


def local(
    alignment_features,
    pairwise_features,
    standardize_scaling,
    standardize_additive,
    first_factor_matrix,
    first_factor_intercept,
    second_factor_matrix,
    second_factor_intercept,
    final_matrix,
    final_intercept,
):
    devices = lax.axis_size("row")
    side = math.isqrt(devices)
    seqs, residues, _ = alignment_features.shape
    tile = residues // side
    width = first_factor_matrix.shape[1]
    left, right = project(
        side,
        alignment_features,
        standardize_scaling,
        standardize_additive,
        first_factor_matrix,
        first_factor_intercept,
        second_factor_matrix,
        second_factor_intercept,
    )

    def swap(x, da, db):
        return lax.ppermute(x, "row", [(i, i ^ (da * side + db)) for i in range(devices)])

    left = [left[0]] + [swap(left[d], d, 0) for d in range(1, side)]
    right = [right[0]] + [swap(right[d], 0, d) for d in range(1, side)]
    left = jnp.concatenate(left)
    mines = [jnp.concatenate([x[part] for x in right]) for part in range(PARTS)]
    left, *mines = lax.optimization_barrier((left, *mines))
    parts = [[mines[0]] + [swap(mines[0], d, 0) for d in range(1, side)]]
    order = [0]
    lefts = [left]
    step = side // 2
    while step > 0:
        left = jnp.concatenate(lefts) if len(lefts) > 1 else lefts[0]
        lefts = [left, swap(left, 0, step)]
        order += [o ^ step for o in order]
        step //= 2
    columns = [[a * side + b for a in range(side)] for b in range(side)]
    for mine in mines[1:]:
        parts[0][1], mine = lax.optimization_barrier((parts[0][1], mine))
        slots = jnp.broadcast_to(mine[None], (side,) + mine.shape)
        parts.append([lax.all_to_all(slots, "row", 0, 0, axis_index_groups=columns, tiled=True)])
    left = arrange_left(lefts, tile)
    wt = final_matrix.reshape(width, width, -1).transpose(2, 1, 0).reshape(-1, width * width)
    total = None
    for part in range(PARTS):
        total = update_part(
            side, seqs, order, part, left, parts[part], wt, total, final_intercept, pairwise_features
        )
    return total.reshape(1, tile, tile, -1)


def solution(mesh):
    placed = (
        P(("grp", "row"), None, None),
        P(("grp", "row"), None, None, None),
        P(),
        P(),
        P(),
        P(),
        P(),
        P(),
        P(),
        P(),
    )
    return jax.shard_map(
        local,
        mesh=mesh,
        in_specs=placed,
        out_specs=P(("grp", "row"), None, None, None),
        check_vma=False,
    )
```

```python
import functools
import math

import jax
import jax.numpy as jnp
from jax import lax
from jax.experimental import pallas as pl
from jax.experimental.pallas import tpu as pltpu
from jax.sharding import PartitionSpec as P

LANES = 128
PARTS = 2
MIB = 1024 * 1024


def in_hbm(x):
    return pltpu.with_memory_space_constraint(x, pltpu.HBM)


def project_kernel(side, *refs):
    sources, refs = refs[:7], refs[7:]
    left_out, right_out, refs = refs[:side], refs[side : 2 * side], refs[2 * side :]
    buffers, normed_ref, sems, x_sems = refs[:7], refs[7], refs[8], refs[9]
    x_ref, gain_ref, offset_ref, wl_ref, bl_ref, wr_ref, br_ref = buffers
    seqs, residues, chans = x_ref.shape
    width = wl_ref.shape[0]
    tile = residues // side
    pack = LANES // width
    rows = tile // pack
    x_copies = [
        pltpu.make_async_copy(sources[0].at[s], x_ref.at[s], x_sems.at[s]) for s in range(seqs)
    ]
    copies = [
        pltpu.make_async_copy(sources[k], buffers[k], sems.at[k]) for k in range(1, len(buffers))
    ]
    for copy in x_copies[:1] + copies + x_copies[1:]:
        copy.start()
    for copy in copies:
        copy.wait()
    me = lax.axis_index("row")
    place_a, place_b = me // side, lax.rem(me, side)
    nt = (((1,), (1,)), ((), ()))
    wl = wl_ref[...]
    placed = [
        jnp.concatenate([wl if k == h else jnp.zeros_like(wl) for k in range(pack)], axis=0)
        for h in range(pack)
    ]
    left_bias = jnp.concatenate([bl_ref[...]] * pack, axis=1)
    right_bias = jnp.broadcast_to(br_ref[...], (tile, width)).T
    for s in range(seqs):
        x_copies[s].wait()
        normed = normed_ref.at[s % 2]
        x = x_ref[s].astype(jnp.float32)
        center = x - jnp.mean(x, axis=-1, keepdims=True)
        variance = jnp.mean(center * center, axis=-1, keepdims=True)
        normed[...] = (
            center * lax.rsqrt(variance + 1e-05) * gain_ref[...] + offset_ref[...]
        ).astype(jnp.bfloat16)
        blocks = []
        for d in range(side):
            b = place_b ^ d
            block = normed[pl.ds(pl.multiple_of(b * tile, tile), tile), :]
            right = lax.dot_general(wr_ref[...], block, nt, preferred_element_type=jnp.float32)
            right_out[d][:, s] = (
                (right + right_bias).astype(jnp.bfloat16).reshape(PARTS, width // PARTS, tile)
            )
            a = place_a ^ d
            blocks.append(normed[pl.ds(pl.multiple_of(a * tile, tile), tile), :])
        total = left_bias
        for h in range(pack):
            picked = jnp.concatenate([block[h * rows : (h + 1) * rows] for block in blocks], axis=0)
            total = total + lax.dot_general(
                picked, placed[h], nt, preferred_element_type=jnp.float32
            )
        left = total.astype(jnp.bfloat16)
        for d in range(side):
            left_out[d][s] = left[d * rows : (d + 1) * rows]


def project(side, x, gain, offset, wl, bl, wr, br):
    seqs, residues, chans = x.shape
    width = wl.shape[1]
    tile = residues // side
    rows = tile * width // LANES
    operands = [in_hbm(o) for o in (x, gain[None], offset[None], wl.T, bl[None], wr.T, br[None])]
    out = pl.pallas_call(
        functools.partial(project_kernel, side),
        in_specs=[pl.BlockSpec(memory_space=pltpu.HBM)] * len(operands),
        out_specs=[pl.BlockSpec(memory_space=pltpu.VMEM)] * (2 * side),
        out_shape=[jax.ShapeDtypeStruct((seqs, rows, LANES), jnp.bfloat16)] * side
        + [jax.ShapeDtypeStruct((PARTS, seqs, width // PARTS, tile), jnp.bfloat16)] * side,
        scratch_shapes=[pltpu.VMEM(o.shape, o.dtype) for o in operands]
        + [
            pltpu.VMEM((2, residues, chans), jnp.bfloat16),
            pltpu.SemaphoreType.DMA((len(operands),)),
            pltpu.SemaphoreType.DMA((seqs,)),
        ],
        compiler_params=pltpu.CompilerParams(vmem_limit_bytes=32 * MIB),
        name="project",
    )(*operands)
    return out[:side], out[side:]


def arrange_kernel(seq_total, *refs):
    left_refs, out_ref, wide = refs[:-2], refs[-2], refs[-1]
    _, rows, lanes = left_refs[0].shape
    depth = out_ref.shape[2]
    at = 0
    for ref in left_refs:
        count = ref.shape[0] * rows
        wide[at : at + count] = ref[...].astype(jnp.float32).reshape(count, lanes)
        at += count
    if depth > seq_total:
        wide[seq_total * rows :] = jnp.zeros(((depth - seq_total) * rows, lanes), jnp.float32)
    for r in range(rows):
        out_ref[r] = wide[pl.ds(r, depth, stride=rows), :].T.astype(jnp.bfloat16)


def arrange_left(lefts, tile):
    _, rows, lanes = lefts[0].shape
    seq_total = sum(x.shape[0] for x in lefts)
    depth = -(-seq_total // LANES) * LANES
    return pl.pallas_call(
        functools.partial(arrange_kernel, seq_total),
        in_specs=[pl.BlockSpec(memory_space=pltpu.VMEM)] * len(lefts),
        out_specs=pl.BlockSpec(memory_space=pltpu.VMEM),
        out_shape=jax.ShapeDtypeStruct((rows, lanes, depth), jnp.bfloat16),
        scratch_shapes=[pltpu.VMEM((depth * rows, lanes), jnp.float32)],
        compiler_params=pltpu.CompilerParams(vmem_limit_bytes=32 * MIB),
        cost_estimate=pl.CostEstimate(flops=MIB, bytes_accessed=8 * MIB, transcendentals=0),
        name="arrange_left",
    )(*lefts)


def update_kernel(side, seqs, group, first, last, left_ref, *refs):
    right_refs, refs = refs[:side], refs[side:]
    wt_ref, refs = refs[0], refs[1:]
    if not first:
        before_ref, refs = refs[0], refs[1:]
    if last:
        bias_ref, pair_ref, refs = refs[0], refs[1], refs[2:]
    out_ref, right_wide, right_flat, outer = refs
    rows, lanes, depth = left_ref.shape
    _, some, tile = right_refs[0].shape
    halves = outer.shape[0] // group
    pack = 2 * halves
    width = lanes // pack
    seq_total = side * side * seqs
    at = pl.program_id(0) * group

    @pl.when(pl.program_id(0) == 0)
    def _():
        for dz in range(side):
            for dy in range(side):
                to = (dy * side + dz) * seqs
                right_wide[to * some : (to + seqs) * some] = (
                    right_refs[dz][dy * seqs : (dy + 1) * seqs]
                    .astype(jnp.float32)
                    .reshape(seqs * some, tile)
                )
        if depth > seq_total:
            right_wide[seq_total * some :] = jnp.zeros(
                ((depth - seq_total) * some, tile), jnp.float32
            )
        for e in range(some):
            right_flat[:, e * tile : (e + 1) * tile] = right_wide[
                pl.ds(e, depth, stride=some), :
            ].astype(jnp.bfloat16)

    def outer_products(q):
        for n in range(some // 2):
            both = jnp.dot(
                left_ref[at + q],
                right_flat[:, 2 * n * tile : (2 * n + 2) * tile],
                preferred_element_type=jnp.float32,
            ).astype(jnp.bfloat16)
            for k in range(2):
                e = 2 * n + k
                for h in range(pack):
                    outer[
                        q * halves + h // 2,
                        e * width : (e + 1) * width,
                        (h % 2) * tile : (h % 2 + 1) * tile,
                    ] = both[h * width : (h + 1) * width, k * tile : (k + 1) * tile]

    def project_back(q):
        for g in range(halves):
            update = jnp.dot(wt_ref[...], outer[q * halves + g], preferred_element_type=jnp.float32)
            if not first:
                update = update + before_ref[at + q, g]
            if not last:
                out_ref[at + q, g] = update
                continue
            for k in range(2):
                h = 2 * g + k
                share = update[:, k * tile : (k + 1) * tile].T * (1.0 / seq_total) + bias_ref[...]
                old = pair_ref[h, at + q].astype(jnp.float32)
                out_ref[h, q] = (old + share).astype(jnp.bfloat16)

    for q in range(group + 1):
        if q < group:
            outer_products(q)
        if q > 0:
            project_back(q - 1)


def update_part(side, seqs, part, left, right, wt, before, bias, pair):
    rows, lanes, depth = left.shape
    some, tile = right[0].shape[-2:]
    chans = wt.shape[0]
    pack = tile // rows
    width = lanes // pack
    halves = pack // 2
    group = 8
    first, last = part == 0, part == PARTS - 1
    in_vmem = pl.BlockSpec(memory_space=pltpu.VMEM)
    operands = [left] + list(right) + [wt[:, part * some * width : (part + 1) * some * width]]
    if not first:
        operands.append(before)
    if last:
        operands += [bias[None], pair.reshape(pack, rows, tile, chans)]
        out_shape = jax.ShapeDtypeStruct((pack, rows, tile, chans), jnp.bfloat16)
        out_spec = pl.BlockSpec((pack, group, tile, chans), lambda g: (0, g, 0, 0))
    else:
        out_shape, out_spec = pltpu.VMEM((rows, halves, chans, 2 * tile), jnp.float32), in_vmem
    return pl.pallas_call(
        functools.partial(update_kernel, side, seqs, group, first, last),
        grid=(rows // group,),
        in_specs=[in_vmem] * len(operands),
        out_specs=out_spec,
        out_shape=out_shape,
        scratch_shapes=[
            pltpu.VMEM((depth * some, tile), jnp.float32),
            pltpu.VMEM((depth, some * tile), jnp.bfloat16),
            pltpu.VMEM((group * halves, some * width, 2 * tile), jnp.bfloat16),
        ],
        compiler_params=pltpu.CompilerParams(vmem_limit_bytes=24 * MIB),
        cost_estimate=pl.CostEstimate(
            flops=2 * tile * tile * some * width * (side * side * seqs + chans),
            bytes_accessed=16 * MIB,
            transcendentals=0,
        ),
        name="update_%d" % part,
    )(*operands)


def local(
    alignment_features,
    pairwise_features,
    standardize_scaling,
    standardize_additive,
    first_factor_matrix,
    first_factor_intercept,
    second_factor_matrix,
    second_factor_intercept,
    final_matrix,
    final_intercept,
):
    devices = lax.axis_size("row")
    side = math.isqrt(devices)
    seqs, residues, _ = alignment_features.shape
    tile = residues // side
    width = first_factor_matrix.shape[1]
    left, right = project(
        side,
        alignment_features,
        standardize_scaling,
        standardize_additive,
        first_factor_matrix,
        first_factor_intercept,
        second_factor_matrix,
        second_factor_intercept,
    )

    def swap(x, da, db):
        return lax.ppermute(x, "row", [(i, i ^ (da * side + db)) for i in range(devices)])

    left = [left[0]] + [swap(left[d], d, 0) for d in range(1, side)]
    right = [right[0]] + [swap(right[d], 0, d) for d in range(1, side)]
    left = jnp.concatenate(left)
    mines = [jnp.concatenate([x[part] for x in right]) for part in range(PARTS)]
    left, *mines = lax.optimization_barrier((left, *mines))
    lefts = [left] + [swap(left, 0, d) for d in range(1, side)]
    parts = [[mine] + [swap(mine, d, 0) for d in range(1, side)] for mine in mines]
    left = arrange_left(lefts, tile)
    wt = final_matrix.reshape(width, width, -1).transpose(2, 1, 0).reshape(-1, width * width)
    total = None
    for part in range(PARTS):
        total = update_part(
            side, seqs, part, left, parts[part], wt, total, final_intercept, pairwise_features
        )
    return total.reshape(1, tile, tile, -1)


def solution(mesh):
    placed = (
        P(("grp", "row"), None, None),
        P(("grp", "row"), None, None, None),
        P(),
        P(),
        P(),
        P(),
        P(),
        P(),
        P(),
        P(),
    )
    return jax.shard_map(
        local,
        mesh=mesh,
        in_specs=placed,
        out_specs=P(("grp", "row"), None, None, None),
        check_vma=False,
    )
```

```python
import functools
import math

import jax
import jax.numpy as jnp
from jax import lax
from jax.experimental import pallas as pl
from jax.experimental.pallas import tpu as pltpu
from jax.sharding import PartitionSpec as P

LANES = 128
PARTS = 2
MIB = 1024 * 1024


def in_hbm(x):
    return pltpu.with_memory_space_constraint(x, pltpu.HBM)


def project_kernel(side, *refs):
    sources, refs = refs[:7], refs[7:]
    left_out, right_out, refs = refs[:side], refs[side : 2 * side], refs[2 * side :]
    buffers, normed_ref, sems, x_sems = refs[:7], refs[7], refs[8], refs[9]
    x_ref, gain_ref, offset_ref, wl_ref, bl_ref, wr_ref, br_ref = buffers
    seqs, residues, chans = x_ref.shape
    width = wl_ref.shape[0]
    tile = residues // side
    pack = LANES // width
    rows = tile // pack
    x_copies = [
        pltpu.make_async_copy(sources[0].at[s], x_ref.at[s], x_sems.at[s]) for s in range(seqs)
    ]
    copies = [
        pltpu.make_async_copy(sources[k], buffers[k], sems.at[k]) for k in range(1, len(buffers))
    ]
    for copy in x_copies[:1] + copies + x_copies[1:]:
        copy.start()
    for copy in copies:
        copy.wait()
    me = lax.axis_index("row")
    place_a, place_b = me // side, lax.rem(me, side)
    nt = (((1,), (1,)), ((), ()))
    wl = wl_ref[...]
    placed = [
        jnp.concatenate([wl if k == h else jnp.zeros_like(wl) for k in range(pack)], axis=0)
        for h in range(pack)
    ]
    left_bias = jnp.concatenate([bl_ref[...]] * pack, axis=1)
    right_bias = jnp.broadcast_to(br_ref[...], (tile, width)).T
    for s in range(seqs):
        x_copies[s].wait()
        normed = normed_ref.at[s % 2]
        x = x_ref[s].astype(jnp.float32)
        center = x - jnp.mean(x, axis=-1, keepdims=True)
        variance = jnp.mean(center * center, axis=-1, keepdims=True)
        normed[...] = (
            center * lax.rsqrt(variance + 1e-05) * gain_ref[...] + offset_ref[...]
        ).astype(jnp.bfloat16)
        blocks = []
        for d in range(side):
            b = place_b ^ d
            block = normed[pl.ds(pl.multiple_of(b * tile, tile), tile), :]
            right = lax.dot_general(wr_ref[...], block, nt, preferred_element_type=jnp.float32)
            right_out[d][:, s] = (
                (right + right_bias).astype(jnp.bfloat16).reshape(PARTS, width // PARTS, tile)
            )
            a = place_a ^ d
            blocks.append(normed[pl.ds(pl.multiple_of(a * tile, tile), tile), :])
        total = left_bias
        for h in range(pack):
            picked = jnp.concatenate([block[h * rows : (h + 1) * rows] for block in blocks], axis=0)
            total = total + lax.dot_general(
                picked, placed[h], nt, preferred_element_type=jnp.float32
            )
        left = total.astype(jnp.bfloat16)
        for d in range(side):
            left_out[d][s] = left[d * rows : (d + 1) * rows]


def project(side, x, gain, offset, wl, bl, wr, br):
    seqs, residues, chans = x.shape
    width = wl.shape[1]
    tile = residues // side
    rows = tile * width // LANES
    operands = [in_hbm(o) for o in (x, gain[None], offset[None], wl.T, bl[None], wr.T, br[None])]
    out = pl.pallas_call(
        functools.partial(project_kernel, side),
        in_specs=[pl.BlockSpec(memory_space=pltpu.HBM)] * len(operands),
        out_specs=[pl.BlockSpec(memory_space=pltpu.VMEM)] * (2 * side),
        out_shape=[jax.ShapeDtypeStruct((seqs, rows, LANES), jnp.bfloat16)] * side
        + [jax.ShapeDtypeStruct((PARTS, seqs, width // PARTS, tile), jnp.bfloat16)] * side,
        scratch_shapes=[pltpu.VMEM(o.shape, o.dtype) for o in operands]
        + [
            pltpu.VMEM((2, residues, chans), jnp.bfloat16),
            pltpu.SemaphoreType.DMA((len(operands),)),
            pltpu.SemaphoreType.DMA((seqs,)),
        ],
        compiler_params=pltpu.CompilerParams(vmem_limit_bytes=32 * MIB),
        name="project",
    )(*operands)
    return out[:side], out[side:]


def arrange_kernel(seq_total, *refs):
    left_refs, out_ref, wide = refs[:-2], refs[-2], refs[-1]
    _, rows, lanes = left_refs[0].shape
    depth = out_ref.shape[2]
    at = 0
    for ref in left_refs:
        count = ref.shape[0] * rows
        wide[at : at + count] = ref[...].astype(jnp.float32).reshape(count, lanes)
        at += count
    if depth > seq_total:
        wide[seq_total * rows :] = jnp.zeros(((depth - seq_total) * rows, lanes), jnp.float32)
    for r in range(rows):
        out_ref[r] = wide[pl.ds(r, depth, stride=rows), :].T.astype(jnp.bfloat16)


def arrange_left(lefts, tile):
    _, rows, lanes = lefts[0].shape
    seq_total = sum(x.shape[0] for x in lefts)
    depth = -(-seq_total // LANES) * LANES
    return pl.pallas_call(
        functools.partial(arrange_kernel, seq_total),
        in_specs=[pl.BlockSpec(memory_space=pltpu.VMEM)] * len(lefts),
        out_specs=pl.BlockSpec(memory_space=pltpu.VMEM),
        out_shape=jax.ShapeDtypeStruct((rows, lanes, depth), jnp.bfloat16),
        scratch_shapes=[pltpu.VMEM((depth * rows, lanes), jnp.float32)],
        compiler_params=pltpu.CompilerParams(vmem_limit_bytes=32 * MIB),
        cost_estimate=pl.CostEstimate(flops=MIB, bytes_accessed=8 * MIB, transcendentals=0),
        name="arrange_left",
    )(*lefts)


def update_kernel(side, seqs, group, first, last, left_ref, *refs):
    right_refs, refs = refs[:side], refs[side:]
    wt_ref, refs = refs[0], refs[1:]
    if not first:
        before_ref, refs = refs[0], refs[1:]
    if last:
        bias_ref, pair_ref, refs = refs[0], refs[1], refs[2:]
    out_ref, right_wide, right_flat, outer = refs
    rows, lanes, depth = left_ref.shape
    _, some, tile = right_refs[0].shape
    halves = outer.shape[0] // group
    pack = 2 * halves
    width = lanes // pack
    seq_total = side * side * seqs
    at = pl.program_id(0) * group

    @pl.when(pl.program_id(0) == 0)
    def _():
        for dz in range(side):
            for dy in range(side):
                to = (dy * side + dz) * seqs
                right_wide[to * some : (to + seqs) * some] = (
                    right_refs[dz][dy * seqs : (dy + 1) * seqs]
                    .astype(jnp.float32)
                    .reshape(seqs * some, tile)
                )
        if depth > seq_total:
            right_wide[seq_total * some :] = jnp.zeros(
                ((depth - seq_total) * some, tile), jnp.float32
            )
        for e in range(some):
            right_flat[:, e * tile : (e + 1) * tile] = right_wide[
                pl.ds(e, depth, stride=some), :
            ].astype(jnp.bfloat16)

    def outer_products(q):
        for n in range(some // 2):
            both = jnp.dot(
                left_ref[at + q],
                right_flat[:, 2 * n * tile : (2 * n + 2) * tile],
                preferred_element_type=jnp.float32,
            ).astype(jnp.bfloat16)
            for k in range(2):
                e = 2 * n + k
                for h in range(pack):
                    outer[
                        q * halves + h // 2,
                        e * width : (e + 1) * width,
                        (h % 2) * tile : (h % 2 + 1) * tile,
                    ] = both[h * width : (h + 1) * width, k * tile : (k + 1) * tile]

    def project_back(q):
        for g in range(halves):
            update = jnp.dot(wt_ref[...], outer[q * halves + g], preferred_element_type=jnp.float32)
            if not first:
                update = update + before_ref[at + q, g]
            if not last:
                out_ref[at + q, g] = update
                continue
            for k in range(2):
                h = 2 * g + k
                share = update[:, k * tile : (k + 1) * tile].T * (1.0 / seq_total) + bias_ref[...]
                old = pair_ref[h, at + q].astype(jnp.float32)
                out_ref[h, q] = (old + share).astype(jnp.bfloat16)

    for q in range(group + 1):
        if q < group:
            outer_products(q)
        if q > 0:
            project_back(q - 1)


def update_part(side, seqs, part, left, right, wt, before, bias, pair):
    rows, lanes, depth = left.shape
    some, tile = right[0].shape[-2:]
    chans = wt.shape[0]
    pack = tile // rows
    width = lanes // pack
    halves = pack // 2
    group = 8
    first, last = part == 0, part == PARTS - 1
    in_vmem = pl.BlockSpec(memory_space=pltpu.VMEM)
    operands = [left] + list(right) + [wt[:, part * some * width : (part + 1) * some * width]]
    if not first:
        operands.append(before)
    if last:
        operands += [bias[None], pair.reshape(pack, rows, tile, chans)]
        out_shape = jax.ShapeDtypeStruct((pack, rows, tile, chans), jnp.bfloat16)
        out_spec = pl.BlockSpec((pack, group, tile, chans), lambda g: (0, g, 0, 0))
    else:
        out_shape, out_spec = pltpu.VMEM((rows, halves, chans, 2 * tile), jnp.float32), in_vmem
    return pl.pallas_call(
        functools.partial(update_kernel, side, seqs, group, first, last),
        grid=(rows // group,),
        in_specs=[in_vmem] * len(operands),
        out_specs=out_spec,
        out_shape=out_shape,
        scratch_shapes=[
            pltpu.VMEM((depth * some, tile), jnp.float32),
            pltpu.VMEM((depth, some * tile), jnp.bfloat16),
            pltpu.VMEM((group * halves, some * width, 2 * tile), jnp.bfloat16),
        ],
        compiler_params=pltpu.CompilerParams(vmem_limit_bytes=24 * MIB),
        cost_estimate=pl.CostEstimate(
            flops=2 * tile * tile * some * width * (side * side * seqs + chans),
            bytes_accessed=16 * MIB,
            transcendentals=0,
        ),
        name="update_%d" % part,
    )(*operands)


def local(
    alignment_features,
    pairwise_features,
    standardize_scaling,
    standardize_additive,
    first_factor_matrix,
    first_factor_intercept,
    second_factor_matrix,
    second_factor_intercept,
    final_matrix,
    final_intercept,
):
    devices = lax.axis_size("row")
    side = math.isqrt(devices)
    seqs, residues, _ = alignment_features.shape
    tile = residues // side
    width = first_factor_matrix.shape[1]
    left, right = project(
        side,
        alignment_features,
        standardize_scaling,
        standardize_additive,
        first_factor_matrix,
        first_factor_intercept,
        second_factor_matrix,
        second_factor_intercept,
    )

    def swap(x, da, db):
        return lax.ppermute(x, "row", [(i, i ^ (da * side + db)) for i in range(devices)])

    left = [left[0]] + [swap(left[d], d, 0) for d in range(1, side)]
    right = [right[0]] + [swap(right[d], 0, d) for d in range(1, side)]
    left = jnp.concatenate(left)
    mines = [jnp.concatenate([x[part] for x in right]) for part in range(PARTS)]
    left, *mines = lax.optimization_barrier((left, *mines))
    lefts = [left] + [swap(left, 0, d) for d in range(1, side)]
    near = swap(jnp.stack(mines), 1, 0)
    parts = [[mines[0], near[0]] + [swap(mines[0], d, 0) for d in range(2, side)]]
    for part in range(1, PARTS):
        pieces = [mines[part], near[part]]
        mask = 2
        while mask < side:
            got = swap(jnp.concatenate(pieces), mask, 0)
            count = mines[part].shape[0]
            pieces += [got[k * count : (k + 1) * count] for k in range(mask)]
            mask *= 2
        parts.append(pieces)
    left = arrange_left(lefts, tile)
    near, final_matrix = lax.optimization_barrier((near, final_matrix))
    wt = final_matrix.reshape(width, width, -1).transpose(2, 1, 0).reshape(-1, width * width)
    total = None
    for part in range(PARTS):
        total = update_part(
            side, seqs, part, left, parts[part], wt, total, final_intercept, pairwise_features
        )
    return total.reshape(1, tile, tile, -1)


def solution(mesh):
    placed = (
        P(("grp", "row"), None, None),
        P(("grp", "row"), None, None, None),
        P(),
        P(),
        P(),
        P(),
        P(),
        P(),
        P(),
        P(),
    )
    return jax.shard_map(
        local,
        mesh=mesh,
        in_specs=placed,
        out_specs=P(("grp", "row"), None, None, None),
        check_vma=False,
    )
```

```python
import functools
import math

import jax
import jax.numpy as jnp
from jax import lax
from jax.experimental import pallas as pl
from jax.experimental.pallas import tpu as pltpu
from jax.sharding import PartitionSpec as P

LANES = 128
PARTS = 2
MIB = 1024 * 1024


def in_hbm(x):
    return pltpu.with_memory_space_constraint(x, pltpu.HBM)


def project_kernel(side, *refs):
    sources, refs = refs[:7], refs[7:]
    left_out, right_out, refs = refs[:side], refs[side : 2 * side], refs[2 * side :]
    buffers, normed_ref, sems, x_sems = refs[:7], refs[7], refs[8], refs[9]
    x_ref, gain_ref, offset_ref, wl_ref, bl_ref, wr_ref, br_ref = buffers
    seqs, residues, chans = x_ref.shape
    width = wl_ref.shape[0]
    tile = residues // side
    pack = LANES // width
    rows = tile // pack
    x_copies = [
        pltpu.make_async_copy(sources[0].at[s], x_ref.at[s], x_sems.at[s]) for s in range(seqs)
    ]
    copies = [
        pltpu.make_async_copy(sources[k], buffers[k], sems.at[k]) for k in range(1, len(buffers))
    ]
    for copy in x_copies[:1] + copies + x_copies[1:]:
        copy.start()
    for copy in copies:
        copy.wait()
    me = lax.axis_index("row")
    place_a, place_b = me // side, lax.rem(me, side)
    nt = (((1,), (1,)), ((), ()))
    wl = wl_ref[...]
    placed = [
        jnp.concatenate([wl if k == h else jnp.zeros_like(wl) for k in range(pack)], axis=0)
        for h in range(pack)
    ]
    left_bias = jnp.concatenate([bl_ref[...]] * pack, axis=1)
    right_bias = jnp.broadcast_to(br_ref[...], (tile, width)).T
    for s in range(seqs):
        x_copies[s].wait()
        normed = normed_ref.at[s % 2]
        x = x_ref[s].astype(jnp.float32)
        center = x - jnp.mean(x, axis=-1, keepdims=True)
        variance = jnp.mean(center * center, axis=-1, keepdims=True)
        normed[...] = (
            center * lax.rsqrt(variance + 1e-05) * gain_ref[...] + offset_ref[...]
        ).astype(jnp.bfloat16)
        blocks = []
        for d in range(side):
            b = place_b ^ d
            block = normed[pl.ds(pl.multiple_of(b * tile, tile), tile), :]
            right = lax.dot_general(wr_ref[...], block, nt, preferred_element_type=jnp.float32)
            right_out[d][:, s] = (
                (right + right_bias).astype(jnp.bfloat16).reshape(PARTS, width // PARTS, tile)
            )
            a = place_a ^ d
            blocks.append(normed[pl.ds(pl.multiple_of(a * tile, tile), tile), :])
        total = left_bias
        for h in range(pack):
            picked = jnp.concatenate([block[h * rows : (h + 1) * rows] for block in blocks], axis=0)
            total = total + lax.dot_general(
                picked, placed[h], nt, preferred_element_type=jnp.float32
            )
        left = total.astype(jnp.bfloat16)
        for d in range(side):
            left_out[d][s] = left[d * rows : (d + 1) * rows]


def project(side, x, gain, offset, wl, bl, wr, br):
    seqs, residues, chans = x.shape
    width = wl.shape[1]
    tile = residues // side
    rows = tile * width // LANES
    operands = [in_hbm(o) for o in (x, gain[None], offset[None], wl.T, bl[None], wr.T, br[None])]
    out = pl.pallas_call(
        functools.partial(project_kernel, side),
        in_specs=[pl.BlockSpec(memory_space=pltpu.HBM)] * len(operands),
        out_specs=[pl.BlockSpec(memory_space=pltpu.VMEM)] * (2 * side),
        out_shape=[jax.ShapeDtypeStruct((seqs, rows, LANES), jnp.bfloat16)] * side
        + [jax.ShapeDtypeStruct((PARTS, seqs, width // PARTS, tile), jnp.bfloat16)] * side,
        scratch_shapes=[pltpu.VMEM(o.shape, o.dtype) for o in operands]
        + [
            pltpu.VMEM((2, residues, chans), jnp.bfloat16),
            pltpu.SemaphoreType.DMA((len(operands),)),
            pltpu.SemaphoreType.DMA((seqs,)),
        ],
        compiler_params=pltpu.CompilerParams(vmem_limit_bytes=32 * MIB),
        name="project",
    )(*operands)
    return out[:side], out[side:]


def arrange_kernel(seq_total, *refs):
    left_refs, out_ref, wide = refs[:-2], refs[-2], refs[-1]
    _, rows, lanes = left_refs[0].shape
    depth = out_ref.shape[2]
    at = 0
    for ref in left_refs:
        count = ref.shape[0] * rows
        wide[at : at + count] = ref[...].astype(jnp.float32).reshape(count, lanes)
        at += count
    if depth > seq_total:
        wide[seq_total * rows :] = jnp.zeros(((depth - seq_total) * rows, lanes), jnp.float32)
    for r in range(rows):
        out_ref[r] = wide[pl.ds(r, depth, stride=rows), :].T.astype(jnp.bfloat16)


def arrange_left(lefts, tile):
    _, rows, lanes = lefts[0].shape
    seq_total = sum(x.shape[0] for x in lefts)
    depth = -(-seq_total // LANES) * LANES
    return pl.pallas_call(
        functools.partial(arrange_kernel, seq_total),
        in_specs=[pl.BlockSpec(memory_space=pltpu.VMEM)] * len(lefts),
        out_specs=pl.BlockSpec(memory_space=pltpu.VMEM),
        out_shape=jax.ShapeDtypeStruct((rows, lanes, depth), jnp.bfloat16),
        scratch_shapes=[pltpu.VMEM((depth * rows, lanes), jnp.float32)],
        compiler_params=pltpu.CompilerParams(vmem_limit_bytes=32 * MIB),
        cost_estimate=pl.CostEstimate(flops=MIB, bytes_accessed=8 * MIB, transcendentals=0),
        name="arrange_left",
    )(*lefts)


def update_kernel(side, seqs, order, rights, group, first, last, left_ref, *refs):
    right_refs, refs = refs[:rights], refs[rights:]
    wt_ref, refs = refs[0], refs[1:]
    if not first:
        before_ref, refs = refs[0], refs[1:]
    if last:
        bias_ref, pair_ref, refs = refs[0], refs[1], refs[2:]
    out_ref, right_wide, right_flat, outer = refs
    rows, lanes, depth = left_ref.shape
    _, some, tile = right_refs[0].shape
    halves = outer.shape[0] // group
    pack = 2 * halves
    width = lanes // pack
    seq_total = side * side * seqs
    at = pl.program_id(0) * group

    @pl.when(pl.program_id(0) == 0)
    def _():
        dz = 0
        for ref in right_refs:
            for start in range(0, ref.shape[0], side * seqs):
                for k, dy in enumerate(order):
                    to = (k * side + dz) * seqs
                    right_wide[to * some : (to + seqs) * some] = (
                        ref[start + dy * seqs : start + (dy + 1) * seqs]
                        .astype(jnp.float32)
                        .reshape(seqs * some, tile)
                    )
                dz += 1
        if depth > seq_total:
            right_wide[seq_total * some :] = jnp.zeros(
                ((depth - seq_total) * some, tile), jnp.float32
            )
        for e in range(some):
            right_flat[:, e * tile : (e + 1) * tile] = right_wide[
                pl.ds(e, depth, stride=some), :
            ].astype(jnp.bfloat16)

    def outer_products(q):
        for n in range(some // 2):
            both = jnp.dot(
                left_ref[at + q],
                right_flat[:, 2 * n * tile : (2 * n + 2) * tile],
                preferred_element_type=jnp.float32,
            ).astype(jnp.bfloat16)
            for k in range(2):
                e = 2 * n + k
                for h in range(pack):
                    outer[
                        q * halves + h // 2,
                        e * width : (e + 1) * width,
                        (h % 2) * tile : (h % 2 + 1) * tile,
                    ] = both[h * width : (h + 1) * width, k * tile : (k + 1) * tile]

    def project_back(q):
        for g in range(halves):
            update = jnp.dot(wt_ref[...], outer[q * halves + g], preferred_element_type=jnp.float32)
            if not first:
                update = update + before_ref[at + q, g]
            if not last:
                out_ref[at + q, g] = update
                continue
            for k in range(2):
                h = 2 * g + k
                share = update[:, k * tile : (k + 1) * tile].T * (1.0 / seq_total) + bias_ref[...]
                old = pair_ref[h, at + q].astype(jnp.float32)
                out_ref[h, q] = (old + share).astype(jnp.bfloat16)

    for q in range(group + 1):
        if q < group:
            outer_products(q)
        if q > 0:
            project_back(q - 1)


def update_part(side, seqs, order, part, left, right, wt, before, bias, pair):
    rows, lanes, depth = left.shape
    some, tile = right[0].shape[-2:]
    chans = wt.shape[0]
    pack = tile // rows
    width = lanes // pack
    halves = pack // 2
    group = 8
    first, last = part == 0, part == PARTS - 1
    in_vmem = pl.BlockSpec(memory_space=pltpu.VMEM)
    operands = [left] + list(right) + [wt[:, part * some * width : (part + 1) * some * width]]
    if not first:
        operands.append(before)
    if last:
        operands += [bias[None], pair.reshape(pack, rows, tile, chans)]
        out_shape = jax.ShapeDtypeStruct((pack, rows, tile, chans), jnp.bfloat16)
        out_spec = pl.BlockSpec((pack, group, tile, chans), lambda g: (0, g, 0, 0))
    else:
        out_shape, out_spec = pltpu.VMEM((rows, halves, chans, 2 * tile), jnp.float32), in_vmem
    return pl.pallas_call(
        functools.partial(update_kernel, side, seqs, order, len(right), group, first, last),
        grid=(rows // group,),
        in_specs=[in_vmem] * len(operands),
        out_specs=out_spec,
        out_shape=out_shape,
        scratch_shapes=[
            pltpu.VMEM((depth * some, tile), jnp.float32),
            pltpu.VMEM((depth, some * tile), jnp.bfloat16),
            pltpu.VMEM((group * halves, some * width, 2 * tile), jnp.bfloat16),
        ],
        compiler_params=pltpu.CompilerParams(vmem_limit_bytes=24 * MIB),
        cost_estimate=pl.CostEstimate(
            flops=2 * tile * tile * some * width * (side * side * seqs + chans),
            bytes_accessed=16 * MIB,
            transcendentals=0,
        ),
        name="update_%d" % part,
    )(*operands)


def local(
    alignment_features,
    pairwise_features,
    standardize_scaling,
    standardize_additive,
    first_factor_matrix,
    first_factor_intercept,
    second_factor_matrix,
    second_factor_intercept,
    final_matrix,
    final_intercept,
):
    devices = lax.axis_size("row")
    side = math.isqrt(devices)
    seqs, residues, _ = alignment_features.shape
    tile = residues // side
    width = first_factor_matrix.shape[1]
    left, right = project(
        side,
        alignment_features,
        standardize_scaling,
        standardize_additive,
        first_factor_matrix,
        first_factor_intercept,
        second_factor_matrix,
        second_factor_intercept,
    )

    def swap(x, da, db):
        return lax.ppermute(x, "row", [(i, i ^ (da * side + db)) for i in range(devices)])

    left = [left[0]] + [swap(left[d], d, 0) for d in range(1, side)]
    right = [right[0]] + [swap(right[d], 0, d) for d in range(1, side)]
    left = jnp.concatenate(left)
    mines = [jnp.concatenate([x[part] for x in right]) for part in range(PARTS)]
    left, *mines = lax.optimization_barrier((left, *mines))
    lefts = [left]
    order = [0]
    mask = side // 2
    while mask > 0:
        lefts += [swap(jnp.concatenate(lefts), 0, mask)]
        order += [o ^ mask for o in order]
        mask //= 2
    near = swap(jnp.stack(mines), 1, 0)
    parts = [[mines[0], near[0]] + [swap(mines[0], d, 0) for d in range(2, side)]]
    for part in range(1, PARTS):
        pieces = [mines[part], near[part]]
        mask = 2
        while mask < side:
            pieces.append(swap(jnp.concatenate(pieces), mask, 0))
            mask *= 2
        parts.append(pieces)
    left = arrange_left(lefts, tile)
    near, final_matrix = lax.optimization_barrier((near, final_matrix))
    wt = final_matrix.reshape(width, width, -1).transpose(2, 1, 0).reshape(-1, width * width)
    total = None
    for part in range(PARTS):
        if part > 0:
            total, *parts[part] = lax.optimization_barrier((total, *parts[part]))
        total = update_part(
            side, seqs, order, part, left, parts[part], wt, total, final_intercept, pairwise_features
        )
    return total.reshape(1, tile, tile, -1)


def solution(mesh):
    placed = (
        P(("grp", "row"), None, None),
        P(("grp", "row"), None, None, None),
        P(),
        P(),
        P(),
        P(),
        P(),
        P(),
        P(),
        P(),
    )
    return jax.shard_map(
        local,
        mesh=mesh,
        in_specs=placed,
        out_specs=P(("grp", "row"), None, None, None),
        check_vma=False,
    )
```

```python
import functools
import math

import jax
import jax.numpy as jnp
from jax import lax
from jax.experimental import pallas as pl
from jax.experimental.pallas import tpu as pltpu
from jax.sharding import PartitionSpec as P

LANES = 128
PARTS = 2
MIB = 1024 * 1024


def in_hbm(x):
    return pltpu.with_memory_space_constraint(x, pltpu.HBM)


def project_kernel(side, *refs):
    sources, refs = refs[:7], refs[7:]
    left_out, right_out, refs = refs[:side], refs[side : 2 * side], refs[2 * side :]
    buffers, normed_ref, sems, x_sems = refs[:7], refs[7], refs[8], refs[9]
    x_ref, gain_ref, offset_ref, wl_ref, bl_ref, wr_ref, br_ref = buffers
    seqs, residues, chans = x_ref.shape
    width = wl_ref.shape[0]
    tile = residues // side
    pack = LANES // width
    rows = tile // pack
    x_copies = [
        pltpu.make_async_copy(sources[0].at[s], x_ref.at[s], x_sems.at[s]) for s in range(seqs)
    ]
    copies = [
        pltpu.make_async_copy(sources[k], buffers[k], sems.at[k]) for k in range(1, len(buffers))
    ]
    for copy in x_copies[:1] + copies + x_copies[1:]:
        copy.start()
    for copy in copies:
        copy.wait()
    me = lax.axis_index("row")
    place_a, place_b = me // side, lax.rem(me, side)
    nt = (((1,), (1,)), ((), ()))
    wl = wl_ref[...]
    placed = [
        jnp.concatenate([wl if k == h else jnp.zeros_like(wl) for k in range(pack)], axis=0)
        for h in range(pack)
    ]
    left_bias = jnp.concatenate([bl_ref[...]] * pack, axis=1)
    right_bias = jnp.broadcast_to(br_ref[...], (tile, width)).T
    for s in range(seqs):
        x_copies[s].wait()
        normed = normed_ref.at[s % 2]
        x = x_ref[s].astype(jnp.float32)
        center = x - jnp.mean(x, axis=-1, keepdims=True)
        variance = jnp.mean(center * center, axis=-1, keepdims=True)
        normed[...] = (
            center * lax.rsqrt(variance + 1e-05) * gain_ref[...] + offset_ref[...]
        ).astype(jnp.bfloat16)
        blocks = []
        for d in range(side):
            b = place_b ^ d
            block = normed[pl.ds(pl.multiple_of(b * tile, tile), tile), :]
            right = lax.dot_general(wr_ref[...], block, nt, preferred_element_type=jnp.float32)
            right_out[d][:, s] = (
                (right + right_bias).astype(jnp.bfloat16).reshape(PARTS, width // PARTS, tile)
            )
            a = place_a ^ d
            blocks.append(normed[pl.ds(pl.multiple_of(a * tile, tile), tile), :])
        total = left_bias
        for h in range(pack):
            picked = jnp.concatenate([block[h * rows : (h + 1) * rows] for block in blocks], axis=0)
            total = total + lax.dot_general(
                picked, placed[h], nt, preferred_element_type=jnp.float32
            )
        left = total.astype(jnp.bfloat16)
        for d in range(side):
            left_out[d][s] = left[d * rows : (d + 1) * rows]


def project(side, x, gain, offset, wl, bl, wr, br):
    seqs, residues, chans = x.shape
    width = wl.shape[1]
    tile = residues // side
    rows = tile * width // LANES
    operands = [in_hbm(o) for o in (x, gain[None], offset[None], wl.T, bl[None], wr.T, br[None])]
    out = pl.pallas_call(
        functools.partial(project_kernel, side),
        in_specs=[pl.BlockSpec(memory_space=pltpu.HBM)] * len(operands),
        out_specs=[pl.BlockSpec(memory_space=pltpu.VMEM)] * (2 * side),
        out_shape=[jax.ShapeDtypeStruct((seqs, rows, LANES), jnp.bfloat16)] * side
        + [jax.ShapeDtypeStruct((PARTS, seqs, width // PARTS, tile), jnp.bfloat16)] * side,
        scratch_shapes=[pltpu.VMEM(o.shape, o.dtype) for o in operands]
        + [
            pltpu.VMEM((2, residues, chans), jnp.bfloat16),
            pltpu.SemaphoreType.DMA((len(operands),)),
            pltpu.SemaphoreType.DMA((seqs,)),
        ],
        compiler_params=pltpu.CompilerParams(vmem_limit_bytes=32 * MIB),
        name="project",
    )(*operands)
    return out[:side], out[side:]


def arrange_kernel(seq_total, *refs):
    left_refs, out_ref, wide = refs[:-2], refs[-2], refs[-1]
    _, rows, lanes = left_refs[0].shape
    depth = out_ref.shape[2]
    at = 0
    for ref in left_refs:
        count = ref.shape[0] * rows
        wide[at : at + count] = ref[...].astype(jnp.float32).reshape(count, lanes)
        at += count
    if depth > seq_total:
        wide[seq_total * rows :] = jnp.zeros(((depth - seq_total) * rows, lanes), jnp.float32)
    for r in range(rows):
        out_ref[r] = wide[pl.ds(r, depth, stride=rows), :].T.astype(jnp.bfloat16)


def arrange_left(lefts, tile):
    _, rows, lanes = lefts[0].shape
    seq_total = sum(x.shape[0] for x in lefts)
    depth = -(-seq_total // LANES) * LANES
    return pl.pallas_call(
        functools.partial(arrange_kernel, seq_total),
        in_specs=[pl.BlockSpec(memory_space=pltpu.VMEM)] * len(lefts),
        out_specs=pl.BlockSpec(memory_space=pltpu.VMEM),
        out_shape=jax.ShapeDtypeStruct((rows, lanes, depth), jnp.bfloat16),
        scratch_shapes=[pltpu.VMEM((depth * rows, lanes), jnp.float32)],
        compiler_params=pltpu.CompilerParams(vmem_limit_bytes=32 * MIB),
        cost_estimate=pl.CostEstimate(flops=MIB, bytes_accessed=8 * MIB, transcendentals=0),
        name="arrange_left",
    )(*lefts)


def update_kernel(side, seqs, order, rights, group, first, last, left_ref, *refs):
    right_refs, refs = refs[:rights], refs[rights:]
    wt_ref, refs = refs[0], refs[1:]
    if not first:
        before_ref, refs = refs[0], refs[1:]
    if last:
        bias_ref, pair_ref, refs = refs[0], refs[1], refs[2:]
    out_ref, right_wide, right_flat, outer = refs
    rows, lanes, depth = left_ref.shape
    _, some, tile = right_refs[0].shape
    halves = outer.shape[0] // group
    pack = 2 * halves
    width = lanes // pack
    seq_total = side * side * seqs
    at = pl.program_id(0) * group

    @pl.when(pl.program_id(0) == 0)
    def _():
        dz = 0
        for ref in right_refs:
            for start in range(0, ref.shape[0], side * seqs):
                for k, dy in enumerate(order):
                    to = (k * side + dz) * seqs
                    right_wide[to * some : (to + seqs) * some] = (
                        ref[start + dy * seqs : start + (dy + 1) * seqs]
                        .astype(jnp.float32)
                        .reshape(seqs * some, tile)
                    )
                dz += 1
        if depth > seq_total:
            right_wide[seq_total * some :] = jnp.zeros(
                ((depth - seq_total) * some, tile), jnp.float32
            )
        for e in range(some):
            right_flat[:, e * tile : (e + 1) * tile] = right_wide[
                pl.ds(e, depth, stride=some), :
            ].astype(jnp.bfloat16)

    def outer_products(q):
        for n in range(some // 2):
            both = jnp.dot(
                left_ref[at + q],
                right_flat[:, 2 * n * tile : (2 * n + 2) * tile],
                preferred_element_type=jnp.float32,
            ).astype(jnp.bfloat16)
            for k in range(2):
                e = 2 * n + k
                for h in range(pack):
                    outer[
                        q * halves + h // 2,
                        e * width : (e + 1) * width,
                        (h % 2) * tile : (h % 2 + 1) * tile,
                    ] = both[h * width : (h + 1) * width, k * tile : (k + 1) * tile]

    def project_back(q):
        for g in range(halves):
            update = jnp.dot(wt_ref[...], outer[q * halves + g], preferred_element_type=jnp.float32)
            if not first:
                update = update + before_ref[at + q, g]
            if not last:
                out_ref[at + q, g] = update
                continue
            for k in range(2):
                h = 2 * g + k
                share = update[:, k * tile : (k + 1) * tile].T * (1.0 / seq_total) + bias_ref[...]
                old = pair_ref[h, at + q].astype(jnp.float32)
                out_ref[h, q] = (old + share).astype(jnp.bfloat16)

    for q in range(group + 1):
        if q < group:
            outer_products(q)
        if q > 0:
            project_back(q - 1)


def update_part(side, seqs, order, part, left, right, wt, before, bias, pair):
    rows, lanes, depth = left.shape
    some, tile = right[0].shape[-2:]
    chans = wt.shape[0]
    pack = tile // rows
    width = lanes // pack
    halves = pack // 2
    group = 8
    first, last = part == 0, part == PARTS - 1
    in_vmem = pl.BlockSpec(memory_space=pltpu.VMEM)
    operands = [left] + list(right) + [wt[:, part * some * width : (part + 1) * some * width]]
    if not first:
        operands.append(before)
    if last:
        operands += [bias[None], pair.reshape(pack, rows, tile, chans)]
        out_shape = jax.ShapeDtypeStruct((pack, rows, tile, chans), jnp.bfloat16)
        out_spec = pl.BlockSpec((pack, group, tile, chans), lambda g: (0, g, 0, 0))
    else:
        out_shape, out_spec = pltpu.VMEM((rows, halves, chans, 2 * tile), jnp.float32), in_vmem
    return pl.pallas_call(
        functools.partial(update_kernel, side, seqs, order, len(right), group, first, last),
        grid=(rows // group,),
        in_specs=[in_vmem] * len(operands),
        out_specs=out_spec,
        out_shape=out_shape,
        scratch_shapes=[
            pltpu.VMEM((depth * some, tile), jnp.float32),
            pltpu.VMEM((depth, some * tile), jnp.bfloat16),
            pltpu.VMEM((group * halves, some * width, 2 * tile), jnp.bfloat16),
        ],
        compiler_params=pltpu.CompilerParams(vmem_limit_bytes=24 * MIB),
        cost_estimate=pl.CostEstimate(
            flops=2 * tile * tile * some * width * (side * side * seqs + chans),
            bytes_accessed=16 * MIB,
            transcendentals=0,
        ),
        name="update_%d" % part,
    )(*operands)


def local(
    alignment_features,
    pairwise_features,
    standardize_scaling,
    standardize_additive,
    first_factor_matrix,
    first_factor_intercept,
    second_factor_matrix,
    second_factor_intercept,
    final_matrix,
    final_intercept,
):
    devices = lax.axis_size("row")
    side = math.isqrt(devices)
    seqs, residues, _ = alignment_features.shape
    tile = residues // side
    width = first_factor_matrix.shape[1]
    left, right = project(
        side,
        alignment_features,
        standardize_scaling,
        standardize_additive,
        first_factor_matrix,
        first_factor_intercept,
        second_factor_matrix,
        second_factor_intercept,
    )

    def swap(x, da, db):
        return lax.ppermute(x, "row", [(i, i ^ (da * side + db)) for i in range(devices)])

    right = [right[0]] + [swap(right[d], 0, d) for d in range(1, side)]
    *left, right[1] = lax.optimization_barrier((*left, right[1]))
    left = [left[0]] + [swap(left[d], d, 0) for d in range(1, side)]
    mines = [jnp.concatenate([x[part] for x in right]) for part in range(PARTS)]
    left = jnp.concatenate(left)
    near = swap(jnp.stack(mines), 1, 0)
    parts = [[mines[0], near[0]] + [swap(mines[0], d, 0) for d in range(2, side)]]
    lefts = [left]
    order = [0]
    mask = side // 2
    while mask > 0:
        lefts += [swap(jnp.concatenate(lefts), 0, mask)]
        order += [o ^ mask for o in order]
        mask //= 2
    lefts[-1], mines[-1] = lax.optimization_barrier((lefts[-1], mines[-1]))
    for part in range(1, PARTS):
        pieces = [mines[part], near[part]]
        mask = 2
        while mask < side:
            pieces.append(swap(jnp.concatenate(pieces), mask, 0))
            mask *= 2
        parts.append(pieces)
    left = arrange_left(lefts, tile)
    near, final_matrix = lax.optimization_barrier((near, final_matrix))
    wt = final_matrix.reshape(width, width, -1).transpose(2, 1, 0).reshape(-1, width * width)
    total = None
    for part in range(PARTS):
        if part > 0:
            total, *parts[part] = lax.optimization_barrier((total, *parts[part]))
        total = update_part(
            side, seqs, order, part, left, parts[part], wt, total, final_intercept, pairwise_features
        )
    return total.reshape(1, tile, tile, -1)


def solution(mesh):
    placed = (
        P(("grp", "row"), None, None),
        P(("grp", "row"), None, None, None),
        P(),
        P(),
        P(),
        P(),
        P(),
        P(),
        P(),
        P(),
    )
    return jax.shard_map(
        local,
        mesh=mesh,
        in_specs=placed,
        out_specs=P(("grp", "row"), None, None, None),
        check_vma=False,
    )
```

```python
import functools
import math

import jax
import jax.numpy as jnp
from jax import lax
from jax.experimental import pallas as pl
from jax.experimental.pallas import tpu as pltpu
from jax.sharding import PartitionSpec as P

LANES = 128
PARTS = 2
MIB = 1024 * 1024


def in_hbm(x):
    return pltpu.with_memory_space_constraint(x, pltpu.HBM)


def project_kernel(side, *refs):
    sources, refs = refs[:7], refs[7:]
    left_out, right_out, refs = refs[:side], refs[side : 2 * side], refs[2 * side :]
    buffers, normed_ref, sems, x_sems = refs[:7], refs[7], refs[8], refs[9]
    x_ref, gain_ref, offset_ref, wl_ref, bl_ref, wr_ref, br_ref = buffers
    seqs, residues, chans = x_ref.shape
    width = wl_ref.shape[0]
    tile = residues // side
    pack = LANES // width
    rows = tile // pack
    x_copies = [
        pltpu.make_async_copy(sources[0].at[s], x_ref.at[s], x_sems.at[s]) for s in range(seqs)
    ]
    copies = [
        pltpu.make_async_copy(sources[k], buffers[k], sems.at[k]) for k in range(1, len(buffers))
    ]
    for copy in x_copies[:1] + copies + x_copies[1:]:
        copy.start()
    for copy in copies:
        copy.wait()
    me = lax.axis_index("row")
    place_a, place_b = me // side, lax.rem(me, side)
    nt = (((1,), (1,)), ((), ()))
    wl = wl_ref[...]
    placed = [
        jnp.concatenate([wl if k == h else jnp.zeros_like(wl) for k in range(pack)], axis=0)
        for h in range(pack)
    ]
    left_bias = jnp.concatenate([bl_ref[...]] * pack, axis=1)
    right_bias = jnp.broadcast_to(br_ref[...], (tile, width)).T
    for s in range(seqs):
        x_copies[s].wait()
        normed = normed_ref.at[s % 2]
        x = x_ref[s].astype(jnp.float32)
        center = x - jnp.mean(x, axis=-1, keepdims=True)
        variance = jnp.mean(center * center, axis=-1, keepdims=True)
        normed[...] = (
            center * lax.rsqrt(variance + 1e-05) * gain_ref[...] + offset_ref[...]
        ).astype(jnp.bfloat16)
        blocks = []
        for d in range(side):
            b = place_b ^ d
            block = normed[pl.ds(pl.multiple_of(b * tile, tile), tile), :]
            right = lax.dot_general(wr_ref[...], block, nt, preferred_element_type=jnp.float32)
            right_out[d][:, s] = (
                (right + right_bias).astype(jnp.bfloat16).reshape(PARTS, width // PARTS, tile)
            )
            a = place_a ^ d
            blocks.append(normed[pl.ds(pl.multiple_of(a * tile, tile), tile), :])
        total = left_bias
        for h in range(pack):
            picked = jnp.concatenate([block[h * rows : (h + 1) * rows] for block in blocks], axis=0)
            total = total + lax.dot_general(
                picked, placed[h], nt, preferred_element_type=jnp.float32
            )
        left = total.astype(jnp.bfloat16)
        for d in range(side):
            left_out[d][s] = left[d * rows : (d + 1) * rows]


def project(side, x, gain, offset, wl, bl, wr, br):
    seqs, residues, chans = x.shape
    width = wl.shape[1]
    tile = residues // side
    rows = tile * width // LANES
    operands = [in_hbm(o) for o in (x, gain[None], offset[None], wl.T, bl[None], wr.T, br[None])]
    out = pl.pallas_call(
        functools.partial(project_kernel, side),
        in_specs=[pl.BlockSpec(memory_space=pltpu.HBM)] * len(operands),
        out_specs=[pl.BlockSpec(memory_space=pltpu.VMEM)] * (2 * side),
        out_shape=[jax.ShapeDtypeStruct((seqs, rows, LANES), jnp.bfloat16)] * side
        + [jax.ShapeDtypeStruct((PARTS, seqs, width // PARTS, tile), jnp.bfloat16)] * side,
        scratch_shapes=[pltpu.VMEM(o.shape, o.dtype) for o in operands]
        + [
            pltpu.VMEM((2, residues, chans), jnp.bfloat16),
            pltpu.SemaphoreType.DMA((len(operands),)),
            pltpu.SemaphoreType.DMA((seqs,)),
        ],
        compiler_params=pltpu.CompilerParams(vmem_limit_bytes=32 * MIB),
        name="project",
    )(*operands)
    return out[:side], out[side:]


def arrange_kernel(seq_total, *refs):
    left_refs, out_ref, wide = refs[:-2], refs[-2], refs[-1]
    _, rows, lanes = left_refs[0].shape
    depth = out_ref.shape[2]
    at = 0
    for ref in left_refs:
        count = ref.shape[0] * rows
        wide[at : at + count] = ref[...].astype(jnp.float32).reshape(count, lanes)
        at += count
    if depth > seq_total:
        wide[seq_total * rows :] = jnp.zeros(((depth - seq_total) * rows, lanes), jnp.float32)
    for r in range(rows):
        out_ref[r] = wide[pl.ds(r, depth, stride=rows), :].T.astype(jnp.bfloat16)


def arrange_left(lefts, tile):
    _, rows, lanes = lefts[0].shape
    seq_total = sum(x.shape[0] for x in lefts)
    depth = -(-seq_total // LANES) * LANES
    return pl.pallas_call(
        functools.partial(arrange_kernel, seq_total),
        in_specs=[pl.BlockSpec(memory_space=pltpu.VMEM)] * len(lefts),
        out_specs=pl.BlockSpec(memory_space=pltpu.VMEM),
        out_shape=jax.ShapeDtypeStruct((rows, lanes, depth), jnp.bfloat16),
        scratch_shapes=[pltpu.VMEM((depth * rows, lanes), jnp.float32)],
        compiler_params=pltpu.CompilerParams(vmem_limit_bytes=32 * MIB),
        cost_estimate=pl.CostEstimate(flops=MIB, bytes_accessed=8 * MIB, transcendentals=0),
        name="arrange_left",
    )(*lefts)


def update_kernel(side, seqs, order, rights, group, first, last, left_ref, *refs):
    right_refs, refs = refs[:rights], refs[rights:]
    wt_ref, refs = refs[0], refs[1:]
    if not first:
        before_ref, refs = refs[0], refs[1:]
    if last:
        bias_ref, pair_ref, refs = refs[0], refs[1], refs[2:]
    out_ref, right_wide, right_flat, outer = refs
    rows, lanes, depth = left_ref.shape
    _, some, tile = right_refs[0].shape
    halves = outer.shape[0] // group
    pack = 2 * halves
    width = lanes // pack
    seq_total = side * side * seqs
    at = pl.program_id(0) * group

    @pl.when(pl.program_id(0) == 0)
    def _():
        dz = 0
        for ref in right_refs:
            for start in range(0, ref.shape[0], side * seqs):
                for k, dy in enumerate(order):
                    to = (k * side + dz) * seqs
                    right_wide[to * some : (to + seqs) * some] = (
                        ref[start + dy * seqs : start + (dy + 1) * seqs]
                        .astype(jnp.float32)
                        .reshape(seqs * some, tile)
                    )
                dz += 1
        if depth > seq_total:
            right_wide[seq_total * some :] = jnp.zeros(
                ((depth - seq_total) * some, tile), jnp.float32
            )
        for e in range(some):
            right_flat[:, e * tile : (e + 1) * tile] = right_wide[
                pl.ds(e, depth, stride=some), :
            ].astype(jnp.bfloat16)

    def outer_products(q):
        for n in range(some // 2):
            both = jnp.dot(
                left_ref[at + q],
                right_flat[:, 2 * n * tile : (2 * n + 2) * tile],
                preferred_element_type=jnp.float32,
            ).astype(jnp.bfloat16)
            for k in range(2):
                e = 2 * n + k
                for h in range(pack):
                    outer[
                        q * halves + h // 2,
                        e * width : (e + 1) * width,
                        (h % 2) * tile : (h % 2 + 1) * tile,
                    ] = both[h * width : (h + 1) * width, k * tile : (k + 1) * tile]

    def project_back(q):
        for g in range(halves):
            update = jnp.dot(wt_ref[...], outer[q * halves + g], preferred_element_type=jnp.float32)
            if not first:
                update = update + before_ref[at + q, g]
            if not last:
                out_ref[at + q, g] = update
                continue
            for k in range(2):
                h = 2 * g + k
                share = update[:, k * tile : (k + 1) * tile].T * (1.0 / seq_total) + bias_ref[...]
                old = pair_ref[h, at + q].astype(jnp.float32)
                out_ref[h, q] = (old + share).astype(jnp.bfloat16)

    for q in range(group + 1):
        if q < group:
            outer_products(q)
        if q > 0:
            project_back(q - 1)


def update_part(side, seqs, order, part, left, right, wt, before, bias, pair):
    rows, lanes, depth = left.shape
    some, tile = right[0].shape[-2:]
    chans = wt.shape[0]
    pack = tile // rows
    width = lanes // pack
    halves = pack // 2
    group = 8
    first, last = part == 0, part == PARTS - 1
    in_vmem = pl.BlockSpec(memory_space=pltpu.VMEM)
    operands = [left] + list(right) + [wt[:, part * some * width : (part + 1) * some * width]]
    if not first:
        operands.append(before)
    if last:
        operands += [bias[None], pair.reshape(pack, rows, tile, chans)]
        out_shape = jax.ShapeDtypeStruct((pack, rows, tile, chans), jnp.bfloat16)
        out_spec = pl.BlockSpec((pack, group, tile, chans), lambda g: (0, g, 0, 0))
    else:
        out_shape, out_spec = pltpu.VMEM((rows, halves, chans, 2 * tile), jnp.float32), in_vmem
    return pl.pallas_call(
        functools.partial(update_kernel, side, seqs, order, len(right), group, first, last),
        grid=(rows // group,),
        in_specs=[in_vmem] * len(operands),
        out_specs=out_spec,
        out_shape=out_shape,
        scratch_shapes=[
            pltpu.VMEM((depth * some, tile), jnp.float32),
            pltpu.VMEM((depth, some * tile), jnp.bfloat16),
            pltpu.VMEM((group * halves, some * width, 2 * tile), jnp.bfloat16),
        ],
        compiler_params=pltpu.CompilerParams(vmem_limit_bytes=24 * MIB),
        cost_estimate=pl.CostEstimate(
            flops=2 * tile * tile * some * width * (side * side * seqs + chans),
            bytes_accessed=16 * MIB,
            transcendentals=0,
        ),
        name="update_%d" % part,
    )(*operands)


def local(
    alignment_features,
    pairwise_features,
    standardize_scaling,
    standardize_additive,
    first_factor_matrix,
    first_factor_intercept,
    second_factor_matrix,
    second_factor_intercept,
    final_matrix,
    final_intercept,
):
    devices = lax.axis_size("row")
    side = math.isqrt(devices)
    seqs, residues, _ = alignment_features.shape
    tile = residues // side
    width = first_factor_matrix.shape[1]
    left, right = project(
        side,
        alignment_features,
        standardize_scaling,
        standardize_additive,
        first_factor_matrix,
        first_factor_intercept,
        second_factor_matrix,
        second_factor_intercept,
    )

    def swap(x, da, db):
        return lax.ppermute(x, "row", [(i, i ^ (da * side + db)) for i in range(devices)])

    right = [right[0]] + [swap(right[d], 0, d) for d in range(1, side)]
    *left, right[1] = lax.optimization_barrier((*left, right[1]))
    left = [left[0]] + [swap(left[d], d, 0) for d in range(1, side)]
    mines = [jnp.concatenate([x[part] for x in right]) for part in range(PARTS)]
    stacked = jnp.stack(mines)
    left[1], mines[0] = lax.optimization_barrier((left[1], mines[0]))
    *left, stacked = lax.optimization_barrier((*left, stacked))
    lefts = [jnp.concatenate(left)]
    order = [0]
    mask = side // 2
    while mask > 0:
        lefts += [swap(jnp.concatenate(lefts), 0, mask)]
        order += [o ^ mask for o in order]
        mask //= 2
    near = swap(stacked, 1, 0)
    parts = [[mines[0], near[0]] + [swap(mines[0], d, 0) for d in range(2, side)]]
    for part in range(1, PARTS):
        pieces = [mines[part], near[part]]
        mask = 2
        while mask < side:
            pieces.append(swap(jnp.concatenate(pieces), mask, 0))
            mask *= 2
        parts.append(pieces)
    left = arrange_left(lefts, tile)
    near, final_matrix = lax.optimization_barrier((near, final_matrix))
    wt = final_matrix.reshape(width, width, -1).transpose(2, 1, 0).reshape(-1, width * width)
    total = None
    for part in range(PARTS):
        if part > 0:
            total, *parts[part] = lax.optimization_barrier((total, *parts[part]))
        total = update_part(
            side, seqs, order, part, left, parts[part], wt, total, final_intercept, pairwise_features
        )
    return total.reshape(1, tile, tile, -1)


def solution(mesh):
    placed = (
        P(("grp", "row"), None, None),
        P(("grp", "row"), None, None, None),
        P(),
        P(),
        P(),
        P(),
        P(),
        P(),
        P(),
        P(),
    )
    return jax.shard_map(
        local,
        mesh=mesh,
        in_specs=placed,
        out_specs=P(("grp", "row"), None, None, None),
        check_vma=False,
    )
```

```python
import functools
import math

import jax
import jax.numpy as jnp
from jax import lax
from jax.experimental import pallas as pl
from jax.experimental.pallas import tpu as pltpu
from jax.sharding import PartitionSpec as P

LANES = 128
PARTS = 2
MIB = 1024 * 1024


def in_hbm(x):
    return pltpu.with_memory_space_constraint(x, pltpu.HBM)


def project_kernel(side, *refs):
    sources, refs = refs[:7], refs[7:]
    left_out, right_out, refs = refs[:side], refs[side : 2 * side], refs[2 * side :]
    buffers, normed_ref, sems, x_sems = refs[:7], refs[7], refs[8], refs[9]
    x_ref, gain_ref, offset_ref, wl_ref, bl_ref, wr_ref, br_ref = buffers
    seqs, residues, chans = x_ref.shape
    width = wl_ref.shape[0]
    tile = residues // side
    pack = LANES // width
    rows = tile // pack
    x_copies = [
        pltpu.make_async_copy(sources[0].at[s], x_ref.at[s], x_sems.at[s]) for s in range(seqs)
    ]
    copies = [
        pltpu.make_async_copy(sources[k], buffers[k], sems.at[k]) for k in range(1, len(buffers))
    ]
    for copy in x_copies[:1] + copies + x_copies[1:]:
        copy.start()
    for copy in copies:
        copy.wait()
    me = lax.axis_index("row")
    place_a, place_b = me // side, lax.rem(me, side)
    nt = (((1,), (1,)), ((), ()))
    wl = wl_ref[...]
    placed = [
        jnp.concatenate([wl if k == h else jnp.zeros_like(wl) for k in range(pack)], axis=0)
        for h in range(pack)
    ]
    left_bias = jnp.concatenate([bl_ref[...]] * pack, axis=1)
    right_bias = jnp.broadcast_to(br_ref[...], (tile, width)).T
    for s in range(seqs):
        x_copies[s].wait()
        normed = normed_ref.at[s % 2]
        x = x_ref[s].astype(jnp.float32)
        center = x - jnp.mean(x, axis=-1, keepdims=True)
        variance = jnp.mean(center * center, axis=-1, keepdims=True)
        normed[...] = (
            center * lax.rsqrt(variance + 1e-05) * gain_ref[...] + offset_ref[...]
        ).astype(jnp.bfloat16)
        blocks = []
        for d in range(side):
            b = place_b ^ d
            block = normed[pl.ds(pl.multiple_of(b * tile, tile), tile), :]
            right = lax.dot_general(wr_ref[...], block, nt, preferred_element_type=jnp.float32)
            right_out[d][:, s] = (
                (right + right_bias).astype(jnp.bfloat16).reshape(PARTS, width // PARTS, tile)
            )
            a = place_a ^ d
            blocks.append(normed[pl.ds(pl.multiple_of(a * tile, tile), tile), :])
        total = left_bias
        for h in range(pack):
            picked = jnp.concatenate([block[h * rows : (h + 1) * rows] for block in blocks], axis=0)
            total = total + lax.dot_general(
                picked, placed[h], nt, preferred_element_type=jnp.float32
            )
        left = total.astype(jnp.bfloat16)
        for d in range(side):
            left_out[d][s] = left[d * rows : (d + 1) * rows]


def project(side, x, gain, offset, wl, bl, wr, br):
    seqs, residues, chans = x.shape
    width = wl.shape[1]
    tile = residues // side
    rows = tile * width // LANES
    operands = [in_hbm(o) for o in (x, gain[None], offset[None], wl.T, bl[None], wr.T, br[None])]
    out = pl.pallas_call(
        functools.partial(project_kernel, side),
        in_specs=[pl.BlockSpec(memory_space=pltpu.HBM)] * len(operands),
        out_specs=[pl.BlockSpec(memory_space=pltpu.VMEM)] * (2 * side),
        out_shape=[jax.ShapeDtypeStruct((seqs, rows, LANES), jnp.bfloat16)] * side
        + [jax.ShapeDtypeStruct((PARTS, seqs, width // PARTS, tile), jnp.bfloat16)] * side,
        scratch_shapes=[pltpu.VMEM(o.shape, o.dtype) for o in operands]
        + [
            pltpu.VMEM((2, residues, chans), jnp.bfloat16),
            pltpu.SemaphoreType.DMA((len(operands),)),
            pltpu.SemaphoreType.DMA((seqs,)),
        ],
        compiler_params=pltpu.CompilerParams(vmem_limit_bytes=32 * MIB),
        name="project",
    )(*operands)
    return out[:side], out[side:]


def arrange_kernel(seq_total, *refs):
    left_refs, out_ref, wide = refs[:-2], refs[-2], refs[-1]
    _, rows, lanes = left_refs[0].shape
    depth = out_ref.shape[2]
    at = 0
    for ref in left_refs:
        count = ref.shape[0] * rows
        wide[at : at + count] = ref[...].astype(jnp.float32).reshape(count, lanes)
        at += count
    if depth > seq_total:
        wide[seq_total * rows :] = jnp.zeros(((depth - seq_total) * rows, lanes), jnp.float32)
    for r in range(rows):
        out_ref[r] = wide[pl.ds(r, depth, stride=rows), :].T.astype(jnp.bfloat16)


def arrange_left(lefts, tile):
    _, rows, lanes = lefts[0].shape
    seq_total = sum(x.shape[0] for x in lefts)
    depth = -(-seq_total // LANES) * LANES
    return pl.pallas_call(
        functools.partial(arrange_kernel, seq_total),
        in_specs=[pl.BlockSpec(memory_space=pltpu.VMEM)] * len(lefts),
        out_specs=pl.BlockSpec(memory_space=pltpu.VMEM),
        out_shape=jax.ShapeDtypeStruct((rows, lanes, depth), jnp.bfloat16),
        scratch_shapes=[pltpu.VMEM((depth * rows, lanes), jnp.float32)],
        compiler_params=pltpu.CompilerParams(vmem_limit_bytes=32 * MIB),
        cost_estimate=pl.CostEstimate(flops=MIB, bytes_accessed=8 * MIB, transcendentals=0),
        name="arrange_left",
    )(*lefts)


def update_kernel(side, seqs, order, rights, group, first, last, left_ref, *refs):
    right_refs, refs = refs[:rights], refs[rights:]
    wt_ref, refs = refs[0], refs[1:]
    if not first:
        before_ref, refs = refs[0], refs[1:]
    if last:
        bias_ref, pair_ref, refs = refs[0], refs[1], refs[2:]
    out_ref, right_wide, right_flat, outer = refs
    rows, lanes, depth = left_ref.shape
    _, some, tile = right_refs[0].shape
    halves = outer.shape[0] // group
    pack = 2 * halves
    width = lanes // pack
    seq_total = side * side * seqs
    at = pl.program_id(0) * group

    @pl.when(pl.program_id(0) == 0)
    def _():
        dz = 0
        for ref in right_refs:
            for start in range(0, ref.shape[0], side * seqs):
                for k, dy in enumerate(order):
                    to = (k * side + dz) * seqs
                    right_wide[to * some : (to + seqs) * some] = (
                        ref[start + dy * seqs : start + (dy + 1) * seqs]
                        .astype(jnp.float32)
                        .reshape(seqs * some, tile)
                    )
                dz += 1
        if depth > seq_total:
            right_wide[seq_total * some :] = jnp.zeros(
                ((depth - seq_total) * some, tile), jnp.float32
            )
        for e in range(some):
            right_flat[:, e * tile : (e + 1) * tile] = right_wide[
                pl.ds(e, depth, stride=some), :
            ].astype(jnp.bfloat16)

    def outer_products(q):
        for n in range(some // 2):
            both = jnp.dot(
                left_ref[at + q],
                right_flat[:, 2 * n * tile : (2 * n + 2) * tile],
                preferred_element_type=jnp.float32,
            ).astype(jnp.bfloat16)
            for k in range(2):
                e = 2 * n + k
                for h in range(pack):
                    outer[
                        q * halves + h // 2,
                        e * width : (e + 1) * width,
                        (h % 2) * tile : (h % 2 + 1) * tile,
                    ] = both[h * width : (h + 1) * width, k * tile : (k + 1) * tile]

    def project_back(q):
        for g in range(halves):
            update = jnp.dot(wt_ref[...], outer[q * halves + g], preferred_element_type=jnp.float32)
            if not first:
                update = update + before_ref[at + q, g]
            if not last:
                out_ref[at + q, g] = update
                continue
            for k in range(2):
                h = 2 * g + k
                share = update[:, k * tile : (k + 1) * tile].T * (1.0 / seq_total) + bias_ref[...]
                old = pair_ref[h, at + q].astype(jnp.float32)
                out_ref[h, q] = (old + share).astype(jnp.bfloat16)

    for q in range(group + 1):
        if q < group:
            outer_products(q)
        if q > 0:
            project_back(q - 1)


def update_part(side, seqs, order, part, left, right, wt, before, bias, pair):
    rows, lanes, depth = left.shape
    some, tile = right[0].shape[-2:]
    chans = wt.shape[0]
    pack = tile // rows
    width = lanes // pack
    halves = pack // 2
    group = 8
    first, last = part == 0, part == PARTS - 1
    in_vmem = pl.BlockSpec(memory_space=pltpu.VMEM)
    operands = [left] + list(right) + [wt[:, part * some * width : (part + 1) * some * width]]
    if not first:
        operands.append(before)
    if last:
        operands += [bias[None], pair.reshape(pack, rows, tile, chans)]
        out_shape = jax.ShapeDtypeStruct((pack, rows, tile, chans), jnp.bfloat16)
        out_spec = pl.BlockSpec((pack, group, tile, chans), lambda g: (0, g, 0, 0))
    else:
        out_shape, out_spec = pltpu.VMEM((rows, halves, chans, 2 * tile), jnp.float32), in_vmem
    return pl.pallas_call(
        functools.partial(update_kernel, side, seqs, order, len(right), group, first, last),
        grid=(rows // group,),
        in_specs=[in_vmem] * len(operands),
        out_specs=out_spec,
        out_shape=out_shape,
        scratch_shapes=[
            pltpu.VMEM((depth * some, tile), jnp.float32),
            pltpu.VMEM((depth, some * tile), jnp.bfloat16),
            pltpu.VMEM((group * halves, some * width, 2 * tile), jnp.bfloat16),
        ],
        compiler_params=pltpu.CompilerParams(vmem_limit_bytes=24 * MIB),
        cost_estimate=pl.CostEstimate(
            flops=2 * tile * tile * some * width * (side * side * seqs + chans),
            bytes_accessed=16 * MIB,
            transcendentals=0,
        ),
        name="update_%d" % part,
    )(*operands)


def local(
    alignment_features,
    pairwise_features,
    standardize_scaling,
    standardize_additive,
    first_factor_matrix,
    first_factor_intercept,
    second_factor_matrix,
    second_factor_intercept,
    final_matrix,
    final_intercept,
):
    devices = lax.axis_size("row")
    side = math.isqrt(devices)
    seqs, residues, _ = alignment_features.shape
    tile = residues // side
    width = first_factor_matrix.shape[1]
    left, right = project(
        side,
        alignment_features,
        standardize_scaling,
        standardize_additive,
        first_factor_matrix,
        first_factor_intercept,
        second_factor_matrix,
        second_factor_intercept,
    )

    def swap(x, da, db):
        return lax.ppermute(x, "row", [(i, i ^ (da * side + db)) for i in range(devices)])

    right = [right[0]] + [swap(right[d], 0, d) for d in range(1, side)]
    *left, right[1] = lax.optimization_barrier((*left, right[1]))
    left = [left[0]] + [swap(left[d], d, 0) for d in range(1, side)]
    mines = [jnp.concatenate([x[part] for x in right]) for part in range(PARTS)]
    stacked = jnp.stack(mines)
    left[1], mines[0] = lax.optimization_barrier((left[1], mines[0]))
    *left, stacked = lax.optimization_barrier((*left, stacked))
    lefts = [jnp.concatenate(left)]
    order = [0]
    mask = side // 2
    while mask > 0:
        lefts += [swap(jnp.concatenate(lefts), 0, mask)]
        order += [o ^ mask for o in order]
        mask //= 2
    near = swap(stacked, 1, 0)
    parts = [[mines[0], near[0]] + [swap(mines[0], d, 0) for d in range(2, side)]]
    lefts[-1], *mines[1:] = lax.optimization_barrier((lefts[-1], *mines[1:]))
    for part in range(1, PARTS):
        pieces = [mines[part], near[part]]
        mask = 2
        while mask < side:
            pieces.append(swap(jnp.concatenate(pieces), mask, 0))
            mask *= 2
        parts.append(pieces)
    left = arrange_left(lefts, tile)
    near, final_matrix = lax.optimization_barrier((near, final_matrix))
    wt = final_matrix.reshape(width, width, -1).transpose(2, 1, 0).reshape(-1, width * width)
    total = None
    for part in range(PARTS):
        if part > 0:
            total, *parts[part] = lax.optimization_barrier((total, *parts[part]))
        total = update_part(
            side, seqs, order, part, left, parts[part], wt, total, final_intercept, pairwise_features
        )
    return total.reshape(1, tile, tile, -1)


def solution(mesh):
    placed = (
        P(("grp", "row"), None, None),
        P(("grp", "row"), None, None, None),
        P(),
        P(),
        P(),
        P(),
        P(),
        P(),
        P(),
        P(),
    )
    return jax.shard_map(
        local,
        mesh=mesh,
        in_specs=placed,
        out_specs=P(("grp", "row"), None, None, None),
        check_vma=False,
    )
```

```python
import functools
import math

import jax
import jax.numpy as jnp
from jax import lax
from jax.experimental import pallas as pl
from jax.experimental.pallas import tpu as pltpu
from jax.sharding import PartitionSpec as P

LANES = 128
PARTS = 2
MIB = 1024 * 1024


def in_hbm(x):
    return pltpu.with_memory_space_constraint(x, pltpu.HBM)


def project_kernel(side, *refs):
    sources, refs = refs[:7], refs[7:]
    left_out, right_out, refs = refs[:side], refs[side : 2 * side], refs[2 * side :]
    buffers, normed_ref, sems, x_sems = refs[:7], refs[7], refs[8], refs[9]
    x_ref, gain_ref, offset_ref, wl_ref, bl_ref, wr_ref, br_ref = buffers
    seqs, residues, chans = x_ref.shape
    width = wl_ref.shape[0]
    tile = residues // side
    pack = LANES // width
    rows = tile // pack
    x_copies = [
        pltpu.make_async_copy(sources[0].at[s], x_ref.at[s], x_sems.at[s]) for s in range(seqs)
    ]
    copies = [
        pltpu.make_async_copy(sources[k], buffers[k], sems.at[k]) for k in range(1, len(buffers))
    ]
    for copy in x_copies[:1] + copies + x_copies[1:]:
        copy.start()
    for copy in copies:
        copy.wait()
    me = lax.axis_index("row")
    place_a, place_b = me // side, lax.rem(me, side)
    nt = (((1,), (1,)), ((), ()))
    wl = wl_ref[...]
    placed = [
        jnp.concatenate([wl if k == h else jnp.zeros_like(wl) for k in range(pack)], axis=0)
        for h in range(pack)
    ]
    left_bias = jnp.concatenate([bl_ref[...]] * pack, axis=1)
    ones = jnp.ones((chans, LANES), jnp.bfloat16)
    right_bias = jnp.broadcast_to(br_ref[...], (tile, width)).T
    for s in range(seqs):
        x_copies[s].wait()
        normed = normed_ref.at[s % 2]
        mean = jnp.dot(x_ref[s], ones, preferred_element_type=jnp.float32) * (1.0 / chans)
        center = [
            x_ref[s, :, k : k + LANES].astype(jnp.float32) - mean for k in range(0, chans, LANES)
        ]
        square = jnp.concatenate([c * c for c in center], axis=1)
        high = square.astype(jnp.bfloat16)
        low = (square - high.astype(jnp.float32)).astype(jnp.bfloat16)
        variance = (
            jnp.dot(high, ones, preferred_element_type=jnp.float32)
            + jnp.dot(low, ones, preferred_element_type=jnp.float32)
        ) * (1.0 / chans)
        scale = lax.rsqrt(variance + 1e-05)
        for k, c in enumerate(center):
            at = slice(k * LANES, (k + 1) * LANES)
            normed[:, at] = (c * scale * gain_ref[:, at] + offset_ref[:, at]).astype(jnp.bfloat16)
        blocks = []
        for d in range(side):
            b = place_b ^ d
            block = normed[pl.ds(pl.multiple_of(b * tile, tile), tile), :]
            right = lax.dot_general(wr_ref[...], block, nt, preferred_element_type=jnp.float32)
            right_out[d][:, s] = (
                (right + right_bias).astype(jnp.bfloat16).reshape(PARTS, width // PARTS, tile)
            )
            a = place_a ^ d
            blocks.append(normed[pl.ds(pl.multiple_of(a * tile, tile), tile), :])
        total = left_bias
        for h in range(pack):
            picked = jnp.concatenate([block[h * rows : (h + 1) * rows] for block in blocks], axis=0)
            total = total + lax.dot_general(
                picked, placed[h], nt, preferred_element_type=jnp.float32
            )
        left = total.astype(jnp.bfloat16)
        for d in range(side):
            left_out[d][s] = left[d * rows : (d + 1) * rows]


def project(side, x, gain, offset, wl, bl, wr, br):
    seqs, residues, chans = x.shape
    width = wl.shape[1]
    tile = residues // side
    rows = tile * width // LANES
    operands = [in_hbm(o) for o in (x, gain[None], offset[None], wl.T, bl[None], wr.T, br[None])]
    out = pl.pallas_call(
        functools.partial(project_kernel, side),
        in_specs=[pl.BlockSpec(memory_space=pltpu.HBM)] * len(operands),
        out_specs=[pl.BlockSpec(memory_space=pltpu.VMEM)] * (2 * side),
        out_shape=[jax.ShapeDtypeStruct((seqs, rows, LANES), jnp.bfloat16)] * side
        + [jax.ShapeDtypeStruct((PARTS, seqs, width // PARTS, tile), jnp.bfloat16)] * side,
        scratch_shapes=[pltpu.VMEM(o.shape, o.dtype) for o in operands]
        + [
            pltpu.VMEM((2, residues, chans), jnp.bfloat16),
            pltpu.SemaphoreType.DMA((len(operands),)),
            pltpu.SemaphoreType.DMA((seqs,)),
        ],
        compiler_params=pltpu.CompilerParams(vmem_limit_bytes=32 * MIB),
        name="project",
    )(*operands)
    return out[:side], out[side:]


def arrange_kernel(seq_total, *refs):
    left_refs, out_ref, wide = refs[:-2], refs[-2], refs[-1]
    _, rows, lanes = left_refs[0].shape
    depth = out_ref.shape[2]
    at = 0
    for ref in left_refs:
        count = ref.shape[0] * rows
        wide[at : at + count] = ref[...].astype(jnp.float32).reshape(count, lanes)
        at += count
    if depth > seq_total:
        wide[seq_total * rows :] = jnp.zeros(((depth - seq_total) * rows, lanes), jnp.float32)
    for r in range(rows):
        out_ref[r] = wide[pl.ds(r, depth, stride=rows), :].astype(jnp.bfloat16).T


def arrange_left(lefts, tile):
    _, rows, lanes = lefts[0].shape
    seq_total = sum(x.shape[0] for x in lefts)
    depth = -(-seq_total // LANES) * LANES
    return pl.pallas_call(
        functools.partial(arrange_kernel, seq_total),
        in_specs=[pl.BlockSpec(memory_space=pltpu.VMEM)] * len(lefts),
        out_specs=pl.BlockSpec(memory_space=pltpu.VMEM),
        out_shape=jax.ShapeDtypeStruct((rows, lanes, depth), jnp.bfloat16),
        scratch_shapes=[pltpu.VMEM((depth * rows, lanes), jnp.float32)],
        compiler_params=pltpu.CompilerParams(vmem_limit_bytes=32 * MIB),
        cost_estimate=pl.CostEstimate(flops=MIB, bytes_accessed=8 * MIB, transcendentals=0),
        name="arrange_left",
    )(*lefts)


def update_kernel(side, seqs, order, rights, group, first, last, left_ref, *refs):
    right_refs, refs = refs[:rights], refs[rights:]
    wt_ref, refs = refs[0], refs[1:]
    if not first:
        before_ref, refs = refs[0], refs[1:]
    if last:
        bias_ref, pair_ref, refs = refs[0], refs[1], refs[2:]
    out_ref, right_wide, right_flat, outer, *refs = refs
    if last:
        ready, sems = refs

        def copy_out(row):
            return pltpu.make_async_copy(ready.at[:, row], out_ref.at[:, row], sems.at[row])

    rows, lanes, depth = left_ref.shape
    _, some, tile = right_refs[0].shape
    halves = outer.shape[0] // group
    pack = 2 * halves
    width = lanes // pack
    seq_total = side * side * seqs
    at = pl.program_id(0) * group

    @pl.when(pl.program_id(0) == 0)
    def _():
        dz = 0
        for ref in right_refs:
            for start in range(0, ref.shape[0], side * seqs):
                for k, dy in enumerate(order):
                    to = (k * side + dz) * seqs
                    right_wide[to * some : (to + seqs) * some] = (
                        ref[start + dy * seqs : start + (dy + 1) * seqs]
                        .astype(jnp.float32)
                        .reshape(seqs * some, tile)
                    )
                dz += 1
        if depth > seq_total:
            right_wide[seq_total * some :] = jnp.zeros(
                ((depth - seq_total) * some, tile), jnp.float32
            )
        for e in range(some):
            right_flat[:, e * tile : (e + 1) * tile] = right_wide[
                pl.ds(e, depth, stride=some), :
            ].astype(jnp.bfloat16)

    def outer_products(q):
        for n in range(some // 2):
            both = jnp.dot(
                left_ref[at + q],
                right_flat[:, 2 * n * tile : (2 * n + 2) * tile],
                preferred_element_type=jnp.float32,
            ).astype(jnp.bfloat16)
            for k in range(2):
                e = 2 * n + k
                for h in range(pack):
                    outer[
                        q * halves + h // 2,
                        e * width : (e + 1) * width,
                        (h % 2) * tile : (h % 2 + 1) * tile,
                    ] = both[h * width : (h + 1) * width, k * tile : (k + 1) * tile]

    def project_back(q):
        for g in range(halves):
            update = jnp.dot(wt_ref[...], outer[q * halves + g], preferred_element_type=jnp.float32)
            if not first:
                update = update + before_ref[at + q, g]
            if not last:
                out_ref[at + q, g] = update
                continue
            for k in range(2):
                h = 2 * g + k
                share = update[:, k * tile : (k + 1) * tile].T * (1.0 / seq_total) + bias_ref[...]
                old = pair_ref[h, at + q].astype(jnp.float32)
                ready[h, at + q] = (old + share).astype(jnp.bfloat16)
        if last:
            copy_out(at + q).start()

    for q in range(group + 1):
        if q < group:
            outer_products(q)
        if q > 0:
            project_back(q - 1)

    if last:

        @pl.when(pl.program_id(0) == pl.num_programs(0) - 1)
        def _():
            for row in range(rows):
                copy_out(row).wait()


def update_part(side, seqs, order, part, left, right, wt, before, bias, pair):
    rows, lanes, depth = left.shape
    some, tile = right[0].shape[-2:]
    chans = wt.shape[0]
    pack = tile // rows
    width = lanes // pack
    halves = pack // 2
    group = 8 if part == PARTS - 1 else 16
    first, last = part == 0, part == PARTS - 1
    in_vmem = pl.BlockSpec(memory_space=pltpu.VMEM)
    scratch = [
        pltpu.VMEM((depth * some, tile), jnp.float32),
        pltpu.VMEM((depth, some * tile), jnp.bfloat16),
        pltpu.VMEM((group * halves, some * width, 2 * tile), jnp.bfloat16),
    ]
    operands = [left] + list(right) + [wt[:, part * some * width : (part + 1) * some * width]]
    if not first:
        operands.append(before)
    if last:
        operands += [bias[None], pair.reshape(pack, rows, tile, chans)]
        out_shape = jax.ShapeDtypeStruct((pack, rows, tile, chans), jnp.bfloat16)
        out_spec = pl.BlockSpec(memory_space=pltpu.HBM)
        scratch += [
            pltpu.VMEM((pack, rows, tile, chans), jnp.bfloat16),
            pltpu.SemaphoreType.DMA((rows,)),
        ]
    else:
        out_shape, out_spec = pltpu.VMEM((rows, halves, chans, 2 * tile), jnp.float32), in_vmem
    return pl.pallas_call(
        functools.partial(update_kernel, side, seqs, order, len(right), group, first, last),
        grid=(rows // group,),
        in_specs=[in_vmem] * len(operands),
        out_specs=out_spec,
        out_shape=out_shape,
        scratch_shapes=scratch,
        compiler_params=pltpu.CompilerParams(vmem_limit_bytes=32 * MIB),
        cost_estimate=pl.CostEstimate(
            flops=2 * tile * tile * some * width * (side * side * seqs + chans),
            bytes_accessed=16 * MIB,
            transcendentals=0,
        ),
        name="update_%d" % part,
    )(*operands)


def local(
    alignment_features,
    pairwise_features,
    standardize_scaling,
    standardize_additive,
    first_factor_matrix,
    first_factor_intercept,
    second_factor_matrix,
    second_factor_intercept,
    final_matrix,
    final_intercept,
):
    devices = lax.axis_size("row")
    side = math.isqrt(devices)
    seqs, residues, _ = alignment_features.shape
    tile = residues // side
    width = first_factor_matrix.shape[1]
    left, right = project(
        side,
        alignment_features,
        standardize_scaling,
        standardize_additive,
        first_factor_matrix,
        first_factor_intercept,
        second_factor_matrix,
        second_factor_intercept,
    )

    def swap(x, da, db):
        return lax.ppermute(x, "row", [(i, i ^ (da * side + db)) for i in range(devices)])

    right = [right[0]] + [swap(right[d], 0, d) for d in range(1, side)]
    *left, right[1] = lax.optimization_barrier((*left, right[1]))
    left = [left[0]] + [swap(left[d], d, 0) for d in range(1, side)]
    mines = [jnp.concatenate([x[part] for x in right]) for part in range(PARTS)]
    stacked = jnp.stack(mines)
    left[1], mines[0] = lax.optimization_barrier((left[1], mines[0]))
    lefts = [jnp.concatenate(left)]
    order = [0]
    mask = side // 2
    while mask > 0:
        lefts += [swap(jnp.concatenate(lefts), 0, mask)]
        order += [o ^ mask for o in order]
        mask //= 2
    near = swap(stacked, 1, 0)
    parts = [[mines[0], near[0]] + [swap(mines[0], d, 0) for d in range(2, side)]]
    lefts[1], *mines[1:] = lax.optimization_barrier((lefts[1], *mines[1:]))
    for part in range(1, PARTS):
        pieces = [mines[part], near[part]]
        mask = 2
        while mask < side:
            pieces.append(swap(jnp.concatenate(pieces), mask, 0))
            mask *= 2
        parts.append(pieces)
    left = arrange_left(lefts, tile)
    near, final_matrix = lax.optimization_barrier((near, final_matrix))
    wt = final_matrix.reshape(width, width, -1).transpose(2, 1, 0).reshape(-1, width * width)
    total = None
    for part in range(PARTS):
        if part > 0:
            total, *parts[part] = lax.optimization_barrier((total, *parts[part]))
        total = update_part(
            side, seqs, order, part, left, parts[part], wt, total, final_intercept, pairwise_features
        )
    return total.reshape(1, tile, tile, -1)


def solution(mesh):
    placed = (
        P(("grp", "row"), None, None),
        P(("grp", "row"), None, None, None),
        P(),
        P(),
        P(),
        P(),
        P(),
        P(),
        P(),
        P(),
    )
    return jax.shard_map(
        local,
        mesh=mesh,
        in_specs=placed,
        out_specs=P(("grp", "row"), None, None, None),
        check_vma=False,
    )
```

```python
import functools
import math

import jax
import jax.numpy as jnp
from jax import lax
from jax.experimental import pallas as pl
from jax.experimental.pallas import tpu as pltpu
from jax.sharding import PartitionSpec as P

LANES = 128
PARTS = 2
MIB = 1024 * 1024


def in_hbm(x):
    return pltpu.with_memory_space_constraint(x, pltpu.HBM)


def project_kernel(side, *refs):
    sources, refs = refs[:7], refs[7:]
    left_out, right_out, refs = refs[:side], refs[side : 2 * side], refs[2 * side :]
    buffers, normed_ref, sems, x_sems = refs[:7], refs[7], refs[8], refs[9]
    x_ref, gain_ref, offset_ref, wl_ref, bl_ref, wr_ref, br_ref = buffers
    seqs, residues, chans = x_ref.shape
    width = wl_ref.shape[0]
    tile = residues // side
    pack = LANES // width
    rows = tile // pack
    x_copies = [
        pltpu.make_async_copy(sources[0].at[s], x_ref.at[s], x_sems.at[s]) for s in range(seqs)
    ]
    copies = [
        pltpu.make_async_copy(sources[k], buffers[k], sems.at[k]) for k in range(1, len(buffers))
    ]
    for copy in x_copies[:1] + copies + x_copies[1:]:
        copy.start()
    for copy in copies:
        copy.wait()
    me = lax.axis_index("row")
    place_a, place_b = me // side, lax.rem(me, side)
    nt = (((1,), (1,)), ((), ()))
    wl = wl_ref[...]
    placed = [
        jnp.concatenate([wl if k == h else jnp.zeros_like(wl) for k in range(pack)], axis=0)
        for h in range(pack)
    ]
    left_bias = jnp.concatenate([bl_ref[...]] * pack, axis=1)
    right_bias = jnp.broadcast_to(br_ref[...], (tile, width)).T
    for s in range(seqs):
        x_copies[s].wait()
        normed = normed_ref.at[s % 2]
        x = x_ref[s].astype(jnp.float32)
        center = x - jnp.mean(x, axis=-1, keepdims=True)
        variance = jnp.mean(center * center, axis=-1, keepdims=True)
        normed[...] = (
            center * lax.rsqrt(variance + 1e-05) * gain_ref[...] + offset_ref[...]
        ).astype(jnp.bfloat16)
        blocks = []
        for d in range(side):
            b = place_b ^ d
            block = normed[pl.ds(pl.multiple_of(b * tile, tile), tile), :]
            right = lax.dot_general(wr_ref[...], block, nt, preferred_element_type=jnp.float32)
            right_out[d][:, s] = (
                (right + right_bias).astype(jnp.bfloat16).reshape(PARTS, width // PARTS, tile)
            )
            a = place_a ^ d
            blocks.append(normed[pl.ds(pl.multiple_of(a * tile, tile), tile), :])
        total = left_bias
        for h in range(pack):
            picked = jnp.concatenate([block[h * rows : (h + 1) * rows] for block in blocks], axis=0)
            total = total + lax.dot_general(
                picked, placed[h], nt, preferred_element_type=jnp.float32
            )
        left = total.astype(jnp.bfloat16)
        for d in range(side):
            left_out[d][s] = left[d * rows : (d + 1) * rows]


def project(side, x, gain, offset, wl, bl, wr, br):
    seqs, residues, chans = x.shape
    width = wl.shape[1]
    tile = residues // side
    rows = tile * width // LANES
    operands = [in_hbm(o) for o in (x, gain[None], offset[None], wl.T, bl[None], wr.T, br[None])]
    out = pl.pallas_call(
        functools.partial(project_kernel, side),
        in_specs=[pl.BlockSpec(memory_space=pltpu.HBM)] * len(operands),
        out_specs=[pl.BlockSpec(memory_space=pltpu.VMEM)] * (2 * side),
        out_shape=[jax.ShapeDtypeStruct((seqs, rows, LANES), jnp.bfloat16)] * side
        + [jax.ShapeDtypeStruct((PARTS, seqs, width // PARTS, tile), jnp.bfloat16)] * side,
        scratch_shapes=[pltpu.VMEM(o.shape, o.dtype) for o in operands]
        + [
            pltpu.VMEM((2, residues, chans), jnp.bfloat16),
            pltpu.SemaphoreType.DMA((len(operands),)),
            pltpu.SemaphoreType.DMA((seqs,)),
        ],
        compiler_params=pltpu.CompilerParams(vmem_limit_bytes=32 * MIB),
        name="project",
    )(*operands)
    return out[:side], out[side:]


def arrange_kernel(seq_total, *refs):
    left_refs, out_ref, wide = refs[:-2], refs[-2], refs[-1]
    _, rows, lanes = left_refs[0].shape
    depth = out_ref.shape[2]
    at = 0
    for ref in left_refs:
        count = ref.shape[0] * rows
        wide[at : at + count] = ref[...].astype(jnp.float32).reshape(count, lanes)
        at += count
    if depth > seq_total:
        wide[seq_total * rows :] = jnp.zeros(((depth - seq_total) * rows, lanes), jnp.float32)
    for r in range(rows):
        out_ref[r] = wide[pl.ds(r, depth, stride=rows), :].T.astype(jnp.bfloat16)


def arrange_left(lefts, tile):
    _, rows, lanes = lefts[0].shape
    seq_total = sum(x.shape[0] for x in lefts)
    depth = -(-seq_total // LANES) * LANES
    return pl.pallas_call(
        functools.partial(arrange_kernel, seq_total),
        in_specs=[pl.BlockSpec(memory_space=pltpu.VMEM)] * len(lefts),
        out_specs=pl.BlockSpec(memory_space=pltpu.VMEM),
        out_shape=jax.ShapeDtypeStruct((rows, lanes, depth), jnp.bfloat16),
        scratch_shapes=[pltpu.VMEM((depth * rows, lanes), jnp.float32)],
        compiler_params=pltpu.CompilerParams(vmem_limit_bytes=32 * MIB),
        cost_estimate=pl.CostEstimate(flops=MIB, bytes_accessed=8 * MIB, transcendentals=0),
        name="arrange_left",
    )(*lefts)


def update_kernel(side, seqs, order, rights, group, first, last, left_ref, *refs):
    right_refs, refs = refs[:rights], refs[rights:]
    wt_ref, refs = refs[0], refs[1:]
    if not first:
        before_ref, refs = refs[0], refs[1:]
    if last:
        bias_ref, pair_ref, refs = refs[0], refs[1], refs[2:]
    out_ref, right_wide, right_flat, outer = refs
    rows, lanes, depth = left_ref.shape
    _, some, tile = right_refs[0].shape
    halves = outer.shape[0] // group
    pack = 2 * halves
    width = lanes // pack
    seq_total = side * side * seqs
    at = pl.program_id(0) * group

    @pl.when(pl.program_id(0) == 0)
    def _():
        dz = 0
        for ref in right_refs:
            for start in range(0, ref.shape[0], side * seqs):
                for k, dy in enumerate(order):
                    to = (k * side + dz) * seqs
                    right_wide[to * some : (to + seqs) * some] = (
                        ref[start + dy * seqs : start + (dy + 1) * seqs]
                        .astype(jnp.float32)
                        .reshape(seqs * some, tile)
                    )
                dz += 1
        if depth > seq_total:
            right_wide[seq_total * some :] = jnp.zeros(
                ((depth - seq_total) * some, tile), jnp.float32
            )
        for e in range(some):
            right_flat[:, e * tile : (e + 1) * tile] = right_wide[
                pl.ds(e, depth, stride=some), :
            ].astype(jnp.bfloat16)

    def outer_products(q):
        for n in range(some // 2):
            both = jnp.dot(
                left_ref[at + q],
                right_flat[:, 2 * n * tile : (2 * n + 2) * tile],
                preferred_element_type=jnp.float32,
            ).astype(jnp.bfloat16)
            for k in range(2):
                e = 2 * n + k
                for h in range(pack):
                    outer[
                        q * halves + h // 2,
                        e * width : (e + 1) * width,
                        (h % 2) * tile : (h % 2 + 1) * tile,
                    ] = both[h * width : (h + 1) * width, k * tile : (k + 1) * tile]

    def project_back(q):
        for g in range(halves):
            update = jnp.dot(wt_ref[...], outer[q * halves + g], preferred_element_type=jnp.float32)
            if not first:
                update = update + before_ref[at + q, g]
            if not last:
                out_ref[at + q, g] = update
                continue
            for k in range(2):
                h = 2 * g + k
                share = update[:, k * tile : (k + 1) * tile].T * (1.0 / seq_total) + bias_ref[...]
                old = pair_ref[h, at + q].astype(jnp.float32)
                out_ref[h, q] = (old + share).astype(jnp.bfloat16)

    for q in range(group + 1):
        if q < group:
            outer_products(q)
        if q > 0:
            project_back(q - 1)


def update_part(side, seqs, order, part, left, right, wt, before, bias, pair):
    rows, lanes, depth = left.shape
    some, tile = right[0].shape[-2:]
    chans = wt.shape[0]
    pack = tile // rows
    width = lanes // pack
    halves = pack // 2
    group = 16 if part == 0 else 16
    first, last = part == 0, part == PARTS - 1
    in_vmem = pl.BlockSpec(memory_space=pltpu.VMEM)
    operands = [left] + list(right) + [wt[:, part * some * width : (part + 1) * some * width]]
    if not first:
        operands.append(before)
    if last:
        operands += [bias[None], pair.reshape(pack, rows, tile, chans)]
        out_shape = jax.ShapeDtypeStruct((pack, rows, tile, chans), jnp.bfloat16)
        out_spec = pl.BlockSpec((pack, group, tile, chans), lambda g: (0, g, 0, 0))
    else:
        out_shape, out_spec = pltpu.VMEM((rows, halves, chans, 2 * tile), jnp.float32), in_vmem
    return pl.pallas_call(
        functools.partial(update_kernel, side, seqs, order, len(right), group, first, last),
        grid=(rows // group,),
        in_specs=[in_vmem] * len(operands),
        out_specs=out_spec,
        out_shape=out_shape,
        scratch_shapes=[
            pltpu.VMEM((depth * some, tile), jnp.float32),
            pltpu.VMEM((depth, some * tile), jnp.bfloat16),
            pltpu.VMEM((group * halves, some * width, 2 * tile), jnp.bfloat16),
        ],
        compiler_params=pltpu.CompilerParams(vmem_limit_bytes=24 * MIB),
        cost_estimate=pl.CostEstimate(
            flops=2 * tile * tile * some * width * (side * side * seqs + chans),
            bytes_accessed=16 * MIB,
            transcendentals=0,
        ),
        name="update_%d" % part,
    )(*operands)


def local(
    alignment_features,
    pairwise_features,
    standardize_scaling,
    standardize_additive,
    first_factor_matrix,
    first_factor_intercept,
    second_factor_matrix,
    second_factor_intercept,
    final_matrix,
    final_intercept,
):
    devices = lax.axis_size("row")
    side = math.isqrt(devices)
    seqs, residues, _ = alignment_features.shape
    tile = residues // side
    width = first_factor_matrix.shape[1]
    left, right = project(
        side,
        alignment_features,
        standardize_scaling,
        standardize_additive,
        first_factor_matrix,
        first_factor_intercept,
        second_factor_matrix,
        second_factor_intercept,
    )

    def swap(x, da, db):
        return lax.ppermute(x, "row", [(i, i ^ (da * side + db)) for i in range(devices)])

    right = [right[0]] + [swap(right[d], 0, d) for d in range(1, side)]
    *left, right[1] = lax.optimization_barrier((*left, right[1]))
    left = [left[0]] + [swap(left[d], d, 0) for d in range(1, side)]
    mines = [jnp.concatenate([x[part] for x in right]) for part in range(PARTS)]
    stacked = jnp.stack(mines)
    left[3], mines[0] = lax.optimization_barrier((left[3], mines[0]))
    lefts = [jnp.concatenate(left)]
    order = [0]
    mask = side // 2
    while mask > 0:
        lefts += [swap(x, 0, mask) for x in lefts]
        order += [o ^ mask for o in order]
        mask //= 2
    near = swap(stacked, 1, 0)
    parts = [[mines[0], near[0]] + [swap(mines[0], d, 0) for d in range(2, side)]]
    lefts[-1], *mines[1:] = lax.optimization_barrier((lefts[-1], *mines[1:]))
    for part in range(1, PARTS):
        pieces = [mines[part], near[part]]
        mask = 2
        while mask < side:
            pieces.append(swap(jnp.concatenate(pieces), mask, 0))
            mask *= 2
        parts.append(pieces)
    left = arrange_left(lefts, tile)
    near, final_matrix = lax.optimization_barrier((near, final_matrix))
    wt = final_matrix.reshape(width, width, -1).transpose(2, 1, 0).reshape(-1, width * width)
    total = None
    for part in range(PARTS):
        if part > 0:
            total, *parts[part] = lax.optimization_barrier((total, *parts[part]))
        total = update_part(
            side, seqs, order, part, left, parts[part], wt, total, final_intercept, pairwise_features
        )
    return total.reshape(1, tile, tile, -1)


def solution(mesh):
    placed = (
        P(("grp", "row"), None, None),
        P(("grp", "row"), None, None, None),
        P(),
        P(),
        P(),
        P(),
        P(),
        P(),
        P(),
        P(),
    )
    return jax.shard_map(
        local,
        mesh=mesh,
        in_specs=placed,
        out_specs=P(("grp", "row"), None, None, None),
        check_vma=False,
    )
```

```python
import functools
import math

import jax
import jax.numpy as jnp
from jax import lax
from jax.experimental import pallas as pl
from jax.experimental.pallas import tpu as pltpu
from jax.sharding import PartitionSpec as P

LANES = 128
PARTS = 2
MIB = 1024 * 1024


def in_hbm(x):
    return pltpu.with_memory_space_constraint(x, pltpu.HBM)


def project_kernel(side, *refs):
    sources, refs = refs[:7], refs[7:]
    left_out, right_out, refs = refs[:side], refs[side : 2 * side], refs[2 * side :]
    buffers, normed_ref, sems, x_sems = refs[:7], refs[7], refs[8], refs[9]
    x_ref, gain_ref, offset_ref, wl_ref, bl_ref, wr_ref, br_ref = buffers
    seqs, residues, chans = x_ref.shape
    width = wl_ref.shape[0]
    tile = residues // side
    pack = LANES // width
    rows = tile // pack
    x_copies = [
        pltpu.make_async_copy(sources[0].at[s], x_ref.at[s], x_sems.at[s]) for s in range(seqs)
    ]
    copies = [
        pltpu.make_async_copy(sources[k], buffers[k], sems.at[k]) for k in range(1, len(buffers))
    ]
    for copy in x_copies[:1] + copies + x_copies[1:]:
        copy.start()
    for copy in copies:
        copy.wait()
    me = lax.axis_index("row")
    place_a, place_b = me // side, lax.rem(me, side)
    nt = (((1,), (1,)), ((), ()))
    wl = wl_ref[...]
    placed = [
        jnp.concatenate([wl if k == h else jnp.zeros_like(wl) for k in range(pack)], axis=0)
        for h in range(pack)
    ]
    left_bias = jnp.concatenate([bl_ref[...]] * pack, axis=1)
    right_bias = jnp.broadcast_to(br_ref[...], (tile, width)).T
    for s in range(seqs):
        x_copies[s].wait()
        normed = normed_ref.at[s % 2]
        x = x_ref[s].astype(jnp.float32)
        center = x - jnp.mean(x, axis=-1, keepdims=True)
        variance = jnp.mean(center * center, axis=-1, keepdims=True)
        normed[...] = (
            center * lax.rsqrt(variance + 1e-05) * gain_ref[...] + offset_ref[...]
        ).astype(jnp.bfloat16)
        blocks = []
        for d in range(side):
            b = place_b ^ d
            block = normed[pl.ds(pl.multiple_of(b * tile, tile), tile), :]
            right = lax.dot_general(wr_ref[...], block, nt, preferred_element_type=jnp.float32)
            right_out[d][:, s] = (
                (right + right_bias).astype(jnp.bfloat16).reshape(PARTS, width // PARTS, tile)
            )
            a = place_a ^ d
            blocks.append(normed[pl.ds(pl.multiple_of(a * tile, tile), tile), :])
        total = left_bias
        for h in range(pack):
            picked = jnp.concatenate([block[h * rows : (h + 1) * rows] for block in blocks], axis=0)
            total = total + lax.dot_general(
                picked, placed[h], nt, preferred_element_type=jnp.float32
            )
        left = total.astype(jnp.bfloat16)
        for d in range(side):
            left_out[d][s] = left[d * rows : (d + 1) * rows]


def project(side, x, gain, offset, wl, bl, wr, br):
    seqs, residues, chans = x.shape
    width = wl.shape[1]
    tile = residues // side
    rows = tile * width // LANES
    operands = [in_hbm(o) for o in (x, gain[None], offset[None], wl.T, bl[None], wr.T, br[None])]
    out = pl.pallas_call(
        functools.partial(project_kernel, side),
        in_specs=[pl.BlockSpec(memory_space=pltpu.HBM)] * len(operands),
        out_specs=[pl.BlockSpec(memory_space=pltpu.VMEM)] * (2 * side),
        out_shape=[jax.ShapeDtypeStruct((seqs, rows, LANES), jnp.bfloat16)] * side
        + [jax.ShapeDtypeStruct((PARTS, seqs, width // PARTS, tile), jnp.bfloat16)] * side,
        scratch_shapes=[pltpu.VMEM(o.shape, o.dtype) for o in operands]
        + [
            pltpu.VMEM((2, residues, chans), jnp.bfloat16),
            pltpu.SemaphoreType.DMA((len(operands),)),
            pltpu.SemaphoreType.DMA((seqs,)),
        ],
        compiler_params=pltpu.CompilerParams(vmem_limit_bytes=32 * MIB),
        name="project",
    )(*operands)
    return out[:side], out[side:]


def arrange_kernel(seq_total, *refs):
    left_refs, out_ref, wide = refs[:-2], refs[-2], refs[-1]
    _, rows, lanes = left_refs[0].shape
    depth = out_ref.shape[2]
    at = 0
    for ref in left_refs:
        count = ref.shape[0] * rows
        wide[at : at + count] = ref[...].astype(jnp.float32).reshape(count, lanes)
        at += count
    if depth > seq_total:
        wide[seq_total * rows :] = jnp.zeros(((depth - seq_total) * rows, lanes), jnp.float32)
    for r in range(rows):
        out_ref[r] = wide[pl.ds(r, depth, stride=rows), :].T.astype(jnp.bfloat16)


def arrange_left(lefts, tile):
    _, rows, lanes = lefts[0].shape
    seq_total = sum(x.shape[0] for x in lefts)
    depth = -(-seq_total // LANES) * LANES
    return pl.pallas_call(
        functools.partial(arrange_kernel, seq_total),
        in_specs=[pl.BlockSpec(memory_space=pltpu.VMEM)] * len(lefts),
        out_specs=pl.BlockSpec(memory_space=pltpu.VMEM),
        out_shape=jax.ShapeDtypeStruct((rows, lanes, depth), jnp.bfloat16),
        scratch_shapes=[pltpu.VMEM((depth * rows, lanes), jnp.float32)],
        compiler_params=pltpu.CompilerParams(vmem_limit_bytes=32 * MIB),
        cost_estimate=pl.CostEstimate(flops=MIB, bytes_accessed=8 * MIB, transcendentals=0),
        name="arrange_left",
    )(*lefts)


def update_kernel(side, seqs, order, rights, group, first, last, left_ref, *refs):
    right_refs, refs = refs[:rights], refs[rights:]
    wt_ref, refs = refs[0], refs[1:]
    if not first:
        before_ref, refs = refs[0], refs[1:]
    if last:
        bias_ref, pair_ref, refs = refs[0], refs[1], refs[2:]
    out_ref, right_wide, right_flat, outer = refs
    rows, lanes, depth = left_ref.shape
    _, some, tile = right_refs[0].shape
    halves = outer.shape[0] // group
    pack = 2 * halves
    width = lanes // pack
    seq_total = side * side * seqs
    at = pl.program_id(0) * group

    @pl.when(pl.program_id(0) == 0)
    def _():
        dz = 0
        for ref in right_refs:
            for start in range(0, ref.shape[0], side * seqs):
                for k, dy in enumerate(order):
                    to = (k * side + dz) * seqs
                    right_wide[to * some : (to + seqs) * some] = (
                        ref[start + dy * seqs : start + (dy + 1) * seqs]
                        .astype(jnp.float32)
                        .reshape(seqs * some, tile)
                    )
                dz += 1
        if depth > seq_total:
            right_wide[seq_total * some :] = jnp.zeros(
                ((depth - seq_total) * some, tile), jnp.float32
            )
        for e in range(some):
            right_flat[:, e * tile : (e + 1) * tile] = right_wide[
                pl.ds(e, depth, stride=some), :
            ].astype(jnp.bfloat16)

    def outer_products(q, n):
        both = jnp.dot(
            left_ref[at + q],
            right_flat[:, 2 * n * tile : (2 * n + 2) * tile],
            preferred_element_type=jnp.float32,
        ).astype(jnp.bfloat16)
        for k in range(2):
            e = 2 * n + k
            for h in range(pack):
                outer[
                    q * halves + h // 2,
                    e * width : (e + 1) * width,
                    (h % 2) * tile : (h % 2 + 1) * tile,
                ] = both[h * width : (h + 1) * width, k * tile : (k + 1) * tile]

    def project_back(q, g):
        update = jnp.dot(wt_ref[...], outer[q * halves + g], preferred_element_type=jnp.float32)
        if not first:
            update = update + before_ref[at + q, g]
        if not last:
            out_ref[at + q, g] = update
            return
        for k in range(2):
            h = 2 * g + k
            share = update[:, k * tile : (k + 1) * tile].T * (1.0 / seq_total) + bias_ref[...]
            old = pair_ref[h, at + q].astype(jnp.float32)
            out_ref[h, q] = (old + share).astype(jnp.bfloat16)

    products = some // 2
    for q in range(group + 1):
        for g in range(halves):
            if q > 0:
                project_back(q - 1, g)
            if q < group:
                for n in range(g * products // halves, (g + 1) * products // halves):
                    outer_products(q, n)


def update_part(side, seqs, order, part, left, right, wt, before, bias, pair):
    rows, lanes, depth = left.shape
    some, tile = right[0].shape[-2:]
    chans = wt.shape[0]
    pack = tile // rows
    width = lanes // pack
    halves = pack // 2
    group = 16
    first, last = part == 0, part == PARTS - 1
    in_vmem = pl.BlockSpec(memory_space=pltpu.VMEM)
    operands = [left] + list(right) + [wt[:, part * some * width : (part + 1) * some * width]]
    if not first:
        operands.append(before)
    if last:
        operands += [bias[None], pair.reshape(pack, rows, tile, chans)]
        out_shape = jax.ShapeDtypeStruct((pack, rows, tile, chans), jnp.bfloat16)
        out_spec = pl.BlockSpec((pack, group, tile, chans), lambda g: (0, g, 0, 0))
    else:
        out_shape, out_spec = pltpu.VMEM((rows, halves, chans, 2 * tile), jnp.float32), in_vmem
    return pl.pallas_call(
        functools.partial(update_kernel, side, seqs, order, len(right), group, first, last),
        grid=(rows // group,),
        in_specs=[in_vmem] * len(operands),
        out_specs=out_spec,
        out_shape=out_shape,
        scratch_shapes=[
            pltpu.VMEM((depth * some, tile), jnp.float32),
            pltpu.VMEM((depth, some * tile), jnp.bfloat16),
            pltpu.VMEM((group * halves, some * width, 2 * tile), jnp.bfloat16),
        ],
        compiler_params=pltpu.CompilerParams(vmem_limit_bytes=24 * MIB),
        cost_estimate=pl.CostEstimate(
            flops=2 * tile * tile * some * width * (side * side * seqs + chans),
            bytes_accessed=16 * MIB,
            transcendentals=0,
        ),
        name="update_%d" % part,
    )(*operands)


def local(
    alignment_features,
    pairwise_features,
    standardize_scaling,
    standardize_additive,
    first_factor_matrix,
    first_factor_intercept,
    second_factor_matrix,
    second_factor_intercept,
    final_matrix,
    final_intercept,
):
    devices = lax.axis_size("row")
    side = math.isqrt(devices)
    seqs, residues, _ = alignment_features.shape
    tile = residues // side
    width = first_factor_matrix.shape[1]
    left, right = project(
        side,
        alignment_features,
        standardize_scaling,
        standardize_additive,
        first_factor_matrix,
        first_factor_intercept,
        second_factor_matrix,
        second_factor_intercept,
    )

    def swap(x, da, db):
        return lax.ppermute(x, "row", [(i, i ^ (da * side + db)) for i in range(devices)])

    right = [right[0]] + [swap(right[d], 0, d) for d in range(1, side)]
    *left, right[1] = lax.optimization_barrier((*left, right[1]))
    left = [left[0]] + [swap(left[d], d, 0) for d in range(1, side)]
    mines = [jnp.concatenate([x[part] for x in right]) for part in range(PARTS)]
    left = jnp.concatenate(left)
    near = swap(jnp.stack(mines), 1, 0)
    parts = [[mines[0], near[0]] + [swap(mines[0], d, 0) for d in range(2, side)]]
    lefts = [left]
    order = [0]
    mask = side // 2
    while mask > 0:
        lefts += [swap(jnp.concatenate(lefts), 0, mask)]
        order += [o ^ mask for o in order]
        mask //= 2
    lefts[-1], mines[-1] = lax.optimization_barrier((lefts[-1], mines[-1]))
    for part in range(1, PARTS):
        pieces = [mines[part], near[part]]
        mask = 2
        while mask < side:
            pieces.append(swap(jnp.concatenate(pieces), mask, 0))
            mask *= 2
        parts.append(pieces)
    left = arrange_left(lefts, tile)
    near, final_matrix = lax.optimization_barrier((near, final_matrix))
    wt = final_matrix.reshape(width, width, -1).transpose(2, 1, 0).reshape(-1, width * width)
    total = None
    for part in range(PARTS):
        if part > 0:
            total, *parts[part] = lax.optimization_barrier((total, *parts[part]))
        total = update_part(
            side, seqs, order, part, left, parts[part], wt, total, final_intercept, pairwise_features
        )
    return total.reshape(1, tile, tile, -1)


def solution(mesh):
    placed = (
        P(("grp", "row"), None, None),
        P(("grp", "row"), None, None, None),
        P(),
        P(),
        P(),
        P(),
        P(),
        P(),
        P(),
        P(),
    )
    return jax.shard_map(
        local,
        mesh=mesh,
        in_specs=placed,
        out_specs=P(("grp", "row"), None, None, None),
        check_vma=False,
    )
```

```python
import functools
import math

import jax
import jax.numpy as jnp
from jax import lax
from jax.experimental import pallas as pl
from jax.experimental.pallas import tpu as pltpu
from jax.sharding import PartitionSpec as P

LANES = 128
PARTS = 2
MIB = 1024 * 1024
RUN = 4


def in_hbm(x):
    return pltpu.with_memory_space_constraint(x, pltpu.HBM)


def project_kernel(side, *refs):
    sources, refs = refs[:7], refs[7:]
    left_out, right_out, refs = refs[:side], refs[side : 2 * side], refs[2 * side :]
    buffers, normed_ref, sems, x_sems = refs[:7], refs[7], refs[8], refs[9]
    x_ref, gain_ref, offset_ref, wl_ref, bl_ref, wr_ref, br_ref = buffers
    seqs, residues, chans = x_ref.shape
    width = wl_ref.shape[0]
    tile = residues // side
    pack = LANES // width
    rows = tile // pack
    x_copies = [
        pltpu.make_async_copy(sources[0].at[s], x_ref.at[s], x_sems.at[s]) for s in range(seqs)
    ]
    copies = [
        pltpu.make_async_copy(sources[k], buffers[k], sems.at[k]) for k in range(1, len(buffers))
    ]
    for copy in x_copies[:1] + copies + x_copies[1:]:
        copy.start()
    for copy in copies:
        copy.wait()
    me = lax.axis_index("row")
    place_a, place_b = me // side, lax.rem(me, side)
    nt = (((1,), (1,)), ((), ()))
    wl = wl_ref[...]
    placed = [
        jnp.concatenate([wl if k == h else jnp.zeros_like(wl) for k in range(pack)], axis=0)
        for h in range(pack)
    ]
    left_bias = jnp.concatenate([bl_ref[...]] * pack, axis=1)
    right_bias = jnp.broadcast_to(br_ref[...], (tile, width)).T
    for s in range(seqs):
        x_copies[s].wait()
        normed = normed_ref.at[s % 2]
        x = x_ref[s].astype(jnp.float32)
        center = x - jnp.mean(x, axis=-1, keepdims=True)
        variance = jnp.mean(center * center, axis=-1, keepdims=True)
        normed[...] = (
            center * lax.rsqrt(variance + 1e-05) * gain_ref[...] + offset_ref[...]
        ).astype(jnp.bfloat16)
        blocks = []
        for d in range(side):
            b = place_b ^ d
            block = normed[pl.ds(pl.multiple_of(b * tile, tile), tile), :]
            right = lax.dot_general(wr_ref[...], block, nt, preferred_element_type=jnp.float32)
            right_out[d][:, s] = (
                (right + right_bias).astype(jnp.bfloat16).reshape(PARTS, width // PARTS, tile)
            )
            a = place_a ^ d
            blocks.append(normed[pl.ds(pl.multiple_of(a * tile, tile), tile), :])
        total = left_bias
        for h in range(pack):
            picked = jnp.concatenate([block[h * rows : (h + 1) * rows] for block in blocks], axis=0)
            total = total + lax.dot_general(
                picked, placed[h], nt, preferred_element_type=jnp.float32
            )
        left = total.astype(jnp.bfloat16)
        for d in range(side):
            left_out[d][s] = left[d * rows : (d + 1) * rows]


def project(side, x, gain, offset, wl, bl, wr, br):
    seqs, residues, chans = x.shape
    width = wl.shape[1]
    tile = residues // side
    rows = tile * width // LANES
    operands = [in_hbm(o) for o in (x, gain[None], offset[None], wl.T, bl[None], wr.T, br[None])]
    out = pl.pallas_call(
        functools.partial(project_kernel, side),
        in_specs=[pl.BlockSpec(memory_space=pltpu.HBM)] * len(operands),
        out_specs=[pl.BlockSpec(memory_space=pltpu.VMEM)] * (2 * side),
        out_shape=[jax.ShapeDtypeStruct((seqs, rows, LANES), jnp.bfloat16)] * side
        + [jax.ShapeDtypeStruct((PARTS, seqs, width // PARTS, tile), jnp.bfloat16)] * side,
        scratch_shapes=[pltpu.VMEM(o.shape, o.dtype) for o in operands]
        + [
            pltpu.VMEM((2, residues, chans), jnp.bfloat16),
            pltpu.SemaphoreType.DMA((len(operands),)),
            pltpu.SemaphoreType.DMA((seqs,)),
        ],
        compiler_params=pltpu.CompilerParams(vmem_limit_bytes=32 * MIB),
        name="project",
    )(*operands)
    return out[:side], out[side:]


def arrange_kernel(seq_total, *refs):
    left_refs, out_ref, wide = refs[:-2], refs[-2], refs[-1]
    _, rows, lanes = left_refs[0].shape
    depth = out_ref.shape[2]
    at = 0
    for ref in left_refs:
        count = ref.shape[0] * rows
        wide[at : at + count] = ref[...].astype(jnp.float32).reshape(count, lanes)
        at += count
    if depth > seq_total:
        wide[seq_total * rows :] = jnp.zeros(((depth - seq_total) * rows, lanes), jnp.float32)
    for r in range(rows):
        out_ref[r] = wide[pl.ds(r, depth, stride=rows), :].T.astype(jnp.bfloat16)


def arrange_left(lefts, tile):
    _, rows, lanes = lefts[0].shape
    seq_total = sum(x.shape[0] for x in lefts)
    depth = -(-seq_total // LANES) * LANES
    return pl.pallas_call(
        functools.partial(arrange_kernel, seq_total),
        in_specs=[pl.BlockSpec(memory_space=pltpu.VMEM)] * len(lefts),
        out_specs=pl.BlockSpec(memory_space=pltpu.VMEM),
        out_shape=jax.ShapeDtypeStruct((rows, lanes, depth), jnp.bfloat16),
        scratch_shapes=[pltpu.VMEM((depth * rows, lanes), jnp.float32)],
        compiler_params=pltpu.CompilerParams(vmem_limit_bytes=32 * MIB),
        cost_estimate=pl.CostEstimate(flops=MIB, bytes_accessed=8 * MIB, transcendentals=0),
        name="arrange_left",
    )(*lefts)


def update_kernel(side, seqs, order, rights, group, first, last, left_ref, *refs):
    right_refs, refs = refs[:rights], refs[rights:]
    wt_ref, refs = refs[0], refs[1:]
    if not first:
        before_ref, refs = refs[0], refs[1:]
    if last:
        bias_ref, pair_ref, refs = refs[0], refs[1], refs[2:]
    out_ref, right_wide, right_flat, outer = refs
    rows, lanes, depth = left_ref.shape
    _, some, tile = right_refs[0].shape
    halves = outer.shape[0] // group
    pack = 2 * halves
    width = lanes // pack
    seq_total = side * side * seqs
    at = pl.program_id(0) * group

    @pl.when(pl.program_id(0) == 0)
    def _():
        dz = 0
        for ref in right_refs:
            for start in range(0, ref.shape[0], side * seqs):
                for k, dy in enumerate(order):
                    to = (k * side + dz) * seqs
                    right_wide[to * some : (to + seqs) * some] = (
                        ref[start + dy * seqs : start + (dy + 1) * seqs]
                        .astype(jnp.float32)
                        .reshape(seqs * some, tile)
                    )
                dz += 1
        if depth > seq_total:
            right_wide[seq_total * some :] = jnp.zeros(
                ((depth - seq_total) * some, tile), jnp.float32
            )
        for e in range(some):
            right_flat[:, e * tile : (e + 1) * tile] = right_wide[
                pl.ds(e, depth, stride=some), :
            ].astype(jnp.bfloat16)

    def outer_products(q):
        for n in range(some // 2):
            both = jnp.dot(
                left_ref[at + q],
                right_flat[:, 2 * n * tile : (2 * n + 2) * tile],
                preferred_element_type=jnp.float32,
            ).astype(jnp.bfloat16)
            for k in range(2):
                e = 2 * n + k
                for h in range(pack):
                    outer[
                        q * halves + h // 2,
                        e * width : (e + 1) * width,
                        (h % 2) * tile : (h % 2 + 1) * tile,
                    ] = both[h * width : (h + 1) * width, k * tile : (k + 1) * tile]

    def project_back(q):
        for g in range(halves):
            update = jnp.dot(wt_ref[...], outer[q * halves + g], preferred_element_type=jnp.float32)
            if not first:
                update = update + before_ref[at + q, g]
            if not last:
                out_ref[at + q, g] = update
                continue
            for k in range(2):
                h = 2 * g + k
                share = update[:, k * tile : (k + 1) * tile].T * (1.0 / seq_total) + bias_ref[...]
                old = pair_ref[h, at + q].astype(jnp.float32)
                out_ref[h, q] = (old + share).astype(jnp.bfloat16)

    for start in range(0, group + RUN, RUN):
        for q in range(start, start + RUN):
            if q < group:
                outer_products(q)
        for q in range(start - RUN, start):
            if q >= 0:
                project_back(q)


def update_part(side, seqs, order, part, left, right, wt, before, bias, pair):
    rows, lanes, depth = left.shape
    some, tile = right[0].shape[-2:]
    chans = wt.shape[0]
    pack = tile // rows
    width = lanes // pack
    halves = pack // 2
    group = 16
    first, last = part == 0, part == PARTS - 1
    in_vmem = pl.BlockSpec(memory_space=pltpu.VMEM)
    operands = [left] + list(right) + [wt[:, part * some * width : (part + 1) * some * width]]
    if not first:
        operands.append(before)
    if last:
        operands += [bias[None], pair.reshape(pack, rows, tile, chans)]
        out_shape = jax.ShapeDtypeStruct((pack, rows, tile, chans), jnp.bfloat16)
        out_spec = pl.BlockSpec((pack, group, tile, chans), lambda g: (0, g, 0, 0))
    else:
        out_shape, out_spec = pltpu.VMEM((rows, halves, chans, 2 * tile), jnp.float32), in_vmem
    return pl.pallas_call(
        functools.partial(update_kernel, side, seqs, order, len(right), group, first, last),
        grid=(rows // group,),
        in_specs=[in_vmem] * len(operands),
        out_specs=out_spec,
        out_shape=out_shape,
        scratch_shapes=[
            pltpu.VMEM((depth * some, tile), jnp.float32),
            pltpu.VMEM((depth, some * tile), jnp.bfloat16),
            pltpu.VMEM((group * halves, some * width, 2 * tile), jnp.bfloat16),
        ],
        compiler_params=pltpu.CompilerParams(vmem_limit_bytes=24 * MIB),
        cost_estimate=pl.CostEstimate(
            flops=2 * tile * tile * some * width * (side * side * seqs + chans),
            bytes_accessed=16 * MIB,
            transcendentals=0,
        ),
        name="update_%d" % part,
    )(*operands)


def local(
    alignment_features,
    pairwise_features,
    standardize_scaling,
    standardize_additive,
    first_factor_matrix,
    first_factor_intercept,
    second_factor_matrix,
    second_factor_intercept,
    final_matrix,
    final_intercept,
):
    devices = lax.axis_size("row")
    side = math.isqrt(devices)
    seqs, residues, _ = alignment_features.shape
    tile = residues // side
    width = first_factor_matrix.shape[1]
    left, right = project(
        side,
        alignment_features,
        standardize_scaling,
        standardize_additive,
        first_factor_matrix,
        first_factor_intercept,
        second_factor_matrix,
        second_factor_intercept,
    )

    def swap(x, da, db):
        return lax.ppermute(x, "row", [(i, i ^ (da * side + db)) for i in range(devices)])

    right = [right[0]] + [swap(right[d], 0, d) for d in range(1, side)]
    *left, right[1] = lax.optimization_barrier((*left, right[1]))
    left = [left[0]] + [swap(left[d], d, 0) for d in range(1, side)]
    mines = [jnp.concatenate([x[part] for x in right]) for part in range(PARTS)]
    left = jnp.concatenate(left)
    near = swap(jnp.stack(mines), 1, 0)
    parts = [[mines[0], near[0]] + [swap(mines[0], d, 0) for d in range(2, side)]]
    lefts = [left]
    order = [0]
    mask = side // 2
    while mask > 0:
        lefts += [swap(jnp.concatenate(lefts), 0, mask)]
        order += [o ^ mask for o in order]
        mask //= 2
    lefts[-1], mines[-1] = lax.optimization_barrier((lefts[-1], mines[-1]))
    for part in range(1, PARTS):
        pieces = [mines[part], near[part]]
        mask = 2
        while mask < side:
            pieces.append(swap(jnp.concatenate(pieces), mask, 0))
            mask *= 2
        parts.append(pieces)
    left = arrange_left(lefts, tile)
    near, final_matrix = lax.optimization_barrier((near, final_matrix))
    wt = final_matrix.reshape(width, width, -1).transpose(2, 1, 0).reshape(-1, width * width)
    total = None
    for part in range(PARTS):
        if part > 0:
            total, *parts[part] = lax.optimization_barrier((total, *parts[part]))
        total = update_part(
            side, seqs, order, part, left, parts[part], wt, total, final_intercept, pairwise_features
        )
    return total.reshape(1, tile, tile, -1)


def solution(mesh):
    placed = (
        P(("grp", "row"), None, None),
        P(("grp", "row"), None, None, None),
        P(),
        P(),
        P(),
        P(),
        P(),
        P(),
        P(),
        P(),
    )
    return jax.shard_map(
        local,
        mesh=mesh,
        in_specs=placed,
        out_specs=P(("grp", "row"), None, None, None),
        check_vma=False,
    )
```

```python
import functools
import math

import jax
import jax.numpy as jnp
from jax import lax
from jax.experimental import pallas as pl
from jax.experimental.pallas import tpu as pltpu
from jax.sharding import PartitionSpec as P

LANES = 128
PARTS = 2
MIB = 1024 * 1024
RUN = 4


def in_hbm(x):
    return pltpu.with_memory_space_constraint(x, pltpu.HBM)


def project_kernel(side, *refs):
    sources, refs = refs[:7], refs[7:]
    left_out, right_out, refs = refs[0], refs[1], refs[2:]
    buffers, sems, x_sems = refs[:7], refs[7], refs[8]
    x_ref, gain_ref, offset_ref, wl_ref, bl_ref, wr_ref, br_ref = buffers
    seqs, residues, chans = x_ref.shape
    width = wl_ref.shape[0]
    tile = residues // side
    pack = LANES // width
    rows = tile // pack
    x_copies = [
        pltpu.make_async_copy(sources[0].at[s], x_ref.at[s], x_sems.at[s]) for s in range(seqs)
    ]
    copies = [
        pltpu.make_async_copy(sources[k], buffers[k], sems.at[k]) for k in range(1, len(buffers))
    ]
    for copy in x_copies[:1] + copies + x_copies[1:]:
        copy.start()
    for copy in copies:
        copy.wait()
    me = lax.axis_index("row")
    place_a, place_b = me // side, lax.rem(me, side)
    nt = (((1,), (1,)), ((), ()))
    wl = wl_ref[...]
    placed = [
        jnp.concatenate([wl if k == h else jnp.zeros_like(wl) for k in range(pack)], axis=0)
        for h in range(pack)
    ]
    left_bias = jnp.concatenate([bl_ref[...]] * pack, axis=1)
    right_bias = jnp.broadcast_to(br_ref[...], (tile, width)).T
    for s in range(seqs):
        x_copies[s].wait()
        x = x_ref[s].astype(jnp.float32)
        center = x - jnp.mean(x, axis=-1, keepdims=True)
        variance = jnp.mean(center * center, axis=-1, keepdims=True)
        normed = (center * lax.rsqrt(variance + 1e-05) * gain_ref[...] + offset_ref[...]).astype(
            jnp.bfloat16
        )
        right = lax.dot_general(wr_ref[...], normed, nt, preferred_element_type=jnp.float32)
        total = left_bias
        for h in range(pack):
            picked = jnp.concatenate(
                [normed[a * tile + h * rows : a * tile + (h + 1) * rows] for a in range(side)],
                axis=0,
            )
            total = total + lax.dot_general(
                picked, placed[h], nt, preferred_element_type=jnp.float32
            )
        left = total.astype(jnp.bfloat16)
        for k in range(side):
            left_out[place_a ^ k, s] = left[k * rows : (k + 1) * rows]
            right_out[place_b ^ k, :, s] = (
                (right[:, k * tile : (k + 1) * tile] + right_bias)
                .astype(jnp.bfloat16)
                .reshape(PARTS, width // PARTS, tile)
            )


def project(side, x, gain, offset, wl, bl, wr, br):
    seqs, residues, chans = x.shape
    width = wl.shape[1]
    tile = residues // side
    rows = tile * width // LANES
    operands = [in_hbm(o) for o in (x, gain[None], offset[None], wl.T, bl[None], wr.T, br[None])]
    out = pl.pallas_call(
        functools.partial(project_kernel, side),
        in_specs=[pl.BlockSpec(memory_space=pltpu.HBM)] * len(operands),
        out_specs=[pl.BlockSpec(memory_space=pltpu.VMEM)] * 2,
        out_shape=[
            jax.ShapeDtypeStruct((side, seqs, rows, LANES), jnp.bfloat16),
            jax.ShapeDtypeStruct((side, PARTS, seqs, width // PARTS, tile), jnp.bfloat16),
        ],
        scratch_shapes=[pltpu.VMEM(o.shape, o.dtype) for o in operands]
        + [
            pltpu.SemaphoreType.DMA((len(operands),)),
            pltpu.SemaphoreType.DMA((seqs,)),
        ],
        compiler_params=pltpu.CompilerParams(vmem_limit_bytes=32 * MIB),
        name="project",
    )(*operands)
    return list(out[0]), list(out[1])


def arrange_kernel(seq_total, *refs):
    left_refs, out_ref, wide = refs[:-2], refs[-2], refs[-1]
    _, rows, lanes = left_refs[0].shape
    depth = out_ref.shape[2]
    at = 0
    for ref in left_refs:
        count = ref.shape[0] * rows
        wide[at : at + count] = ref[...].astype(jnp.float32).reshape(count, lanes)
        at += count
    if depth > seq_total:
        wide[seq_total * rows :] = jnp.zeros(((depth - seq_total) * rows, lanes), jnp.float32)
    for r in range(rows):
        out_ref[r] = wide[pl.ds(r, depth, stride=rows), :].T.astype(jnp.bfloat16)


def arrange_left(lefts, tile):
    _, rows, lanes = lefts[0].shape
    seq_total = sum(x.shape[0] for x in lefts)
    depth = -(-seq_total // LANES) * LANES
    return pl.pallas_call(
        functools.partial(arrange_kernel, seq_total),
        in_specs=[pl.BlockSpec(memory_space=pltpu.VMEM)] * len(lefts),
        out_specs=pl.BlockSpec(memory_space=pltpu.VMEM),
        out_shape=jax.ShapeDtypeStruct((rows, lanes, depth), jnp.bfloat16),
        scratch_shapes=[pltpu.VMEM((depth * rows, lanes), jnp.float32)],
        compiler_params=pltpu.CompilerParams(vmem_limit_bytes=32 * MIB),
        cost_estimate=pl.CostEstimate(flops=MIB, bytes_accessed=8 * MIB, transcendentals=0),
        name="arrange_left",
    )(*lefts)


def update_kernel(side, seqs, order, rights, group, first, last, left_ref, *refs):
    right_refs, refs = refs[:rights], refs[rights:]
    wt_ref, refs = refs[0], refs[1:]
    if not first:
        before_ref, refs = refs[0], refs[1:]
    if last:
        bias_ref, pair_ref, refs = refs[0], refs[1], refs[2:]
    out_ref, right_wide, right_flat, outer = refs
    rows, lanes, depth = left_ref.shape
    _, some, tile = right_refs[0].shape
    halves = outer.shape[0] // group
    pack = 2 * halves
    width = lanes // pack
    seq_total = side * side * seqs
    at = pl.program_id(0) * group

    @pl.when(pl.program_id(0) == 0)
    def _():
        dz = 0
        for ref in right_refs:
            for start in range(0, ref.shape[0], side * seqs):
                for k, dy in enumerate(order):
                    to = (k * side + dz) * seqs
                    right_wide[to * some : (to + seqs) * some] = (
                        ref[start + dy * seqs : start + (dy + 1) * seqs]
                        .astype(jnp.float32)
                        .reshape(seqs * some, tile)
                    )
                dz += 1
        if depth > seq_total:
            right_wide[seq_total * some :] = jnp.zeros(
                ((depth - seq_total) * some, tile), jnp.float32
            )
        for e in range(some):
            right_flat[:, e * tile : (e + 1) * tile] = right_wide[
                pl.ds(e, depth, stride=some), :
            ].astype(jnp.bfloat16)

    def outer_products(q):
        for n in range(some // 2):
            both = jnp.dot(
                left_ref[at + q],
                right_flat[:, 2 * n * tile : (2 * n + 2) * tile],
                preferred_element_type=jnp.float32,
            ).astype(jnp.bfloat16)
            for k in range(2):
                e = 2 * n + k
                for h in range(pack):
                    outer[
                        q * halves + h // 2,
                        e * width : (e + 1) * width,
                        (h % 2) * tile : (h % 2 + 1) * tile,
                    ] = both[h * width : (h + 1) * width, k * tile : (k + 1) * tile]

    def project_back(q):
        for g in range(halves):
            update = jnp.dot(wt_ref[...], outer[q * halves + g], preferred_element_type=jnp.float32)
            if not first:
                update = update + before_ref[at + q, g]
            if not last:
                out_ref[at + q, g] = update
                continue
            for k in range(2):
                h = 2 * g + k
                share = update[:, k * tile : (k + 1) * tile].T * (1.0 / seq_total) + bias_ref[...]
                old = pair_ref[h, at + q].astype(jnp.float32)
                out_ref[h, q] = (old + share).astype(jnp.bfloat16)

    for start in range(0, group + RUN, RUN):
        for q in range(start, start + RUN):
            if q < group:
                outer_products(q)
        for q in range(start - RUN, start):
            if q >= 0:
                project_back(q)


def update_part(side, seqs, order, part, left, right, wt, before, bias, pair):
    rows, lanes, depth = left.shape
    some, tile = right[0].shape[-2:]
    chans = wt.shape[0]
    pack = tile // rows
    width = lanes // pack
    halves = pack // 2
    group = 16
    first, last = part == 0, part == PARTS - 1
    in_vmem = pl.BlockSpec(memory_space=pltpu.VMEM)
    operands = [left] + list(right) + [wt[:, part * some * width : (part + 1) * some * width]]
    if not first:
        operands.append(before)
    if last:
        operands += [bias[None], pair.reshape(pack, rows, tile, chans)]
        out_shape = jax.ShapeDtypeStruct((pack, rows, tile, chans), jnp.bfloat16)
        out_spec = pl.BlockSpec((pack, group, tile, chans), lambda g: (0, g, 0, 0))
    else:
        out_shape, out_spec = pltpu.VMEM((rows, halves, chans, 2 * tile), jnp.float32), in_vmem
    return pl.pallas_call(
        functools.partial(update_kernel, side, seqs, order, len(right), group, first, last),
        grid=(rows // group,),
        in_specs=[in_vmem] * len(operands),
        out_specs=out_spec,
        out_shape=out_shape,
        scratch_shapes=[
            pltpu.VMEM((depth * some, tile), jnp.float32),
            pltpu.VMEM((depth, some * tile), jnp.bfloat16),
            pltpu.VMEM((group * halves, some * width, 2 * tile), jnp.bfloat16),
        ],
        compiler_params=pltpu.CompilerParams(vmem_limit_bytes=24 * MIB),
        cost_estimate=pl.CostEstimate(
            flops=2 * tile * tile * some * width * (side * side * seqs + chans),
            bytes_accessed=16 * MIB,
            transcendentals=0,
        ),
        name="update_%d" % part,
    )(*operands)


def local(
    alignment_features,
    pairwise_features,
    standardize_scaling,
    standardize_additive,
    first_factor_matrix,
    first_factor_intercept,
    second_factor_matrix,
    second_factor_intercept,
    final_matrix,
    final_intercept,
):
    devices = lax.axis_size("row")
    side = math.isqrt(devices)
    seqs, residues, _ = alignment_features.shape
    tile = residues // side
    width = first_factor_matrix.shape[1]
    left, right = project(
        side,
        alignment_features,
        standardize_scaling,
        standardize_additive,
        first_factor_matrix,
        first_factor_intercept,
        second_factor_matrix,
        second_factor_intercept,
    )

    def swap(x, da, db):
        return lax.ppermute(x, "row", [(i, i ^ (da * side + db)) for i in range(devices)])

    right = [right[0]] + [swap(right[d], 0, d) for d in range(1, side)]
    *left, right[1] = lax.optimization_barrier((*left, right[1]))
    left = [left[0]] + [swap(left[d], d, 0) for d in range(1, side)]
    mines = [jnp.concatenate([x[part] for x in right]) for part in range(PARTS)]
    left = jnp.concatenate(left)
    near = swap(jnp.stack(mines), 1, 0)
    parts = [[mines[0], near[0]] + [swap(mines[0], d, 0) for d in range(2, side)]]
    lefts = [left]
    order = [0]
    mask = side // 2
    while mask > 0:
        lefts += [swap(jnp.concatenate(lefts), 0, mask)]
        order += [o ^ mask for o in order]
        mask //= 2
    lefts[-1], mines[-1] = lax.optimization_barrier((lefts[-1], mines[-1]))
    for part in range(1, PARTS):
        pieces = [mines[part], near[part]]
        mask = 2
        while mask < side:
            pieces.append(swap(jnp.concatenate(pieces), mask, 0))
            mask *= 2
        parts.append(pieces)
    left = arrange_left(lefts, tile)
    near, final_matrix = lax.optimization_barrier((near, final_matrix))
    wt = final_matrix.reshape(width, width, -1).transpose(2, 1, 0).reshape(-1, width * width)
    total = None
    for part in range(PARTS):
        if part > 0:
            total, *parts[part] = lax.optimization_barrier((total, *parts[part]))
        total = update_part(
            side, seqs, order, part, left, parts[part], wt, total, final_intercept, pairwise_features
        )
    return total.reshape(1, tile, tile, -1)


def solution(mesh):
    placed = (
        P(("grp", "row"), None, None),
        P(("grp", "row"), None, None, None),
        P(),
        P(),
        P(),
        P(),
        P(),
        P(),
        P(),
        P(),
    )
    return jax.shard_map(
        local,
        mesh=mesh,
        in_specs=placed,
        out_specs=P(("grp", "row"), None, None, None),
        check_vma=False,
    )
```

```python
import functools
import math

import jax
import jax.numpy as jnp
from jax import lax
from jax.experimental import pallas as pl
from jax.experimental.pallas import tpu as pltpu
from jax.sharding import PartitionSpec as P

LANES = 128
PARTS = 2
MIB = 1024 * 1024
RUN = 4


def in_hbm(x):
    return pltpu.with_memory_space_constraint(x, pltpu.HBM)


def project_kernel(side, *refs):
    sources, refs = refs[:7], refs[7:]
    left_out, right_out, refs = refs[:side], refs[side : 2 * side], refs[2 * side :]
    buffers, left_all, right_all, sems, x_sems = refs[:7], refs[7], refs[8], refs[9], refs[10]
    x_ref, gain_ref, offset_ref, wl_ref, bl_ref, wr_ref, br_ref = buffers
    seqs, residues, chans = x_ref.shape
    width = wl_ref.shape[0]
    tile = residues // side
    pack = LANES // width
    rows = tile // pack
    x_copies = [
        pltpu.make_async_copy(sources[0].at[s], x_ref.at[s], x_sems.at[s]) for s in range(seqs)
    ]
    copies = [
        pltpu.make_async_copy(sources[k], buffers[k], sems.at[k]) for k in range(1, len(buffers))
    ]
    for copy in x_copies[:1] + copies + x_copies[1:]:
        copy.start()
    for copy in copies:
        copy.wait()
    me = lax.axis_index("row")
    place_a, place_b = me // side, lax.rem(me, side)
    wl, wr = wl_ref[...], wr_ref[...]
    blank = jnp.zeros_like(wl)
    weights = []
    for h in range(pack):
        left_rows = jnp.concatenate([wl if k == h else blank for k in range(pack)], axis=0)
        right_rows = jnp.concatenate([wr] + [blank] * (pack - 1), axis=0)
        weights.append(jnp.concatenate([left_rows.T, right_rows.T], axis=1))
    left_bias = jnp.concatenate([bl_ref[...]] * pack, axis=1)
    right_bias = jnp.concatenate([br_ref[...]] * pack, axis=1)
    for s in range(seqs):
        x_copies[s].wait()
        x = x_ref[s].astype(jnp.float32)
        center = x - jnp.mean(x, axis=-1, keepdims=True)
        variance = jnp.mean(center * center, axis=-1, keepdims=True)
        normed = (center * lax.rsqrt(variance + 1e-05) * gain_ref[...] + offset_ref[...]).astype(
            jnp.bfloat16
        )
        total = left_bias
        rights = []
        for h in range(pack):
            picked = jnp.concatenate(
                [normed[a * tile + h * rows : a * tile + (h + 1) * rows] for a in range(side)],
                axis=0,
            )
            both = jnp.dot(picked, weights[h], preferred_element_type=jnp.float32)
            total = total + both[:, :LANES]
            rights.append((both[:, LANES:] + right_bias).astype(jnp.bfloat16))
        left = total.astype(jnp.bfloat16)
        for k in range(side):
            left_all[place_a ^ k, s] = left[k * rows : (k + 1) * rows]
            right = jnp.concatenate([r[k * rows : (k + 1) * rows] for r in rights], axis=0).T
            right_all[place_b ^ k, :, s] = right[:width].reshape(PARTS, width // PARTS, tile)
    for d in range(side):
        left_out[d][...] = left_all[d]
        right_out[d][...] = right_all[d]


def project(side, x, gain, offset, wl, bl, wr, br):
    seqs, residues, chans = x.shape
    width = wl.shape[1]
    tile = residues // side
    rows = tile * width // LANES
    operands = [in_hbm(o) for o in (x, gain[None], offset[None], wl.T, bl[None], wr.T, br[None])]
    out = pl.pallas_call(
        functools.partial(project_kernel, side),
        in_specs=[pl.BlockSpec(memory_space=pltpu.HBM)] * len(operands),
        out_specs=[pl.BlockSpec(memory_space=pltpu.VMEM)] * (2 * side),
        out_shape=[jax.ShapeDtypeStruct((seqs, rows, LANES), jnp.bfloat16)] * side
        + [jax.ShapeDtypeStruct((PARTS, seqs, width // PARTS, tile), jnp.bfloat16)] * side,
        scratch_shapes=[pltpu.VMEM(o.shape, o.dtype) for o in operands]
        + [
            pltpu.VMEM((side, seqs, rows, LANES), jnp.bfloat16),
            pltpu.VMEM((side, PARTS, seqs, width // PARTS, tile), jnp.bfloat16),
            pltpu.SemaphoreType.DMA((len(operands),)),
            pltpu.SemaphoreType.DMA((seqs,)),
        ],
        compiler_params=pltpu.CompilerParams(vmem_limit_bytes=32 * MIB),
        name="project",
    )(*operands)
    return out[:side], out[side:]


def arrange_kernel(seq_total, *refs):
    left_refs, out_ref, wide = refs[:-2], refs[-2], refs[-1]
    _, rows, lanes = left_refs[0].shape
    depth = out_ref.shape[2]
    at = 0
    for ref in left_refs:
        count = ref.shape[0] * rows
        wide[at : at + count] = ref[...].astype(jnp.float32).reshape(count, lanes)
        at += count
    if depth > seq_total:
        wide[seq_total * rows :] = jnp.zeros(((depth - seq_total) * rows, lanes), jnp.float32)
    for r in range(rows):
        out_ref[r] = wide[pl.ds(r, depth, stride=rows), :].T.astype(jnp.bfloat16)


def arrange_left(lefts, tile):
    _, rows, lanes = lefts[0].shape
    seq_total = sum(x.shape[0] for x in lefts)
    depth = -(-seq_total // LANES) * LANES
    return pl.pallas_call(
        functools.partial(arrange_kernel, seq_total),
        in_specs=[pl.BlockSpec(memory_space=pltpu.VMEM)] * len(lefts),
        out_specs=pl.BlockSpec(memory_space=pltpu.VMEM),
        out_shape=jax.ShapeDtypeStruct((rows, lanes, depth), jnp.bfloat16),
        scratch_shapes=[pltpu.VMEM((depth * rows, lanes), jnp.float32)],
        compiler_params=pltpu.CompilerParams(vmem_limit_bytes=32 * MIB),
        cost_estimate=pl.CostEstimate(flops=MIB, bytes_accessed=8 * MIB, transcendentals=0),
        name="arrange_left",
    )(*lefts)


def update_kernel(side, seqs, order, rights, group, first, last, left_ref, *refs):
    right_refs, refs = refs[:rights], refs[rights:]
    wt_ref, refs = refs[0], refs[1:]
    if not first:
        before_ref, refs = refs[0], refs[1:]
    if last:
        bias_ref, pair_ref, refs = refs[0], refs[1], refs[2:]
    out_ref, right_wide, right_flat, outer = refs
    rows, lanes, depth = left_ref.shape
    _, some, tile = right_refs[0].shape
    halves = outer.shape[0] // group
    pack = 2 * halves
    width = lanes // pack
    seq_total = side * side * seqs
    at = pl.program_id(0) * group

    @pl.when(pl.program_id(0) == 0)
    def _():
        dz = 0
        for ref in right_refs:
            for start in range(0, ref.shape[0], side * seqs):
                for k, dy in enumerate(order):
                    to = (k * side + dz) * seqs
                    right_wide[to * some : (to + seqs) * some] = (
                        ref[start + dy * seqs : start + (dy + 1) * seqs]
                        .astype(jnp.float32)
                        .reshape(seqs * some, tile)
                    )
                dz += 1
        if depth > seq_total:
            right_wide[seq_total * some :] = jnp.zeros(
                ((depth - seq_total) * some, tile), jnp.float32
            )
        for e in range(some):
            right_flat[:, e * tile : (e + 1) * tile] = right_wide[
                pl.ds(e, depth, stride=some), :
            ].astype(jnp.bfloat16)

    def outer_products(q):
        for n in range(some // 2):
            both = jnp.dot(
                left_ref[at + q],
                right_flat[:, 2 * n * tile : (2 * n + 2) * tile],
                preferred_element_type=jnp.float32,
            ).astype(jnp.bfloat16)
            for k in range(2):
                e = 2 * n + k
                for h in range(pack):
                    outer[
                        q * halves + h // 2,
                        e * width : (e + 1) * width,
                        (h % 2) * tile : (h % 2 + 1) * tile,
                    ] = both[h * width : (h + 1) * width, k * tile : (k + 1) * tile]

    def project_back(q):
        for g in range(halves):
            update = jnp.dot(wt_ref[...], outer[q * halves + g], preferred_element_type=jnp.float32)
            if not first:
                update = update + before_ref[at + q, g]
            if not last:
                out_ref[at + q, g] = update
                continue
            for k in range(2):
                h = 2 * g + k
                share = update[:, k * tile : (k + 1) * tile].T * (1.0 / seq_total) + bias_ref[...]
                old = pair_ref[h, at + q].astype(jnp.float32)
                out_ref[h, q] = (old + share).astype(jnp.bfloat16)

    for start in range(0, group + RUN, RUN):
        for q in range(start, start + RUN):
            if q < group:
                outer_products(q)
        for q in range(start - RUN, start):
            if q >= 0:
                project_back(q)


def update_part(side, seqs, order, part, left, right, wt, before, bias, pair):
    rows, lanes, depth = left.shape
    some, tile = right[0].shape[-2:]
    chans = wt.shape[0]
    pack = tile // rows
    width = lanes // pack
    halves = pack // 2
    group = 16
    first, last = part == 0, part == PARTS - 1
    in_vmem = pl.BlockSpec(memory_space=pltpu.VMEM)
    operands = [left] + list(right) + [wt[:, part * some * width : (part + 1) * some * width]]
    if not first:
        operands.append(before)
    if last:
        operands += [bias[None], pair.reshape(pack, rows, tile, chans)]
        out_shape = jax.ShapeDtypeStruct((pack, rows, tile, chans), jnp.bfloat16)
        out_spec = pl.BlockSpec((pack, group, tile, chans), lambda g: (0, g, 0, 0))
    else:
        out_shape, out_spec = pltpu.VMEM((rows, halves, chans, 2 * tile), jnp.float32), in_vmem
    return pl.pallas_call(
        functools.partial(update_kernel, side, seqs, order, len(right), group, first, last),
        grid=(rows // group,),
        in_specs=[in_vmem] * len(operands),
        out_specs=out_spec,
        out_shape=out_shape,
        scratch_shapes=[
            pltpu.VMEM((depth * some, tile), jnp.float32),
            pltpu.VMEM((depth, some * tile), jnp.bfloat16),
            pltpu.VMEM((group * halves, some * width, 2 * tile), jnp.bfloat16),
        ],
        compiler_params=pltpu.CompilerParams(vmem_limit_bytes=24 * MIB),
        cost_estimate=pl.CostEstimate(
            flops=2 * tile * tile * some * width * (side * side * seqs + chans),
            bytes_accessed=16 * MIB,
            transcendentals=0,
        ),
        name="update_%d" % part,
    )(*operands)


def local(
    alignment_features,
    pairwise_features,
    standardize_scaling,
    standardize_additive,
    first_factor_matrix,
    first_factor_intercept,
    second_factor_matrix,
    second_factor_intercept,
    final_matrix,
    final_intercept,
):
    devices = lax.axis_size("row")
    side = math.isqrt(devices)
    seqs, residues, _ = alignment_features.shape
    tile = residues // side
    width = first_factor_matrix.shape[1]
    left, right = project(
        side,
        alignment_features,
        standardize_scaling,
        standardize_additive,
        first_factor_matrix,
        first_factor_intercept,
        second_factor_matrix,
        second_factor_intercept,
    )

    def swap(x, da, db):
        return lax.ppermute(x, "row", [(i, i ^ (da * side + db)) for i in range(devices)])

    right = [right[0]] + [swap(right[d], 0, d) for d in range(1, side)]
    *left, right[1] = lax.optimization_barrier((*left, right[1]))
    left = [left[0]] + [swap(left[d], d, 0) for d in range(1, side)]
    mines = [jnp.concatenate([x[part] for x in right]) for part in range(PARTS)]
    left = jnp.concatenate(left)
    near = swap(jnp.stack(mines), 1, 0)
    parts = [[mines[0], near[0]] + [swap(mines[0], d, 0) for d in range(2, side)]]
    lefts = [left]
    order = [0]
    mask = side // 2
    while mask > 0:
        lefts += [swap(jnp.concatenate(lefts), 0, mask)]
        order += [o ^ mask for o in order]
        mask //= 2
    lefts[-1], mines[-1] = lax.optimization_barrier((lefts[-1], mines[-1]))
    for part in range(1, PARTS):
        pieces = [mines[part], near[part]]
        mask = 2
        while mask < side:
            pieces.append(swap(jnp.concatenate(pieces), mask, 0))
            mask *= 2
        parts.append(pieces)
    left = arrange_left(lefts, tile)
    near, final_matrix = lax.optimization_barrier((near, final_matrix))
    wt = final_matrix.reshape(width, width, -1).transpose(2, 1, 0).reshape(-1, width * width)
    total = None
    for part in range(PARTS):
        if part > 0:
            total, *parts[part] = lax.optimization_barrier((total, *parts[part]))
        total = update_part(
            side, seqs, order, part, left, parts[part], wt, total, final_intercept, pairwise_features
        )
    return total.reshape(1, tile, tile, -1)


def solution(mesh):
    placed = (
        P(("grp", "row"), None, None),
        P(("grp", "row"), None, None, None),
        P(),
        P(),
        P(),
        P(),
        P(),
        P(),
        P(),
        P(),
    )
    return jax.shard_map(
        local,
        mesh=mesh,
        in_specs=placed,
        out_specs=P(("grp", "row"), None, None, None),
        check_vma=False,
    )
```

```python
import functools
import math

import jax
import jax.numpy as jnp
from jax import lax
from jax.experimental import pallas as pl
from jax.experimental.pallas import tpu as pltpu
from jax.sharding import PartitionSpec as P

LANES = 128
PARTS = 2
MIB = 1024 * 1024
RUN = 4


def in_hbm(x):
    return pltpu.with_memory_space_constraint(x, pltpu.HBM)


def project_kernel(side, *refs):
    sources, refs = refs[:7], refs[7:]
    left_out, right_out, refs = refs[:side], refs[side : 2 * side], refs[2 * side :]
    buffers, left_all, right_all, sems, x_sems = refs[:7], refs[7], refs[8], refs[9], refs[10]
    x_ref, gain_ref, offset_ref, wl_ref, bl_ref, wr_ref, br_ref = buffers
    seqs, residues, chans = x_ref.shape
    width = wl_ref.shape[0]
    tile = residues // side
    pack = LANES // width
    rows = tile // pack
    x_copies = [
        pltpu.make_async_copy(sources[0].at[s], x_ref.at[s], x_sems.at[s]) for s in range(seqs)
    ]
    copies = [
        pltpu.make_async_copy(sources[k], buffers[k], sems.at[k]) for k in range(1, len(buffers))
    ]
    for copy in x_copies[:1] + copies + x_copies[1:]:
        copy.start()
    for copy in copies:
        copy.wait()
    me = lax.axis_index("row")
    place_a, place_b = me // side, lax.rem(me, side)
    wl, wr = wl_ref[...], wr_ref[...]
    blank = jnp.zeros_like(wl)
    weights = []
    for h in range(pack):
        left_rows = jnp.concatenate([wl if k == h else blank for k in range(pack)], axis=0)
        right_rows = jnp.concatenate([wr] + [blank] * (pack - 1), axis=0)
        weights.append(jnp.concatenate([left_rows.T, right_rows.T], axis=1))
    left_bias = jnp.concatenate([bl_ref[...]] * pack, axis=1)
    right_bias = jnp.concatenate([br_ref[...]] * pack, axis=1)
    for s in range(seqs):
        x_copies[s].wait()
        x = x_ref[s].astype(jnp.float32)
        center = x - jnp.mean(x, axis=-1, keepdims=True)
        variance = jnp.mean(center * center, axis=-1, keepdims=True)
        normed = (center * lax.rsqrt(variance + 1e-05) * gain_ref[...] + offset_ref[...]).astype(
            jnp.bfloat16
        )
        total = left_bias
        rights = []
        for h in range(pack):
            picked = jnp.concatenate(
                [normed[a * tile + h * rows : a * tile + (h + 1) * rows] for a in range(side)],
                axis=0,
            )
            both = jnp.dot(picked, weights[h], preferred_element_type=jnp.float32)
            total = total + both[:, :LANES]
            rights.append((both[:, LANES:] + right_bias).astype(jnp.bfloat16))
        left = total.astype(jnp.bfloat16)
        for k in range(side):
            left_all[place_a ^ k, s] = left[k * rows : (k + 1) * rows]
            right = jnp.concatenate([r[k * rows : (k + 1) * rows] for r in rights], axis=0).T
            right_all[place_b ^ k, :, s] = right[:width].reshape(PARTS, width // PARTS, tile)
    for d in range(side):
        left_out[d][...] = left_all[d]
        right_out[d][...] = right_all[d]


def project(side, x, gain, offset, wl, bl, wr, br):
    seqs, residues, chans = x.shape
    width = wl.shape[1]
    tile = residues // side
    rows = tile * width // LANES
    operands = [in_hbm(o) for o in (x, gain[None], offset[None], wl.T, bl[None], wr.T, br[None])]
    out = pl.pallas_call(
        functools.partial(project_kernel, side),
        in_specs=[pl.BlockSpec(memory_space=pltpu.HBM)] * len(operands),
        out_specs=[pl.BlockSpec(memory_space=pltpu.VMEM)] * (2 * side),
        out_shape=[jax.ShapeDtypeStruct((seqs, rows, LANES), jnp.bfloat16)] * side
        + [jax.ShapeDtypeStruct((PARTS, seqs, width // PARTS, tile), jnp.bfloat16)] * side,
        scratch_shapes=[pltpu.VMEM(o.shape, o.dtype) for o in operands]
        + [
            pltpu.VMEM((side, seqs, rows, LANES), jnp.bfloat16),
            pltpu.VMEM((side, PARTS, seqs, width // PARTS, tile), jnp.bfloat16),
            pltpu.SemaphoreType.DMA((len(operands),)),
            pltpu.SemaphoreType.DMA((seqs,)),
        ],
        compiler_params=pltpu.CompilerParams(vmem_limit_bytes=32 * MIB),
        name="project",
    )(*operands)
    return out[:side], out[side:]


def arrange_kernel(seq_total, *refs):
    left_refs, out_ref, wide = refs[:-2], refs[-2], refs[-1]
    _, rows, lanes = left_refs[0].shape
    depth = out_ref.shape[2]
    at = 0
    for ref in left_refs:
        count = ref.shape[0] * rows
        wide[at : at + count] = ref[...].astype(jnp.float32).reshape(count, lanes)
        at += count
    if depth > seq_total:
        wide[seq_total * rows :] = jnp.zeros(((depth - seq_total) * rows, lanes), jnp.float32)
    for r in range(rows):
        out_ref[r] = wide[pl.ds(r, depth, stride=rows), :].T.astype(jnp.bfloat16)


def arrange_left(lefts, tile):
    _, rows, lanes = lefts[0].shape
    seq_total = sum(x.shape[0] for x in lefts)
    depth = -(-seq_total // LANES) * LANES
    return pl.pallas_call(
        functools.partial(arrange_kernel, seq_total),
        in_specs=[pl.BlockSpec(memory_space=pltpu.VMEM)] * len(lefts),
        out_specs=pl.BlockSpec(memory_space=pltpu.VMEM),
        out_shape=jax.ShapeDtypeStruct((rows, lanes, depth), jnp.bfloat16),
        scratch_shapes=[pltpu.VMEM((depth * rows, lanes), jnp.float32)],
        compiler_params=pltpu.CompilerParams(vmem_limit_bytes=32 * MIB),
        cost_estimate=pl.CostEstimate(flops=MIB, bytes_accessed=8 * MIB, transcendentals=0),
        name="arrange_left",
    )(*lefts)


def update_kernel(side, seqs, order, rights, group, first, last, left_ref, *refs):
    right_refs, refs = refs[:rights], refs[rights:]
    wt_ref, refs = refs[0], refs[1:]
    if not first:
        before_ref, refs = refs[0], refs[1:]
    if last:
        bias_ref, pair_ref, refs = refs[0], refs[1], refs[2:]
    out_ref, right_wide, right_flat, outer = refs
    rows, lanes, depth = left_ref.shape
    _, some, tile = right_refs[0].shape
    pack = outer.shape[2] // tile
    width = lanes // pack
    seq_total = side * side * seqs
    at = pl.program_id(0) * group

    @pl.when(pl.program_id(0) == 0)
    def _():
        dz = 0
        for ref in right_refs:
            for start in range(0, ref.shape[0], side * seqs):
                for k, dy in enumerate(order):
                    to = (k * side + dz) * seqs
                    right_wide[to * some : (to + seqs) * some] = (
                        ref[start + dy * seqs : start + (dy + 1) * seqs]
                        .astype(jnp.float32)
                        .reshape(seqs * some, tile)
                    )
                dz += 1
        if depth > seq_total:
            right_wide[seq_total * some :] = jnp.zeros(
                ((depth - seq_total) * some, tile), jnp.float32
            )
        for e in range(some):
            right_flat[:, e * tile : (e + 1) * tile] = right_wide[
                pl.ds(e, depth, stride=some), :
            ].astype(jnp.bfloat16)

    def outer_products(q):
        for n in range(some // 2):
            both = jnp.dot(
                left_ref[at + q],
                right_flat[:, 2 * n * tile : (2 * n + 2) * tile],
                preferred_element_type=jnp.float32,
            ).astype(jnp.bfloat16)
            for k in range(2):
                e = 2 * n + k
                for h in range(pack):
                    outer[q, e * width : (e + 1) * width, h * tile : (h + 1) * tile] = both[h * width : (h + 1) * width, k * tile : (k + 1) * tile]

    def project_back(q):
        update = jnp.dot(wt_ref[...], outer[q], preferred_element_type=jnp.float32)
        if not first:
            update = update + before_ref[at + q]
        if not last:
            out_ref[at + q] = update
            return
        for h in range(pack):
            share = update[:, h * tile : (h + 1) * tile].T * (1.0 / seq_total) + bias_ref[...]
            old = pair_ref[h, at + q].astype(jnp.float32)
            out_ref[h, q] = (old + share).astype(jnp.bfloat16)

    for start in range(0, group + RUN, RUN):
        for q in range(start, start + RUN):
            if q < group:
                outer_products(q)
        for q in range(start - RUN, start):
            if q >= 0:
                project_back(q)


def update_part(side, seqs, order, part, left, right, wt, before, bias, pair):
    rows, lanes, depth = left.shape
    some, tile = right[0].shape[-2:]
    chans = wt.shape[0]
    pack = tile // rows
    width = lanes // pack
    group = 16
    first, last = part == 0, part == PARTS - 1
    in_vmem = pl.BlockSpec(memory_space=pltpu.VMEM)
    operands = [left] + list(right) + [wt[:, part * some * width : (part + 1) * some * width]]
    if not first:
        operands.append(before)
    if last:
        operands += [bias[None], pair.reshape(pack, rows, tile, chans)]
        out_shape = jax.ShapeDtypeStruct((pack, rows, tile, chans), jnp.bfloat16)
        out_spec = pl.BlockSpec((pack, group, tile, chans), lambda g: (0, g, 0, 0))
    else:
        out_shape, out_spec = pltpu.VMEM((rows, chans, pack * tile), jnp.float32), in_vmem
    return pl.pallas_call(
        functools.partial(update_kernel, side, seqs, order, len(right), group, first, last),
        grid=(rows // group,),
        in_specs=[in_vmem] * len(operands),
        out_specs=out_spec,
        out_shape=out_shape,
        scratch_shapes=[
            pltpu.VMEM((depth * some, tile), jnp.float32),
            pltpu.VMEM((depth, some * tile), jnp.bfloat16),
            pltpu.VMEM((group, some * width, pack * tile), jnp.bfloat16),
        ],
        compiler_params=pltpu.CompilerParams(vmem_limit_bytes=24 * MIB),
        cost_estimate=pl.CostEstimate(
            flops=2 * tile * tile * some * width * (side * side * seqs + chans),
            bytes_accessed=16 * MIB,
            transcendentals=0,
        ),
        name="update_%d" % part,
    )(*operands)


def local(
    alignment_features,
    pairwise_features,
    standardize_scaling,
    standardize_additive,
    first_factor_matrix,
    first_factor_intercept,
    second_factor_matrix,
    second_factor_intercept,
    final_matrix,
    final_intercept,
):
    devices = lax.axis_size("row")
    side = math.isqrt(devices)
    seqs, residues, _ = alignment_features.shape
    tile = residues // side
    width = first_factor_matrix.shape[1]
    left, right = project(
        side,
        alignment_features,
        standardize_scaling,
        standardize_additive,
        first_factor_matrix,
        first_factor_intercept,
        second_factor_matrix,
        second_factor_intercept,
    )

    def swap(x, da, db):
        return lax.ppermute(x, "row", [(i, i ^ (da * side + db)) for i in range(devices)])

    right = [right[0]] + [swap(right[d], 0, d) for d in range(1, side)]
    *left, right[1] = lax.optimization_barrier((*left, right[1]))
    left = [left[0]] + [swap(left[d], d, 0) for d in range(1, side)]
    mines = [jnp.concatenate([x[part] for x in right]) for part in range(PARTS)]
    left = jnp.concatenate(left)
    near = swap(jnp.stack(mines), 1, 0)
    parts = [[mines[0], near[0]] + [swap(mines[0], d, 0) for d in range(2, side)]]
    lefts = [left]
    order = [0]
    mask = side // 2
    while mask > 0:
        lefts += [swap(jnp.concatenate(lefts), 0, mask)]
        order += [o ^ mask for o in order]
        mask //= 2
    lefts[-1], mines[-1] = lax.optimization_barrier((lefts[-1], mines[-1]))
    for part in range(1, PARTS):
        pieces = [mines[part], near[part]]
        mask = 2
        while mask < side:
            pieces.append(swap(jnp.concatenate(pieces), mask, 0))
            mask *= 2
        parts.append(pieces)
    left = arrange_left(lefts, tile)
    near, final_matrix = lax.optimization_barrier((near, final_matrix))
    wt = final_matrix.reshape(width, width, -1).transpose(2, 1, 0).reshape(-1, width * width)
    total = None
    for part in range(PARTS):
        if part > 0:
            total, *parts[part] = lax.optimization_barrier((total, *parts[part]))
        total = update_part(
            side, seqs, order, part, left, parts[part], wt, total, final_intercept, pairwise_features
        )
    return total.reshape(1, tile, tile, -1)


def solution(mesh):
    placed = (
        P(("grp", "row"), None, None),
        P(("grp", "row"), None, None, None),
        P(),
        P(),
        P(),
        P(),
        P(),
        P(),
        P(),
        P(),
    )
    return jax.shard_map(
        local,
        mesh=mesh,
        in_specs=placed,
        out_specs=P(("grp", "row"), None, None, None),
        check_vma=False,
    )
```

```python
import functools
import math

import jax
import jax.numpy as jnp
from jax import lax
from jax.experimental import pallas as pl
from jax.experimental.pallas import tpu as pltpu
from jax.sharding import PartitionSpec as P

LANES = 128
PARTS = 2
MIB = 1024 * 1024
RUN = 4


def in_hbm(x):
    return pltpu.with_memory_space_constraint(x, pltpu.HBM)


def project_kernel(side, *refs):
    sources, refs = refs[:7], refs[7:]
    left_out, right_out, refs = refs[:side], refs[side : 2 * side], refs[2 * side :]
    buffers, left_all, right_all, sems, x_sems = refs[:7], refs[7], refs[8], refs[9], refs[10]
    x_ref, gain_ref, offset_ref, wl_ref, bl_ref, wr_ref, br_ref = buffers
    seqs, residues, chans = x_ref.shape
    width = wl_ref.shape[0]
    tile = residues // side
    pack = LANES // width
    rows = tile // pack
    x_copies = [
        pltpu.make_async_copy(sources[0].at[s], x_ref.at[s], x_sems.at[s]) for s in range(seqs)
    ]
    copies = [
        pltpu.make_async_copy(sources[k], buffers[k], sems.at[k]) for k in range(1, len(buffers))
    ]
    for copy in x_copies[:1] + copies + x_copies[1:]:
        copy.start()
    for copy in copies:
        copy.wait()
    me = lax.axis_index("row")
    place_a, place_b = me // side, lax.rem(me, side)
    wl, wr = wl_ref[...], wr_ref[...]
    blank = jnp.zeros_like(wl)
    weights = []
    for h in range(pack):
        left_rows = jnp.concatenate([wl if k == h else blank for k in range(pack)], axis=0)
        right_rows = jnp.concatenate([wr] + [blank] * (pack - 1), axis=0)
        weights.append(jnp.concatenate([left_rows.T, right_rows.T], axis=1))
    left_bias = jnp.concatenate([bl_ref[...]] * pack, axis=1)
    right_bias = jnp.concatenate([br_ref[...]] * pack, axis=1)
    for s in range(seqs):
        x_copies[s].wait()
        x = x_ref[s].astype(jnp.float32)
        center = x - jnp.mean(x, axis=-1, keepdims=True)
        variance = jnp.mean(center * center, axis=-1, keepdims=True)
        normed = (center * lax.rsqrt(variance + 1e-05) * gain_ref[...] + offset_ref[...]).astype(
            jnp.bfloat16
        )
        total = left_bias
        rights = []
        for h in range(pack):
            picked = jnp.concatenate(
                [normed[a * tile + h * rows : a * tile + (h + 1) * rows] for a in range(side)],
                axis=0,
            )
            both = jnp.dot(picked, weights[h], preferred_element_type=jnp.float32)
            total = total + both[:, :LANES]
            rights.append((both[:, LANES:] + right_bias).astype(jnp.bfloat16))
        left = total.astype(jnp.bfloat16)
        for k in range(side):
            left_all[place_a ^ k, s] = left[k * rows : (k + 1) * rows]
            right = jnp.concatenate([r[k * rows : (k + 1) * rows] for r in rights], axis=0).T
            right_all[place_b ^ k, :, s] = right[:width].reshape(PARTS, width // PARTS, tile)
    for d in range(side):
        left_out[d][...] = left_all[d]
        right_out[d][...] = right_all[d]


def project(side, x, gain, offset, wl, bl, wr, br):
    seqs, residues, chans = x.shape
    width = wl.shape[1]
    tile = residues // side
    rows = tile * width // LANES
    operands = [in_hbm(o) for o in (x, gain[None], offset[None], wl.T, bl[None], wr.T, br[None])]
    out = pl.pallas_call(
        functools.partial(project_kernel, side),
        in_specs=[pl.BlockSpec(memory_space=pltpu.HBM)] * len(operands),
        out_specs=[pl.BlockSpec(memory_space=pltpu.VMEM)] * (2 * side),
        out_shape=[jax.ShapeDtypeStruct((seqs, rows, LANES), jnp.bfloat16)] * side
        + [jax.ShapeDtypeStruct((PARTS, seqs, width // PARTS, tile), jnp.bfloat16)] * side,
        scratch_shapes=[pltpu.VMEM(o.shape, o.dtype) for o in operands]
        + [
            pltpu.VMEM((side, seqs, rows, LANES), jnp.bfloat16),
            pltpu.VMEM((side, PARTS, seqs, width // PARTS, tile), jnp.bfloat16),
            pltpu.SemaphoreType.DMA((len(operands),)),
            pltpu.SemaphoreType.DMA((seqs,)),
        ],
        compiler_params=pltpu.CompilerParams(vmem_limit_bytes=32 * MIB),
        name="project",
    )(*operands)
    return out[:side], out[side:]


def arrange_kernel(seq_total, *refs):
    left_refs, out_ref, wide = refs[:-2], refs[-2], refs[-1]
    _, rows, lanes = left_refs[0].shape
    depth = out_ref.shape[2]
    at = 0
    for ref in left_refs:
        count = ref.shape[0] * rows
        wide[at : at + count] = ref[...].astype(jnp.float32).reshape(count, lanes)
        at += count
    if depth > seq_total:
        wide[seq_total * rows :] = jnp.zeros(((depth - seq_total) * rows, lanes), jnp.float32)
    for r in range(rows):
        out_ref[r] = wide[pl.ds(r, depth, stride=rows), :].T.astype(jnp.bfloat16)


def arrange_left(lefts, tile):
    _, rows, lanes = lefts[0].shape
    seq_total = sum(x.shape[0] for x in lefts)
    depth = -(-seq_total // LANES) * LANES
    return pl.pallas_call(
        functools.partial(arrange_kernel, seq_total),
        in_specs=[pl.BlockSpec(memory_space=pltpu.VMEM)] * len(lefts),
        out_specs=pl.BlockSpec(memory_space=pltpu.VMEM),
        out_shape=jax.ShapeDtypeStruct((rows, lanes, depth), jnp.bfloat16),
        scratch_shapes=[pltpu.VMEM((depth * rows, lanes), jnp.float32)],
        compiler_params=pltpu.CompilerParams(vmem_limit_bytes=32 * MIB),
        cost_estimate=pl.CostEstimate(flops=MIB, bytes_accessed=8 * MIB, transcendentals=0),
        name="arrange_left",
    )(*lefts)


def update_kernel(side, seqs, order, rights, group, first, last, left_ref, *refs):
    right_refs, refs = refs[:rights], refs[rights:]
    wt_ref, refs = refs[0], refs[1:]
    if not first:
        before_ref, refs = refs[0], refs[1:]
    if last:
        bias_ref, pair_ref, refs = refs[0], refs[1], refs[2:]
    out_ref, right_wide, right_flat, outer, *refs = refs
    if last:
        ready, sems = refs

        def copy_out(row):
            return pltpu.make_async_copy(ready.at[:, row], out_ref.at[:, row], sems.at[row])

    rows, lanes, depth = left_ref.shape
    _, some, tile = right_refs[0].shape
    halves = outer.shape[0] // group
    pack = 2 * halves
    width = lanes // pack
    seq_total = side * side * seqs
    at = pl.program_id(0) * group

    @pl.when(pl.program_id(0) == 0)
    def _():
        dz = 0
        for ref in right_refs:
            for start in range(0, ref.shape[0], side * seqs):
                for k, dy in enumerate(order):
                    to = (k * side + dz) * seqs
                    right_wide[to * some : (to + seqs) * some] = (
                        ref[start + dy * seqs : start + (dy + 1) * seqs]
                        .astype(jnp.float32)
                        .reshape(seqs * some, tile)
                    )
                dz += 1
        if depth > seq_total:
            right_wide[seq_total * some :] = jnp.zeros(
                ((depth - seq_total) * some, tile), jnp.float32
            )
        for e in range(some):
            right_flat[:, e * tile : (e + 1) * tile] = right_wide[
                pl.ds(e, depth, stride=some), :
            ].astype(jnp.bfloat16)

    def outer_products(q):
        for n in range(some // 2):
            both = jnp.dot(
                left_ref[at + q],
                right_flat[:, 2 * n * tile : (2 * n + 2) * tile],
                preferred_element_type=jnp.float32,
            ).astype(jnp.bfloat16)
            for k in range(2):
                e = 2 * n + k
                for h in range(pack):
                    outer[
                        q * halves + h // 2,
                        e * width : (e + 1) * width,
                        (h % 2) * tile : (h % 2 + 1) * tile,
                    ] = both[h * width : (h + 1) * width, k * tile : (k + 1) * tile]

    def project_back(q):
        for g in range(halves):
            update = jnp.dot(wt_ref[...], outer[q * halves + g], preferred_element_type=jnp.float32)
            if not first:
                update = update + before_ref[at + q, g]
            if not last:
                out_ref[at + q, g] = update
                continue
            for k in range(2):
                h = 2 * g + k
                share = update[:, k * tile : (k + 1) * tile].T * (1.0 / seq_total) + bias_ref[...]
                old = pair_ref[h, at + q].astype(jnp.float32)
                ready[h, at + q] = (old + share).astype(jnp.bfloat16)
        if last:
            copy_out(at + q).start()

    for start in range(0, group + RUN, RUN):
        for q in range(start, start + RUN):
            if q < group:
                outer_products(q)
        for q in range(start - RUN, start):
            if q >= 0:
                project_back(q)

    if last:

        @pl.when(pl.program_id(0) == pl.num_programs(0) - 1)
        def _():
            for row in range(rows):
                copy_out(row).wait()


def update_part(side, seqs, order, part, left, right, wt, before, bias, pair):
    rows, lanes, depth = left.shape
    some, tile = right[0].shape[-2:]
    chans = wt.shape[0]
    pack = tile // rows
    width = lanes // pack
    halves = pack // 2
    group = 16 if part < PARTS - 1 else rows
    first, last = part == 0, part == PARTS - 1
    in_vmem = pl.BlockSpec(memory_space=pltpu.VMEM)
    scratch = [
        pltpu.VMEM((depth * some, tile), jnp.float32),
        pltpu.VMEM((depth, some * tile), jnp.bfloat16),
        pltpu.VMEM((group * halves, some * width, 2 * tile), jnp.bfloat16),
    ]
    operands = [left] + list(right) + [wt[:, part * some * width : (part + 1) * some * width]]
    if not first:
        operands.append(before)
    if last:
        operands += [bias[None], pair.reshape(pack, rows, tile, chans)]
        out_shape = jax.ShapeDtypeStruct((pack, rows, tile, chans), jnp.bfloat16)
        out_spec = pl.BlockSpec(memory_space=pltpu.HBM)
        scratch += [
            pltpu.VMEM((pack, rows, tile, chans), jnp.bfloat16),
            pltpu.SemaphoreType.DMA((rows,)),
        ]
    else:
        out_shape, out_spec = pltpu.VMEM((rows, halves, chans, 2 * tile), jnp.float32), in_vmem
    return pl.pallas_call(
        functools.partial(update_kernel, side, seqs, order, len(right), group, first, last),
        grid=(rows // group,),
        in_specs=[in_vmem] * len(operands),
        out_specs=out_spec,
        out_shape=out_shape,
        scratch_shapes=scratch,
        compiler_params=pltpu.CompilerParams(vmem_limit_bytes=32 * MIB),
        cost_estimate=pl.CostEstimate(
            flops=2 * tile * tile * some * width * (side * side * seqs + chans),
            bytes_accessed=16 * MIB,
            transcendentals=0,
        ),
        name="update_%d" % part,
    )(*operands)


def local(
    alignment_features,
    pairwise_features,
    standardize_scaling,
    standardize_additive,
    first_factor_matrix,
    first_factor_intercept,
    second_factor_matrix,
    second_factor_intercept,
    final_matrix,
    final_intercept,
):
    devices = lax.axis_size("row")
    side = math.isqrt(devices)
    seqs, residues, _ = alignment_features.shape
    tile = residues // side
    width = first_factor_matrix.shape[1]
    left, right = project(
        side,
        alignment_features,
        standardize_scaling,
        standardize_additive,
        first_factor_matrix,
        first_factor_intercept,
        second_factor_matrix,
        second_factor_intercept,
    )

    def swap(x, da, db):
        return lax.ppermute(x, "row", [(i, i ^ (da * side + db)) for i in range(devices)])

    right = [right[0]] + [swap(right[d], 0, d) for d in range(1, side)]
    *left, right[1] = lax.optimization_barrier((*left, right[1]))
    left = [left[0]] + [swap(left[d], d, 0) for d in range(1, side)]
    mines = [jnp.concatenate([x[part] for x in right]) for part in range(PARTS)]
    left = jnp.concatenate(left)
    near = swap(jnp.stack(mines), 1, 0)
    parts = [[mines[0], near[0]] + [swap(mines[0], d, 0) for d in range(2, side)]]
    lefts = [left]
    order = [0]
    mask = side // 2
    while mask > 0:
        lefts += [swap(jnp.concatenate(lefts), 0, mask)]
        order += [o ^ mask for o in order]
        mask //= 2
    lefts[-1], mines[-1] = lax.optimization_barrier((lefts[-1], mines[-1]))
    for part in range(1, PARTS):
        pieces = [mines[part], near[part]]
        mask = 2
        while mask < side:
            pieces.append(swap(jnp.concatenate(pieces), mask, 0))
            mask *= 2
        parts.append(pieces)
    left = arrange_left(lefts, tile)
    near, final_matrix = lax.optimization_barrier((near, final_matrix))
    wt = final_matrix.reshape(width, width, -1).transpose(2, 1, 0).reshape(-1, width * width)
    total = None
    for part in range(PARTS):
        if part > 0:
            total, *parts[part] = lax.optimization_barrier((total, *parts[part]))
        total = update_part(
            side, seqs, order, part, left, parts[part], wt, total, final_intercept, pairwise_features
        )
    return total.reshape(1, tile, tile, -1)


def solution(mesh):
    placed = (
        P(("grp", "row"), None, None),
        P(("grp", "row"), None, None, None),
        P(),
        P(),
        P(),
        P(),
        P(),
        P(),
        P(),
        P(),
    )
    return jax.shard_map(
        local,
        mesh=mesh,
        in_specs=placed,
        out_specs=P(("grp", "row"), None, None, None),
        check_vma=False,
    )
```

```python
import functools
import math

import jax
import jax.numpy as jnp
from jax import lax
from jax.experimental import pallas as pl
from jax.experimental.pallas import tpu as pltpu
from jax.sharding import PartitionSpec as P

LANES = 128
PARTS = 2
MIB = 1024 * 1024
RUN = 8


def in_hbm(x):
    return pltpu.with_memory_space_constraint(x, pltpu.HBM)


def project_kernel(side, *refs):
    sources, refs = refs[:7], refs[7:]
    left_out, right_out, refs = refs[:side], refs[side : 2 * side], refs[2 * side :]
    buffers, left_all, right_all, sems, x_sems = refs[:7], refs[7], refs[8], refs[9], refs[10]
    x_ref, gain_ref, offset_ref, wl_ref, bl_ref, wr_ref, br_ref = buffers
    seqs, residues, chans = x_ref.shape
    width = wl_ref.shape[0]
    tile = residues // side
    pack = LANES // width
    rows = tile // pack
    x_copies = [
        pltpu.make_async_copy(sources[0].at[s], x_ref.at[s], x_sems.at[s]) for s in range(seqs)
    ]
    copies = [
        pltpu.make_async_copy(sources[k], buffers[k], sems.at[k]) for k in range(1, len(buffers))
    ]
    for copy in x_copies[:1] + copies + x_copies[1:]:
        copy.start()
    for copy in copies:
        copy.wait()
    me = lax.axis_index("row")
    place_a, place_b = me // side, lax.rem(me, side)
    wl, wr = wl_ref[...], wr_ref[...]
    blank = jnp.zeros_like(wl)
    weights = []
    for h in range(pack):
        left_rows = jnp.concatenate([wl if k == h else blank for k in range(pack)], axis=0)
        right_rows = jnp.concatenate([wr] + [blank] * (pack - 1), axis=0)
        weights.append(jnp.concatenate([left_rows.T, right_rows.T], axis=1))
    left_bias = jnp.concatenate([bl_ref[...]] * pack, axis=1)
    right_bias = jnp.concatenate([br_ref[...]] * pack, axis=1)
    for s in range(seqs):
        x_copies[s].wait()
        x = x_ref[s].astype(jnp.float32)
        center = x - jnp.mean(x, axis=-1, keepdims=True)
        variance = jnp.mean(center * center, axis=-1, keepdims=True)
        normed = (center * lax.rsqrt(variance + 1e-05) * gain_ref[...] + offset_ref[...]).astype(
            jnp.bfloat16
        )
        total = left_bias
        rights = []
        for h in range(pack):
            picked = jnp.concatenate(
                [normed[a * tile + h * rows : a * tile + (h + 1) * rows] for a in range(side)],
                axis=0,
            )
            both = jnp.dot(picked, weights[h], preferred_element_type=jnp.float32)
            total = total + both[:, :LANES]
            rights.append((both[:, LANES:] + right_bias).astype(jnp.bfloat16))
        left = total.astype(jnp.bfloat16)
        for k in range(side):
            left_all[place_a ^ k, s] = left[k * rows : (k + 1) * rows]
            right = jnp.concatenate([r[k * rows : (k + 1) * rows] for r in rights], axis=0).T
            right_all[place_b ^ k, :, s] = right[:width].reshape(PARTS, width // PARTS, tile)
    for d in range(side):
        left_out[d][...] = left_all[d]
        right_out[d][...] = right_all[d]


def project(side, x, gain, offset, wl, bl, wr, br):
    seqs, residues, chans = x.shape
    width = wl.shape[1]
    tile = residues // side
    rows = tile * width // LANES
    operands = [in_hbm(o) for o in (x, gain[None], offset[None], wl.T, bl[None], wr.T, br[None])]
    out = pl.pallas_call(
        functools.partial(project_kernel, side),
        in_specs=[pl.BlockSpec(memory_space=pltpu.HBM)] * len(operands),
        out_specs=[pl.BlockSpec(memory_space=pltpu.VMEM)] * (2 * side),
        out_shape=[jax.ShapeDtypeStruct((seqs, rows, LANES), jnp.bfloat16)] * side
        + [jax.ShapeDtypeStruct((PARTS, seqs, width // PARTS, tile), jnp.bfloat16)] * side,
        scratch_shapes=[pltpu.VMEM(o.shape, o.dtype) for o in operands]
        + [
            pltpu.VMEM((side, seqs, rows, LANES), jnp.bfloat16),
            pltpu.VMEM((side, PARTS, seqs, width // PARTS, tile), jnp.bfloat16),
            pltpu.SemaphoreType.DMA((len(operands),)),
            pltpu.SemaphoreType.DMA((seqs,)),
        ],
        compiler_params=pltpu.CompilerParams(vmem_limit_bytes=32 * MIB),
        name="project",
    )(*operands)
    return out[:side], out[side:]


def arrange_kernel(seq_total, *refs):
    left_refs, out_ref, wide = refs[:-2], refs[-2], refs[-1]
    _, rows, lanes = left_refs[0].shape
    depth = out_ref.shape[2]
    at = 0
    for ref in left_refs:
        count = ref.shape[0] * rows
        wide[at : at + count] = ref[...].astype(jnp.float32).reshape(count, lanes)
        at += count
    if depth > seq_total:
        wide[seq_total * rows :] = jnp.zeros(((depth - seq_total) * rows, lanes), jnp.float32)
    for r in range(rows):
        out_ref[r] = wide[pl.ds(r, depth, stride=rows), :].T.astype(jnp.bfloat16)


def arrange_left(lefts, tile):
    _, rows, lanes = lefts[0].shape
    seq_total = sum(x.shape[0] for x in lefts)
    depth = -(-seq_total // LANES) * LANES
    return pl.pallas_call(
        functools.partial(arrange_kernel, seq_total),
        in_specs=[pl.BlockSpec(memory_space=pltpu.VMEM)] * len(lefts),
        out_specs=pl.BlockSpec(memory_space=pltpu.VMEM),
        out_shape=jax.ShapeDtypeStruct((rows, lanes, depth), jnp.bfloat16),
        scratch_shapes=[pltpu.VMEM((depth * rows, lanes), jnp.float32)],
        compiler_params=pltpu.CompilerParams(vmem_limit_bytes=32 * MIB),
        cost_estimate=pl.CostEstimate(flops=MIB, bytes_accessed=8 * MIB, transcendentals=0),
        name="arrange_left",
    )(*lefts)


def update_kernel(side, seqs, order, rights, group, first, last, left_ref, *refs):
    right_refs, refs = refs[:rights], refs[rights:]
    wt_ref, refs = refs[0], refs[1:]
    if not first:
        before_ref, refs = refs[0], refs[1:]
    if last:
        bias_ref, pair_ref, refs = refs[0], refs[1], refs[2:]
    out_ref, right_wide, right_flat, outer, *refs = refs
    if last:
        ready, sems = refs

        def copy_out(row):
            return pltpu.make_async_copy(ready.at[:, row], out_ref.at[:, row], sems.at[row])

    rows, lanes, depth = left_ref.shape
    _, some, tile = right_refs[0].shape
    halves = outer.shape[0] // group
    pack = 2 * halves
    width = lanes // pack
    seq_total = side * side * seqs
    at = pl.program_id(0) * group

    @pl.when(pl.program_id(0) == 0)
    def _():
        dz = 0
        for ref in right_refs:
            for start in range(0, ref.shape[0], side * seqs):
                for k, dy in enumerate(order):
                    to = (k * side + dz) * seqs
                    right_wide[to * some : (to + seqs) * some] = (
                        ref[start + dy * seqs : start + (dy + 1) * seqs]
                        .astype(jnp.float32)
                        .reshape(seqs * some, tile)
                    )
                dz += 1
        if depth > seq_total:
            right_wide[seq_total * some :] = jnp.zeros(
                ((depth - seq_total) * some, tile), jnp.float32
            )
        for e in range(some):
            right_flat[:, e * tile : (e + 1) * tile] = right_wide[
                pl.ds(e, depth, stride=some), :
            ].astype(jnp.bfloat16)

    def outer_products(q):
        for n in range(some // 2):
            both = jnp.dot(
                left_ref[at + q],
                right_flat[:, 2 * n * tile : (2 * n + 2) * tile],
                preferred_element_type=jnp.float32,
            ).astype(jnp.bfloat16)
            for k in range(2):
                e = 2 * n + k
                for h in range(pack):
                    outer[
                        q * halves + h // 2,
                        e * width : (e + 1) * width,
                        (h % 2) * tile : (h % 2 + 1) * tile,
                    ] = both[h * width : (h + 1) * width, k * tile : (k + 1) * tile]

    def project_back(q):
        for g in range(halves):
            update = jnp.dot(wt_ref[...], outer[q * halves + g], preferred_element_type=jnp.float32)
            if not first:
                update = update + before_ref[at + q, g]
            if not last:
                out_ref[at + q, g] = update
                continue
            for k in range(2):
                h = 2 * g + k
                share = update[:, k * tile : (k + 1) * tile].T * (1.0 / seq_total) + bias_ref[...]
                old = pair_ref[h, at + q].astype(jnp.float32)
                ready[h, at + q] = (old + share).astype(jnp.bfloat16)
        if last:
            copy_out(at + q).start()

    for start in range(0, group + RUN, RUN):
        for q in range(start, start + RUN):
            if q < group:
                outer_products(q)
        for q in range(start - RUN, start):
            if q >= 0:
                project_back(q)

    if last:

        @pl.when(pl.program_id(0) == pl.num_programs(0) - 1)
        def _():
            for row in range(rows):
                copy_out(row).wait()


def update_part(side, seqs, order, part, left, right, wt, before, bias, pair):
    rows, lanes, depth = left.shape
    some, tile = right[0].shape[-2:]
    chans = wt.shape[0]
    pack = tile // rows
    width = lanes // pack
    halves = pack // 2
    group = 16 if part < PARTS - 1 else rows
    first, last = part == 0, part == PARTS - 1
    in_vmem = pl.BlockSpec(memory_space=pltpu.VMEM)
    scratch = [
        pltpu.VMEM((depth * some, tile), jnp.float32),
        pltpu.VMEM((depth, some * tile), jnp.bfloat16),
        pltpu.VMEM((group * halves, some * width, 2 * tile), jnp.bfloat16),
    ]
    operands = [left] + list(right) + [wt[:, part * some * width : (part + 1) * some * width]]
    if not first:
        operands.append(before)
    if last:
        operands += [bias[None], pair.reshape(pack, rows, tile, chans)]
        out_shape = jax.ShapeDtypeStruct((pack, rows, tile, chans), jnp.bfloat16)
        out_spec = pl.BlockSpec(memory_space=pltpu.HBM)
        scratch += [
            pltpu.VMEM((pack, rows, tile, chans), jnp.bfloat16),
            pltpu.SemaphoreType.DMA((rows,)),
        ]
    else:
        out_shape, out_spec = pltpu.VMEM((rows, halves, chans, 2 * tile), jnp.float32), in_vmem
    return pl.pallas_call(
        functools.partial(update_kernel, side, seqs, order, len(right), group, first, last),
        grid=(rows // group,),
        in_specs=[in_vmem] * len(operands),
        out_specs=out_spec,
        out_shape=out_shape,
        scratch_shapes=scratch,
        compiler_params=pltpu.CompilerParams(vmem_limit_bytes=32 * MIB),
        cost_estimate=pl.CostEstimate(
            flops=2 * tile * tile * some * width * (side * side * seqs + chans),
            bytes_accessed=16 * MIB,
            transcendentals=0,
        ),
        name="update_%d" % part,
    )(*operands)


def local(
    alignment_features,
    pairwise_features,
    standardize_scaling,
    standardize_additive,
    first_factor_matrix,
    first_factor_intercept,
    second_factor_matrix,
    second_factor_intercept,
    final_matrix,
    final_intercept,
):
    devices = lax.axis_size("row")
    side = math.isqrt(devices)
    seqs, residues, _ = alignment_features.shape
    tile = residues // side
    width = first_factor_matrix.shape[1]
    left, right = project(
        side,
        alignment_features,
        standardize_scaling,
        standardize_additive,
        first_factor_matrix,
        first_factor_intercept,
        second_factor_matrix,
        second_factor_intercept,
    )

    def swap(x, da, db):
        return lax.ppermute(x, "row", [(i, i ^ (da * side + db)) for i in range(devices)])

    right = [right[0]] + [swap(right[d], 0, d) for d in range(1, side)]
    *left, right[1] = lax.optimization_barrier((*left, right[1]))
    left = [left[0]] + [swap(left[d], d, 0) for d in range(1, side)]
    mines = [jnp.concatenate([x[part] for x in right]) for part in range(PARTS)]
    left = jnp.concatenate(left)
    near = swap(jnp.stack(mines), 1, 0)
    parts = [[mines[0], near[0]] + [swap(mines[0], d, 0) for d in range(2, side)]]
    lefts = [left]
    order = [0]
    mask = side // 2
    while mask > 0:
        lefts += [swap(jnp.concatenate(lefts), 0, mask)]
        order += [o ^ mask for o in order]
        mask //= 2
    lefts[-1], mines[-1] = lax.optimization_barrier((lefts[-1], mines[-1]))
    for part in range(1, PARTS):
        pieces = [mines[part], near[part]]
        mask = 2
        while mask < side:
            pieces.append(swap(jnp.concatenate(pieces), mask, 0))
            mask *= 2
        parts.append(pieces)
    left = arrange_left(lefts, tile)
    near, final_matrix = lax.optimization_barrier((near, final_matrix))
    wt = final_matrix.reshape(width, width, -1).transpose(2, 1, 0).reshape(-1, width * width)
    total = None
    for part in range(PARTS):
        if part > 0:
            total, *parts[part] = lax.optimization_barrier((total, *parts[part]))
        total = update_part(
            side, seqs, order, part, left, parts[part], wt, total, final_intercept, pairwise_features
        )
    return total.reshape(1, tile, tile, -1)


def solution(mesh):
    placed = (
        P(("grp", "row"), None, None),
        P(("grp", "row"), None, None, None),
        P(),
        P(),
        P(),
        P(),
        P(),
        P(),
        P(),
        P(),
    )
    return jax.shard_map(
        local,
        mesh=mesh,
        in_specs=placed,
        out_specs=P(("grp", "row"), None, None, None),
        check_vma=False,
    )
```
